32 devices in a mesh: dev: 32 (over z, y, x, core).
Axes of the slice: x: 2, y: 2, z: 4, core: 2. Of those that a mesh axis runs over, the one named last changes fastest.
Arguments:
- tokens: bfloat16 [8192, 1088], P('dev'), may hold values from -6 to 6
- attn_weight: bfloat16 [4352, 1088], P('dev')
- mlp_weight: bfloat16 [8704, 1088], P('dev'), may hold values from -0.1875 to 0.1875
- vectors: bfloat16 [13056], P('dev')
- cotangent: bfloat16 [8192, 1088], P('dev'), may hold values from -6 to 6
- seq_lengths: int32 [32], replicated, may hold values from 128 to 256, as said below
- seq_device: int32 [32], replicated, may hold values from 0 to 31, as said below
- seq_offset: int32 [32], replicated, may hold values from 0 to 128, as said below
Outputs:
- output: bfloat16 [8192, 1088], P('dev')
- grad_tokens: float32 [8192, 1088], P('dev')
- grad_attn: float32 [4352, 1088], P('dev')
- grad_mlp: float32 [8704, 1088], P('dev')
- grad_vectors: float32 [13056], P('dev')
The draws below stay inside these ranges and needn't reach their ends.
Inputs may be any that keep to these rules, and one draw needn't show every extreme that they name: Sequence j has seq_lengths[j] tokens; some sequence has exactly 256 and some exactly 128. `seq_device`: A permutation: each device holds exactly one sequence. Sequence j fills slots seq_offset[j] to seq_offset[j] + seq_lengths[j] - 1 of its device; the other slots are empty.
All inputs are finite; a program needn't handle non-finite values.
Results may differ from the reference program's by a relative error of at most 0.01.
Values may be sent and summed in bfloat16 or wider, within the bound.
No kernel may reach another device: no remote copies, remote signals or barrier semaphores. Data moves between devices by JAX's collectives and lax.ppermute only.
A program may use at most 256 MiB of HBM per device.

```python
import math
import jax
import jax.numpy as jnp
from jax import lax

D = 1088
HEADS = 17
HEAD_SIZE = 64
FF = 4352
SLOTS = 256
SHORTEST = 128
TOKENS = 8192
N_DEV = 32


def layout(key):
    key_len, key_pick, key_off, key_dev = jax.random.split(key, 4)
    lengths = jax.random.randint(key_len, (N_DEV,), SHORTEST, SLOTS + 1)
    picks = jax.random.permutation(key_pick, N_DEV)
    lengths = lengths.at[picks[0]].set(SLOTS).at[picks[1]].set(SHORTEST)
    room = SLOTS - lengths + 1
    offsets = jax.random.randint(key_off, (N_DEV,), 0, room)
    offsets = offsets.at[picks[1]].set(SLOTS - SHORTEST)
    device = jax.random.permutation(key_dev, N_DEV)
    return (lengths.astype(jnp.int32), device.astype(jnp.int32), offsets.astype(jnp.int32))


def draw_seq_lengths(key, part):
    return layout(key)[0]


def draw_seq_device(key, part):
    return layout(key)[1]


def draw_seq_offset(key, part):
    return layout(key)[2]


def draw_attn_weight(key, part):
    key = jax.random.fold_in(key, 7)
    base = jax.random.normal(key, (4 * D, D), jnp.float32) * D ** (-0.5)
    rows = jnp.arange(4 * D, dtype=jnp.int32)[:, None]
    return (jnp.where(rows >= 3 * D, 8.0, 1.0) * base).astype(jnp.bfloat16)


def draw_vectors(key, part):
    key = jax.random.fold_in(key, 11)
    key_gain, key_shift = jax.random.split(key)
    gains = jax.random.uniform(key_gain, (8 * D + FF,), jnp.float32, 0.6, 1.4)
    shifts = 0.3 * jax.random.normal(key_shift, (8 * D + FF,), jnp.float32)
    segment = jnp.arange(8 * D + FF, dtype=jnp.int32) // D
    is_gain = (segment == 0) | (segment == 5)
    return jnp.where(is_gain, gains, shifts).astype(jnp.bfloat16)


def spiked(values, key, source, target, parts, factor):
    owner, partner = [(jnp.arange(values.shape[dim]) // (values.shape[dim] // parts)).reshape([-1 if axis == dim else 1 for axis in range(values.ndim)]) for dim in (source, target)]
    chosen = jax.random.permutation(key, parts)[partner]
    strong = (owner == chosen) | (owner == (partner + parts // 2) % parts)
    return jnp.where(strong, factor * values, values)


def levels(stream_key, extent, cuts, smallest, top_value):
    def one(dim, parts):
        heights = jax.random.uniform(jax.random.fold_in(jax.random.fold_in(stream_key, 6), dim), (parts,), jnp.float32, smallest / len(cuts), top_value / len(cuts))
        return jnp.repeat(jnp.exp(heights), extent[dim] // parts).reshape((-1,) + (1,) * (len(extent) - dim - 1))

    level = one(*cuts[0])
    for cut in cuts[1:]:
        level = level * one(*cut)
    return level


def gaussian(stream_key, dims, scale, reach, shards=(), kind=jnp.bfloat16):
    level = levels(stream_key, dims, shards, -0.22, 0.18) if shards else 1.0
    values = jax.random.normal(stream_key, dims, jnp.float32) * scale * level
    return jnp.minimum(jnp.maximum(values, -reach), reach).astype(kind)


def bell_draw_with(own_key, dims, scale, limit, cuts, heavy, kind=jnp.bfloat16):
    values = scale * jax.random.normal(own_key, dims, jnp.float32)
    if cuts:
        values = values * levels(own_key, dims, cuts, -0.22, 0.18)
    return jnp.clip(spiked(values, jax.random.fold_in(own_key, 3), *heavy), -limit, limit).astype(kind)


def setup_inputs(seed: int = 0) -> dict:
    key_of = jax.random.split(jax.random.key(seed), 9)
    tokens = gaussian(key_of[0], (TOKENS, D), 1.0, 6.0, ((0, 32),))
    attn_weight = draw_attn_weight(jax.random.fold_in(key_of[8], 71), 0)
    mlp_weight = gaussian(key_of[2], (2 * FF, D), D ** -0.5, 0.1875, ((0, 32),))
    vectors = draw_vectors(jax.random.fold_in(key_of[8], 71), 0)
    cotangent = bell_draw_with(key_of[4], (TOKENS, D), 1.0, 6.0, ((0, 32),), (0, 1, 32, 2.75))
    seq_lengths = draw_seq_lengths(jax.random.fold_in(key_of[8], 71), 0)
    seq_device = draw_seq_device(jax.random.fold_in(key_of[8], 71), 0)
    seq_offset = draw_seq_offset(jax.random.fold_in(key_of[8], 71), 0)
    return dict(tokens=tokens, attn_weight=attn_weight, mlp_weight=mlp_weight, vectors=vectors, cotangent=cotangent, seq_lengths=seq_lengths, seq_device=seq_device, seq_offset=seq_offset)


@jax.custom_vjp
def low(v):
    return lax.optimization_barrier(v.astype(jnp.bfloat16)).astype(jnp.float32)

@jax.custom_vjp
def low_back(v):
    return v

def low_keep(v):
    return (low(v), None)

def low_pass(kept, grad):
    return (grad,)

def back_keep(v):
    return (v, None)

def back_low(kept, grad):
    return (low(grad),)
low.defvjp(low_keep, low_pass)
low_back.defvjp(back_keep, back_low)

def product(spec, left, right):
    return jnp.einsum(spec, left, right, precision=lax.Precision.HIGHEST)

def normalize(values, gain, shift):
    centre = values - lax.optimization_barrier(jnp.mean(values, axis=-1, keepdims=True))
    spread = lax.optimization_barrier(jnp.mean(centre * centre, axis=-1, keepdims=True))
    return centre * lax.rsqrt(spread + 1e-05) * gain + shift

def layer(block, keep, attn_w, mlp_w, vec):
    width = D
    pieces = [vec[number * width:(number + 1) * width] for number in range(8)]
    gain_one, shift_one, query_bias, value_bias, out_bias, gain_two, shift_two, down_bias = pieces
    up_bias = vec[8 * width:]
    count, span = (block.shape[0], block.shape[1])
    shape = (count, span, HEADS, HEAD_SIZE)
    first = low(normalize(block, gain_one, shift_one))
    queries = low_back(low(product('gsd,od->gso', first, attn_w[:width]) + query_bias))
    keys = low_back(low(product('gsd,od->gso', first, attn_w[width:2 * width])))
    values = low_back(low(product('gsd,od->gso', first, attn_w[2 * width:3 * width]) + value_bias))
    scores = low_back(product('gqhd,gkhd->ghqk', queries.reshape(shape), keys.reshape(shape)) * HEAD_SIZE ** (-0.5))
    position = jnp.arange(span, dtype=jnp.int32)
    causal = position[None, None, :, None] >= position[None, None, None, :]
    same = keep[:, None, :, None] == keep[:, None, None, :]
    scores = jnp.where(causal & same, scores, -1e+30)
    probs = low(jax.nn.softmax(scores, axis=-1))
    mixed = product('ghqk,gkhd->gqhd', probs, values.reshape(shape)).reshape(count, span, width)
    mixed = low_back(low(mixed))
    branch = low_back(product('gsd,od->gso', mixed, attn_w[3 * width:]) + out_bias)
    middle = block + branch
    second = low(normalize(middle, gain_two, shift_two))
    up_sum = low_back(product('gsd,fd->gsf', second, mlp_w[:FF]) + up_bias)
    activated = low(jax.nn.gelu(up_sum, approximate=False))
    down = product('gsf,fd->gsd', activated, mlp_w[FF:]) + down_bias
    return jnp.where(keep[:, :, None] == 1, middle + down, 0.0)

def reference(tokens, attn_weight, mlp_weight, vectors, cotangent, seq_lengths, seq_device, seq_offset):
    buffers = N_DEV
    owner = (seq_device[None, :] == jnp.arange(buffers, dtype=jnp.int32)[:, None]).astype(jnp.int32)
    begin = lax.optimization_barrier(jnp.sum(owner * seq_offset[None, :], axis=1))
    finish = begin + lax.optimization_barrier(jnp.sum(owner * seq_lengths[None, :], axis=1))
    slots = jnp.arange(SLOTS, dtype=jnp.int32)
    keep = ((slots[None, :] >= begin[:, None]) & (slots[None, :] < finish[:, None])).astype(jnp.int32)
    group = math.gcd(buffers, max(1, 2048 // SLOTS))
    rounds = buffers // group
    keep = keep.reshape(rounds, group, SLOTS)
    inputs = tokens.astype(jnp.float32).reshape(rounds, group, SLOTS, D)
    grad_output = cotangent.astype(jnp.float32).reshape(rounds, group, SLOTS, D)
    checked = jax.checkpoint(layer)

    def forward(values_in, attn_w, mlp_w, vec):

        def step(carry, item):
            return (carry, checked(item[0], item[1], attn_w, mlp_w, vec))
        return lax.scan(step, jnp.zeros((), jnp.float32), (values_in, keep))[1]
    result, pull = jax.vjp(forward, inputs, attn_weight.astype(jnp.float32), mlp_weight.astype(jnp.float32), vectors.astype(jnp.float32))
    grad_inputs, grad_attn, grad_mlp, grad_vec = pull(grad_output)
    return (result.reshape(TOKENS, D).astype(jnp.bfloat16), grad_inputs.reshape(TOKENS, D), grad_attn, grad_mlp, grad_vec)
```

```python
import jax
import jax.numpy as jnp
from jax import lax
from jax.sharding import PartitionSpec as P

D = 1088
HEADS = 17
HEAD_SIZE = 64
FF = 4352


epsilon = 1e-05
neg_large = -1e30


def normalize(values, gain, shift):
    centre = values - jnp.mean(values, axis=-1, keepdims=True)
    spread = jnp.mean(centre * centre, axis=-1, keepdims=True)
    factor = lax.rsqrt(spread + epsilon)
    normed = centre * factor
    return (normed * gain + shift, normed, factor)


def normalize_back(grad_out, normed, factor, gain):
    inner = grad_out * gain
    return factor * (
        inner
        - jnp.mean(inner, axis=-1, keepdims=True)
        - normed * jnp.mean(inner * normed, axis=-1, keepdims=True)
    )


def split_vectors(whole_vec):
    width = D
    pieces = [
        whole_vec[number * width : (number + 1) * width].astype(jnp.float32) for number in range(8)
    ]
    return pieces + [whole_vec[8 * width :].astype(jnp.float32)]


def gelu_exact(values):
    return jax.nn.gelu(values, approximate=False)


def allowed_pairs(keep):
    position = jnp.arange(keep.shape[0], dtype=jnp.int32)
    return (position[None, :] <= position[:, None]) & (keep[None, :] == keep[:, None])


def attend(queries, keys, values, allowed, scale):
    scores = jnp.einsum("qhd,khd->hqk", queries, keys, preferred_element_type=jnp.float32) * scale
    scores = jnp.where(allowed[None], scores, neg_large)
    top = jnp.max(scores, axis=-1, keepdims=True)
    expo = jnp.exp(scores - top)
    total = jnp.sum(expo, axis=-1, keepdims=True)
    weights = (expo / total).astype(jnp.bfloat16)
    mixed = jnp.einsum("hqk,khd->qhd", weights, values, preferred_element_type=jnp.float32)
    return (mixed, top + jnp.log(total))


def attend_back(queries, keys, values, allowed, scale, grad_mixed, log_total):
    scores = jnp.einsum("qhd,khd->hqk", queries, keys, preferred_element_type=jnp.float32) * scale
    scores = jnp.where(allowed[None], scores, neg_large)
    probs = jnp.exp(scores - log_total)
    grad_values = jnp.einsum(
        "hqk,qhd->khd", probs.astype(jnp.bfloat16), grad_mixed, preferred_element_type=jnp.float32
    )
    grad_probs = jnp.einsum("qhd,khd->hqk", grad_mixed, values, preferred_element_type=jnp.float32)
    inner = jnp.sum(probs * grad_probs, axis=-1, keepdims=True)
    grad_scores = (probs * (grad_probs - inner)).astype(jnp.bfloat16)
    grad_queries = (
        jnp.einsum("hqk,khd->qhd", grad_scores, keys, preferred_element_type=jnp.float32) * scale
    )
    grad_keys = (
        jnp.einsum("hqk,qhd->khd", grad_scores, queries, preferred_element_type=jnp.float32) * scale
    )
    return (grad_queries, grad_keys, grad_values)


def gather_rows(own):
    beside = swap(own, 1)
    across = swap(own, 2)
    return jnp.concatenate([own, beside, across, swap(across, 1)], axis=0)


def reduce_rows(partial):
    rows = partial.shape[0] // 4
    given = jnp.concatenate([partial[rows : 2 * rows], partial[3 * rows :]], axis=0)
    taken = swap(given, 1)
    far = (partial[2 * rows : 3 * rows] + taken[rows:]).astype(jnp.bfloat16)
    return partial[:rows] + taken[:rows] + swap(far, 2).astype(jnp.float32)


def swap(piece, mask):
    devices = lax.axis_size("dev")
    return lax.ppermute(piece, "dev", [(number, number ^ mask) for number in range(devices)])


def same_low(devices):
    return [list(range(low, devices, 4)) for low in range(4)]


def gather_vectors(own):
    here = lax.axis_index("dev")
    whole = own
    mask = 1
    while mask < lax.axis_size("dev"):
        other = swap(whole, mask)
        upper = (here & mask) != 0
        whole = jnp.concatenate(
            [jnp.where(upper, other, whole), jnp.where(upper, whole, other)], axis=0
        )
        mask *= 2
    return whole


def scatter_vectors(whole):
    here = lax.axis_index("dev")
    mask = lax.axis_size("dev") // 2
    while mask:
        half = whole.shape[0] // 2
        upper = (here & mask) != 0
        mine = jnp.where(upper, whole[half:], whole[:half])
        yours = jnp.where(upper, whole[:half], whole[half:])
        whole = mine + swap(yours, mask)
        mask //= 2
    return whole


def gather_hidden(shard):
    devices = lax.axis_size("dev")
    here = lax.axis_index("dev")
    half = devices // 2
    if devices != 32:
        both = lax.all_gather(
            shard, "dev", axis=0, tiled=True, axis_index_groups=same_low(devices)
        )
        rows = both.shape[0] // 2
        blocks = jnp.arange(half // 4, dtype=jnp.int32) * 4 + (here & 3)
        return [(both[:rows], both[rows:], blocks)]
    first = here < half
    one, two, three = swap(shard, 8), swap(shard, 16), swap(shard, 24)
    up = jnp.concatenate([jnp.where(first, shard, two), jnp.where(first, one, three)], axis=0)
    down = jnp.concatenate([jnp.where(first, two, shard), jnp.where(first, three, one)], axis=0)
    block = here & (half - 1)
    blocks = jnp.stack([block, block ^ 8])
    return [(swap(up, 4), swap(down, 4), blocks ^ 4), (up, down, blocks)]


def scatter_hidden(grads):
    devices = lax.axis_size("dev")
    if devices != 32:
        both = jnp.concatenate(grads[0], axis=0).astype(jnp.bfloat16)
        return lax.psum_scatter(
            both, "dev", scatter_dimension=0, tiled=True, axis_index_groups=same_low(devices)
        ).astype(jnp.float32)
    first = lax.axis_index("dev") < devices // 2
    low = jnp.bfloat16
    up = grads[1][0] + swap(grads[0][0].astype(low), 4).astype(jnp.float32)
    down = grads[1][1] + swap(grads[0][1].astype(low), 4).astype(jnp.float32)
    rows = up.shape[0] // 2
    mine = jnp.where(first, up[:rows], down[:rows])
    two = jnp.where(first, down[:rows], up[:rows]).astype(low)
    one = jnp.where(first, up[rows:], down[rows:]).astype(low)
    three = jnp.where(first, down[rows:], up[rows:]).astype(low)
    return (
        mine
        + swap(one, 8).astype(jnp.float32)
        + swap(two, 16).astype(jnp.float32)
        + swap(three, 24).astype(jnp.float32)
    )


def shards(
    tokens, attn_weight, mlp_weight, vectors, cotangent, seq_lengths, seq_device, seq_offset
):
    total_rows = tokens.shape[0]
    width = D
    scale = HEAD_SIZE ** (-0.5)
    low = jnp.bfloat16
    devices = lax.axis_size("dev")
    here = lax.axis_index("dev")
    chosen = (seq_device == here).astype(jnp.int32)
    begin = jnp.sum(chosen * seq_offset)
    finish = begin + jnp.sum(chosen * seq_lengths)
    positions = jnp.arange(total_rows, dtype=jnp.int32)
    keep = ((positions >= begin) & (positions < finish)).astype(jnp.int32)
    live = keep[:, None] == 1
    allowed = allowed_pairs(keep)
    head_shape = (total_rows, HEADS, HEAD_SIZE)

    full_vec = gather_vectors(vectors)
    full_attn = lax.all_gather(attn_weight, "dev", axis=0, tiled=True)
    grad_down = jnp.where(live, cotangent, jnp.zeros_like(cotangent))
    hidden_parts = gather_hidden(mlp_weight)
    grad_down_rows = gather_rows(grad_down)

    (
        gain_one,
        shift_one,
        query_bias,
        value_bias,
        out_bias,
        gain_two,
        shift_two,
        down_bias,
        up_bias,
    ) = split_vectors(full_vec)
    up_bias = up_bias.reshape(devices // 2, -1)

    inputs = tokens.astype(jnp.float32)
    first_out, normed_one, factor_one = normalize(inputs, gain_one, shift_one)
    first_low = first_out.astype(low)
    projected = jnp.einsum(
        "rd,od->ro", first_low, full_attn[: 3 * width], preferred_element_type=jnp.float32
    )
    queries = (projected[:, :width] + query_bias).astype(low).reshape(head_shape)
    keys = projected[:, width : 2 * width].astype(low).reshape(head_shape)
    values = (projected[:, 2 * width :] + value_bias).astype(low).reshape(head_shape)
    mixed, log_total = attend(queries, keys, values, allowed, scale)
    mixed_low = mixed.reshape(total_rows, width).astype(low)
    branch = (
        jnp.einsum(
            "rd,od->ro", mixed_low, full_attn[3 * width :], preferred_element_type=jnp.float32
        )
        + out_bias
    )
    middle = inputs + branch
    second_out, normed_two, factor_two = normalize(middle, gain_two, shift_two)
    second_low = gather_rows(second_out.astype(low))

    down_rows = 0.0
    second_rows = 0.0
    grads = []
    grad_up_bias = jnp.zeros_like(up_bias)
    for up_weight, down_weight, blocks in hidden_parts:
        bias = up_bias[blocks].reshape(-1)
        up_sum = (
            jnp.einsum("rd,fd->rf", second_low, up_weight, preferred_element_type=jnp.float32)
            + bias
        )
        activated, gelu_back = jax.vjp(gelu_exact, up_sum)
        act_low = activated.astype(low)
        grad_act = jnp.einsum(
            "rd,fd->rf", grad_down_rows, down_weight, preferred_element_type=jnp.float32
        )
        grad_up = gelu_back(grad_act)[0].astype(low)
        grad_down_weight = jnp.einsum(
            "rf,rd->fd", act_low, grad_down_rows, preferred_element_type=jnp.float32
        )
        grad_up_weight = jnp.einsum(
            "rf,rd->fd", grad_up, second_low, preferred_element_type=jnp.float32
        )
        grads.append((grad_up_weight, grad_down_weight))
        column_sums = jnp.sum(grad_up.astype(jnp.float32), axis=0)
        grad_up_bias = grad_up_bias.at[blocks].set(
            column_sums.reshape(blocks.shape[0], -1)
        )
        second_rows = second_rows + jnp.dot(
            grad_up, up_weight, preferred_element_type=jnp.float32
        )
        down_rows = down_rows + jnp.dot(act_low, down_weight, preferred_element_type=jnp.float32)
    grad_second = reduce_rows(second_rows)
    down = reduce_rows(down_rows) + down_bias
    output = jnp.where(live, middle + down, 0.0).astype(low)
    mlp_share = scatter_hidden(grads)

    grad_down_wide = grad_down.astype(jnp.float32)
    grad_down_bias = jnp.sum(grad_down_wide, axis=0)
    grad_gain_two = jnp.sum(grad_second * normed_two, axis=0)
    grad_shift_two = jnp.sum(grad_second, axis=0)
    grad_middle = grad_down_wide + normalize_back(grad_second, normed_two, factor_two, gain_two)
    grad_branch = grad_middle.astype(low)
    grad_out_weight = jnp.einsum(
        "ro,rd->od", grad_branch, mixed_low, preferred_element_type=jnp.float32
    )
    grad_out_bias = jnp.sum(grad_branch.astype(jnp.float32), axis=0)
    grad_mixed = jnp.dot(grad_branch, full_attn[3 * width :], preferred_element_type=jnp.float32)
    grad_mixed_low = grad_mixed.astype(low).reshape(head_shape)
    grad_queries, grad_keys, grad_values = attend_back(
        queries, keys, values, allowed, scale, grad_mixed_low, log_total
    )
    grad_projected = jnp.concatenate(
        [
            grad_queries.reshape(total_rows, width),
            grad_keys.reshape(total_rows, width),
            grad_values.reshape(total_rows, width),
        ],
        axis=1,
    ).astype(low)
    grad_proj_weight = jnp.einsum(
        "ro,rd->od", grad_projected, first_low, preferred_element_type=jnp.float32
    )
    grad_attn = jnp.concatenate(
        [grad_proj_weight.astype(low), grad_out_weight.astype(low)], axis=0
    )
    attn_share = lax.psum_scatter(grad_attn, "dev", scatter_dimension=0, tiled=True)
    grad_columns = jnp.sum(grad_projected.astype(jnp.float32), axis=0)
    grad_first = jnp.dot(grad_projected, full_attn[: 3 * width], preferred_element_type=jnp.float32)
    grad_gain_one = jnp.sum(grad_first * normed_one, axis=0)
    grad_shift_one = jnp.sum(grad_first, axis=0)
    grad_inputs = grad_middle + normalize_back(grad_first, normed_one, factor_one, gain_one)
    grad_vec = jnp.concatenate(
        [
            grad_gain_one,
            grad_shift_one,
            grad_columns[:width],
            grad_columns[2 * width :],
            grad_out_bias,
            grad_gain_two,
            grad_shift_two,
            grad_down_bias,
            grad_up_bias.reshape(-1),
        ],
        axis=0,
    )
    vec_share = scatter_vectors(grad_vec)
    return (output, grad_inputs, attn_share.astype(jnp.float32), mlp_share, vec_share)


def solution(mesh):
    return jax.shard_map(
        shards,
        mesh=mesh,
        in_specs=(
            P("dev", None),
            P("dev", None),
            P("dev", None),
            P("dev"),
            P("dev", None),
            P(),
            P(),
            P(),
        ),
        out_specs=(P("dev", None), P("dev", None), P("dev", None), P("dev", None), P("dev")),
        check_vma=False,
    )
```

```python
import jax
import jax.numpy as jnp
from jax import lax
from jax.sharding import PartitionSpec as P

D = 1088
HEADS = 17
HEAD_SIZE = 64
FF = 4352


epsilon = 1e-05
neg_large = -1e30


def normalize(values, gain, shift):
    centre = values - jnp.mean(values, axis=-1, keepdims=True)
    spread = jnp.mean(centre * centre, axis=-1, keepdims=True)
    factor = lax.rsqrt(spread + epsilon)
    normed = centre * factor
    return (normed * gain + shift, normed, factor)


def normalize_back(grad_out, normed, factor, gain):
    inner = grad_out * gain
    return factor * (
        inner
        - jnp.mean(inner, axis=-1, keepdims=True)
        - normed * jnp.mean(inner * normed, axis=-1, keepdims=True)
    )


def split_vectors(whole_vec):
    width = D
    pieces = [
        whole_vec[number * width : (number + 1) * width].astype(jnp.float32) for number in range(8)
    ]
    return pieces + [whole_vec[8 * width :].astype(jnp.float32)]


def gelu_exact(values):
    return jax.nn.gelu(values, approximate=False)


def allowed_pairs(keep):
    position = jnp.arange(keep.shape[0], dtype=jnp.int32)
    return (position[None, :] <= position[:, None]) & (keep[None, :] == keep[:, None])


def attend(queries, keys, values, allowed, scale):
    scores = jnp.einsum("qhd,khd->hqk", queries, keys, preferred_element_type=jnp.float32) * scale
    scores = jnp.where(allowed[None], scores, neg_large)
    top = jnp.max(scores, axis=-1, keepdims=True)
    expo = jnp.exp(scores - top)
    total = jnp.sum(expo, axis=-1, keepdims=True)
    weights = (expo / total).astype(jnp.bfloat16)
    mixed = jnp.einsum("hqk,khd->qhd", weights, values, preferred_element_type=jnp.float32)
    return (mixed, top + jnp.log(total))


def attend_back(queries, keys, values, allowed, scale, grad_mixed, log_total):
    scores = jnp.einsum("qhd,khd->hqk", queries, keys, preferred_element_type=jnp.float32) * scale
    scores = jnp.where(allowed[None], scores, neg_large)
    probs = jnp.exp(scores - log_total)
    grad_values = jnp.einsum(
        "hqk,qhd->hdk", probs.astype(jnp.bfloat16), grad_mixed, preferred_element_type=jnp.float32
    )
    grad_probs = jnp.einsum("qhd,khd->hqk", grad_mixed, values, preferred_element_type=jnp.float32)
    inner = jnp.sum(probs * grad_probs, axis=-1, keepdims=True)
    grad_scores = (probs * (grad_probs - inner)).astype(jnp.bfloat16)
    grad_queries = (
        jnp.einsum("hqk,khd->hdq", grad_scores, keys, preferred_element_type=jnp.float32) * scale
    )
    grad_keys = (
        jnp.einsum("hqk,qhd->hdk", grad_scores, queries, preferred_element_type=jnp.float32) * scale
    )
    return (grad_queries, grad_keys, grad_values)


def gather_rows(own):
    across = swap(own, 2)
    beside = swap(own, 1)
    return jnp.concatenate([own, across, beside, swap(across, 1)], axis=0)


def reduce_near(partial):
    half = partial.shape[0] // 2
    low = jnp.bfloat16
    both = partial[:half] + swap(partial[half:].astype(low), 1).astype(jnp.float32)
    rows = half // 2
    return (both[:rows], both[rows:].astype(low))


def after(values, others):
    return lax.optimization_barrier((values, others))[0]


def swap(piece, mask):
    devices = lax.axis_size("dev")
    return lax.ppermute(piece, "dev", [(number, number ^ mask) for number in range(devices)])


def same_low(devices):
    return [list(range(low, devices, 4)) for low in range(4)]


def gather_vectors(own):
    here = lax.axis_index("dev")
    whole = own
    mask = 1
    while mask < lax.axis_size("dev"):
        other = swap(whole, mask)
        upper = (here & mask) != 0
        whole = jnp.concatenate(
            [jnp.where(upper, other, whole), jnp.where(upper, whole, other)], axis=0
        )
        mask *= 2
    return whole


def scatter_vectors(whole):
    here = lax.axis_index("dev")
    mask = lax.axis_size("dev") // 2
    while mask:
        half = whole.shape[0] // 2
        upper = (here & mask) != 0
        mine = jnp.where(upper, whole[half:], whole[:half])
        yours = jnp.where(upper, whole[:half], whole[half:])
        whole = mine + swap(yours, mask)
        mask //= 2
    return whole


def gather_attn(shard, vectors):
    devices = lax.axis_size("dev")
    if devices != 32:
        return (lax.all_gather(shard, "dev", axis=0, tiled=True), gather_vectors(vectors), shard)
    here = lax.axis_index("dev")
    rows, width = shard.shape
    spare = 8
    extra = jnp.pad(vectors[None, :], ((0, spare - 1), (0, width - vectors.shape[0])))
    zero = jnp.concatenate([shard, extra], axis=0)
    one, two, three = swap(zero, 8), swap(zero, 16), swap(zero, 24)
    odd = (here & 8) != 0
    upper = (here & 16) != 0
    near = (jnp.where(odd, one, zero), jnp.where(odd, zero, one))
    far = (jnp.where(odd, three, two), jnp.where(odd, two, three))
    top = jnp.stack([jnp.where(upper, far[0], near[0]), jnp.where(upper, far[1], near[1])])
    bottom = jnp.stack([jnp.where(upper, near[0], far[0]), jnp.where(upper, near[1], far[1])])
    ready = (one, two, three)
    pieces = {(0, 0): top, (0, 1): bottom}
    pieces[4, 0] = swap(top, 4)
    pieces[2, 1] = swap(bottom, 2)
    pieces[2, 0] = swap(top, 2)
    pieces[4, 1] = swap(bottom, 4)
    pieces[6, 0] = swap(pieces[4, 0], 2)
    pieces[6, 1] = swap(pieces[2, 1], 4)
    for place in list(pieces):
        pieces[place[0] ^ 1, place[1]] = swap(pieces[place], 1)
    whole = jnp.zeros((4, 8, rows, width), shard.dtype)
    vector = jnp.zeros((4, 8, 1, vectors.shape[0]), vectors.dtype)
    for (mask, half), piece in pieces.items():
        start = (2 * half, (here & 7) ^ mask, 0, 0)
        whole = lax.dynamic_update_slice(whole, piece[:, None, :rows], start)
        vector = lax.dynamic_update_slice(
            vector, piece[:, None, rows : rows + 1, : vectors.shape[0]], start
        )
    return (whole.reshape(-1, width), vector.reshape(-1), (ready, (pieces[6, 0], pieces[6, 1])))


def scatter_attn(grads, sources):
    devices = lax.axis_size("dev")
    low = jnp.bfloat16
    first, mixed = sources
    own, width = first[0].shape
    if devices != 32:
        product = jnp.concatenate(
            [
                jnp.dot(grads[: 3 * width], first[0], preferred_element_type=jnp.float32),
                jnp.dot(grads[3 * width :], mixed[0], preferred_element_type=jnp.float32),
            ],
            axis=0,
        ).astype(low)
        return lax.psum_scatter(product, "dev", scatter_dimension=0, tiled=True).astype(jnp.float32)
    here = lax.axis_index("dev")
    block = here & 7
    grads = grads.reshape(4, 8, -1, own)
    rows = grads.shape[2]
    order = (6, 2, 4, 0)
    mine = jnp.stack([lax.dynamic_index_in_dim(grads, block ^ mask, 1, False) for mask in order])
    yours = jnp.stack(
        [lax.dynamic_index_in_dim(grads, block ^ mask ^ 1, 1, False) for mask in order]
    )
    both = jnp.concatenate([mine, swap(yours, 1)], axis=-1)
    first = jnp.concatenate(first, axis=0)
    mixed = jnp.concatenate(mixed, axis=0)

    def upper_part(place):
        left = both[place, :2].reshape(2 * rows, 2 * own)
        return jnp.dot(left, first, preferred_element_type=jnp.float32)

    def lower_part(place):
        return jnp.concatenate(
            [
                jnp.dot(both[place, 2], first, preferred_element_type=jnp.float32),
                jnp.dot(both[place, 3], mixed, preferred_element_type=jnp.float32),
            ],
            axis=0,
        )

    def wide(value):
        return value.astype(jnp.float32)

    across_diagonal = swap(upper_part(0).astype(low), 2)
    along_diagonal = swap(lower_part(0).astype(low), 4)
    across_upper = swap(upper_part(1).astype(low), 2)
    along_lower = swap(lower_part(2).astype(low), 4)
    across_lower = swap((lower_part(1) + wide(along_diagonal)).astype(low), 2)
    along_upper = swap((upper_part(2) + wide(across_diagonal)).astype(low), 4)
    upper = upper_part(3) + wide(across_upper) + wide(along_upper)
    lower = lower_part(3) + wide(across_lower) + wide(along_lower)
    total = jnp.concatenate([upper, lower], axis=0).reshape(4, rows, width)
    layer = here >> 3

    def part(mask):
        return lax.dynamic_index_in_dim(total, layer ^ mask, 0, False)

    result = part(0)
    for mask in (1, 2, 3):
        result = result + wide(swap(part(mask).astype(low), 8 * mask))
    return result


def gather_hidden(shard, attn_ready):
    devices = lax.axis_size("dev")
    here = lax.axis_index("dev")
    half = devices // 2
    if devices != 32:
        both = lax.all_gather(
            shard, "dev", axis=0, tiled=True, axis_index_groups=same_low(devices)
        )
        rows = both.shape[0] // 2
        blocks = jnp.arange(half // 4, dtype=jnp.int32) * 4 + (here & 3)
        return [(both[:rows], both[rows:], blocks)]
    layers_ready, all_ready = attn_ready
    held = [shard] + [swap(after(shard, layers_ready), 8 * mask) for mask in (1, 2, 3)]
    moved = [swap(shard, 4)] + [swap(after(piece, all_ready), 4) for piece in held[1:]]
    first = here < half
    block = here & (half - 1)
    blocks = jnp.stack([block, block ^ 8])
    parts = []
    for pieces, numbers in ((held, blocks), (moved, blocks ^ 4)):
        zero, one, two, three = pieces
        up = jnp.concatenate([jnp.where(first, zero, two), jnp.where(first, one, three)], axis=0)
        down = jnp.concatenate([jnp.where(first, two, zero), jnp.where(first, three, one)], axis=0)
        parts.append((up, down, numbers))
    return parts


def scatter_hidden(grads, others):
    devices = lax.axis_size("dev")
    if devices != 32:
        both = jnp.concatenate(grads[0], axis=0).astype(jnp.bfloat16)
        return lax.psum_scatter(
            both, "dev", scatter_dimension=0, tiled=True, axis_index_groups=same_low(devices)
        ).astype(jnp.float32)
    first = lax.axis_index("dev") < devices // 2
    low = jnp.bfloat16
    moved = [swap(part.astype(low), 4) for part in grads[1]]
    moved = after(moved, others)
    up, down = [own + part.astype(jnp.float32) for own, part in zip(grads[0], moved)]
    rows = up.shape[0] // 2
    mine = jnp.where(first, up[:rows], down[:rows])
    two = jnp.where(first, down[:rows], up[:rows]).astype(low)
    one = jnp.where(first, up[rows:], down[rows:]).astype(low)
    three = jnp.where(first, down[rows:], up[rows:]).astype(low)
    return (
        mine
        + swap(one, 8).astype(jnp.float32)
        + swap(two, 16).astype(jnp.float32)
        + swap(three, 24).astype(jnp.float32)
    )


def shards(
    tokens, attn_weight, mlp_weight, vectors, cotangent, seq_lengths, seq_device, seq_offset
):
    total_rows = tokens.shape[0]
    width = D
    scale = HEAD_SIZE ** (-0.5)
    low = jnp.bfloat16
    devices = lax.axis_size("dev")
    here = lax.axis_index("dev")
    chosen = (seq_device == here).astype(jnp.int32)
    begin = jnp.sum(chosen * seq_offset)
    finish = begin + jnp.sum(chosen * seq_lengths)
    positions = jnp.arange(total_rows, dtype=jnp.int32)
    keep = ((positions >= begin) & (positions < finish)).astype(jnp.int32)
    live = keep[:, None] == 1
    allowed = allowed_pairs(keep)
    head_shape = (total_rows, HEADS, HEAD_SIZE)

    full_attn, full_vec, attn_ready = gather_attn(attn_weight, vectors)
    grad_down = jnp.where(live, cotangent, jnp.zeros_like(cotangent))
    hidden_parts = gather_hidden(mlp_weight, attn_ready)
    grad_down_rows = gather_rows(grad_down)

    (
        gain_one,
        shift_one,
        query_bias,
        value_bias,
        out_bias,
        gain_two,
        shift_two,
        down_bias,
        up_bias,
    ) = split_vectors(full_vec)
    up_bias = up_bias.reshape(devices // 2, -1)

    inputs = tokens.astype(jnp.float32)
    first_out, normed_one, factor_one = normalize(inputs, gain_one, shift_one)
    first_low = first_out.astype(low)
    first_beside = swap(first_low, 1)
    projected = jnp.einsum(
        "rd,od->ro", first_low, full_attn[: 3 * width], preferred_element_type=jnp.float32
    )
    queries = (projected[:, :width] + query_bias).astype(low).reshape(head_shape)
    keys = projected[:, width : 2 * width].astype(low).reshape(head_shape)
    values = (projected[:, 2 * width :] + value_bias).astype(low).reshape(head_shape)
    mixed, log_total = attend(queries, keys, values, allowed, scale)
    mixed_low = mixed.reshape(total_rows, width).astype(low)
    mixed_beside = swap(mixed_low, 1)
    branch = (
        jnp.einsum(
            "rd,od->ro", mixed_low, full_attn[3 * width :], preferred_element_type=jnp.float32
        )
        + out_bias
    )
    middle = inputs + branch
    second_out, normed_two, factor_two = normalize(middle, gain_two, shift_two)
    second_low = gather_rows(second_out.astype(low))

    second_rows = 0.0
    kept = []
    grad_up_bias = jnp.zeros_like(up_bias)
    for up_weight, down_weight, blocks in hidden_parts:
        bias = up_bias[blocks].reshape(-1)
        up_sum = (
            jnp.einsum("rd,fd->rf", second_low, up_weight, preferred_element_type=jnp.float32)
            + bias
        )
        activated, gelu_back = jax.vjp(gelu_exact, up_sum)
        act_low = activated.astype(low)
        grad_act = jnp.einsum(
            "rd,fd->rf", grad_down_rows, down_weight, preferred_element_type=jnp.float32
        )
        grad_up = gelu_back(grad_act)[0].astype(low)
        second_rows = second_rows + jnp.dot(
            grad_up, up_weight, preferred_element_type=jnp.float32
        )
        column_sums = jnp.sum(grad_up.astype(jnp.float32), axis=0)
        grad_up_bias = grad_up_bias.at[blocks].set(column_sums.reshape(blocks.shape[0], -1))
        kept.append((act_low, grad_up))
    grad_second, far = reduce_near(second_rows)
    grad_second = grad_second + swap(far, 2).astype(jnp.float32)
    kept = after(kept, far)
    grads = [
        (
            jnp.einsum("rf,rd->fd", grad_up, second_low, preferred_element_type=jnp.float32),
            jnp.einsum("rf,rd->fd", act_low, grad_down_rows, preferred_element_type=jnp.float32),
        )
        for act_low, grad_up in kept
    ]
    down = 0.0
    for (act_low, grad_up), (up_weight, down_weight, blocks) in zip(kept, hidden_parts):
        down = down + jnp.dot(act_low, down_weight, preferred_element_type=jnp.float32)
    down, far = reduce_near(down)
    down = down + swap(far, 2).astype(jnp.float32) + down_bias
    output = jnp.where(live, middle + down, 0.0).astype(low)

    grad_down_wide = grad_down.astype(jnp.float32)
    grad_down_bias = jnp.sum(grad_down_wide, axis=0)
    grad_gain_two = jnp.sum(grad_second * normed_two, axis=0)
    grad_shift_two = jnp.sum(grad_second, axis=0)
    grad_middle = grad_down_wide + normalize_back(grad_second, normed_two, factor_two, gain_two)
    grad_branch = grad_middle.astype(low)
    grad_out_bias = jnp.sum(grad_branch.astype(jnp.float32), axis=0)
    grad_mixed = jnp.dot(grad_branch, full_attn[3 * width :], preferred_element_type=jnp.float32)
    grad_mixed_low = grad_mixed.astype(low).reshape(head_shape)
    grad_queries, grad_keys, grad_values = attend_back(
        queries, keys, values, allowed, scale, grad_mixed_low, log_total
    )
    grad_features = jnp.concatenate(
        [
            grad_queries.reshape(width, total_rows).astype(low),
            grad_keys.reshape(width, total_rows).astype(low),
            grad_values.reshape(width, total_rows).astype(low),
            grad_branch.T,
        ],
        axis=0,
    )
    attn_share = scatter_attn(
        grad_features, ((first_low, first_beside), (mixed_low, mixed_beside))
    )
    mlp_share = scatter_hidden(grads, grad_features)
    grad_projected = grad_features[: 3 * width]
    grad_columns = jnp.sum(grad_projected.astype(jnp.float32), axis=1)
    grad_first = jnp.einsum(
        "fr,fd->rd", grad_projected, full_attn[: 3 * width], preferred_element_type=jnp.float32
    )
    grad_gain_one = jnp.sum(grad_first * normed_one, axis=0)
    grad_shift_one = jnp.sum(grad_first, axis=0)
    grad_inputs = grad_middle + normalize_back(grad_first, normed_one, factor_one, gain_one)
    grad_vec = jnp.concatenate(
        [
            grad_gain_one,
            grad_shift_one,
            grad_columns[:width],
            grad_columns[2 * width :],
            grad_out_bias,
            grad_gain_two,
            grad_shift_two,
            grad_down_bias,
            grad_up_bias.reshape(-1),
        ],
        axis=0,
    )
    vec_share = scatter_vectors(grad_vec)
    return (output, grad_inputs, attn_share, mlp_share, vec_share)


def solution(mesh):
    return jax.shard_map(
        shards,
        mesh=mesh,
        in_specs=(
            P("dev", None),
            P("dev", None),
            P("dev", None),
            P("dev"),
            P("dev", None),
            P(),
            P(),
            P(),
        ),
        out_specs=(P("dev", None), P("dev", None), P("dev", None), P("dev", None), P("dev")),
        check_vma=False,
    )
```

```python
import jax
import jax.numpy as jnp
from jax import lax
from jax.experimental import pallas as pl
from jax.experimental.pallas import tpu as pltpu
from jax.sharding import PartitionSpec as P

D = 1088
HEADS = 17
HEAD_SIZE = 64
FF = 4352


epsilon = 1e-05
neg_large = -1e30


def normalize(values, gain, shift):
    centre = values - jnp.mean(values, axis=-1, keepdims=True)
    spread = jnp.mean(centre * centre, axis=-1, keepdims=True)
    factor = lax.rsqrt(spread + epsilon)
    normed = centre * factor
    return (normed * gain + shift, normed, factor)


def normalize_back(grad_out, normed, factor, gain):
    inner = grad_out * gain
    return factor * (
        inner
        - jnp.mean(inner, axis=-1, keepdims=True)
        - normed * jnp.mean(inner * normed, axis=-1, keepdims=True)
    )


def split_vectors(whole_vec):
    width = D
    pieces = [
        whole_vec[number * width : (number + 1) * width].astype(jnp.float32) for number in range(8)
    ]
    return pieces + [whole_vec[8 * width :].astype(jnp.float32)]


def gelu_parts(values):
    share = 0.5 + 0.5 * lax.erf(values * (0.5**0.5))
    density = jnp.exp(-0.5 * values * values) * ((2.0 * jnp.pi) ** (-0.5))
    return (values * share, share + values * density)


def allowed_pairs(keep):
    position = jnp.arange(keep.shape[0], dtype=jnp.int32)
    return (position[None, :] <= position[:, None]) & (keep[None, :] == keep[:, None])


def attend(queries, keys, values, allowed, scale):
    scores = jnp.einsum("qhd,khd->hqk", queries, keys, preferred_element_type=jnp.float32) * scale
    scores = jnp.where(allowed[None], scores, neg_large)
    top = jnp.max(scores, axis=-1, keepdims=True)
    expo = jnp.exp(scores - top)
    total = jnp.sum(expo, axis=-1, keepdims=True)
    weights = (expo / total).astype(jnp.bfloat16)
    mixed = jnp.einsum("hqk,khd->qhd", weights, values, preferred_element_type=jnp.float32)
    return (mixed, top + jnp.log(total))


def attend_back(queries, keys, values, allowed, scale, grad_mixed, log_total):
    scores = jnp.einsum("qhd,khd->hqk", queries, keys, preferred_element_type=jnp.float32) * scale
    scores = jnp.where(allowed[None], scores, neg_large)
    probs = jnp.exp(scores - log_total)
    grad_values = jnp.einsum(
        "hqk,qhd->hdk", probs.astype(jnp.bfloat16), grad_mixed, preferred_element_type=jnp.float32
    )
    grad_probs = jnp.einsum("qhd,khd->hqk", grad_mixed, values, preferred_element_type=jnp.float32)
    inner = jnp.sum(probs * grad_probs, axis=-1, keepdims=True)
    grad_scores = (probs * (grad_probs - inner)).astype(jnp.bfloat16)
    grad_queries = (
        jnp.einsum("hqk,khd->hdq", grad_scores, keys, preferred_element_type=jnp.float32) * scale
    )
    grad_keys = (
        jnp.einsum("hqk,qhd->hdk", grad_scores, queries, preferred_element_type=jnp.float32) * scale
    )
    return (grad_queries, grad_keys, grad_values)


def gather_rows(own):
    across = swap(own, 2)
    beside = swap(own, 1)
    return jnp.concatenate([own, across, beside, swap(across, 1)], axis=0)


def row_products(left_parts, right_parts, start, stop):
    total = 0.0
    for left, right in zip(left_parts, right_parts):
        total = total + jnp.dot(left[start:stop], right, preferred_element_type=jnp.float32)
    return total


def reduce_near(left_parts, right_parts):
    low = jnp.bfloat16
    rows = left_parts[0].shape[0] // 4
    given = row_products(left_parts, right_parts, 2 * rows, 4 * rows).astype(low)
    taken = swap(given, 1).astype(jnp.float32)
    far = row_products(left_parts, right_parts, rows, 2 * rows) + taken[rows:]
    near = row_products(left_parts, right_parts, 0, rows) + taken[:rows]
    return (near, far.astype(low))


def after(values, others):
    return lax.optimization_barrier((values, others))[0]


def swap(piece, mask):
    devices = lax.axis_size("dev")
    return lax.ppermute(piece, "dev", [(number, number ^ mask) for number in range(devices)])


def same_low(devices):
    return [list(range(low, devices, 4)) for low in range(4)]


def gather_vectors(own):
    here = lax.axis_index("dev")
    whole = own
    mask = 1
    while mask < lax.axis_size("dev"):
        other = swap(whole, mask)
        upper = (here & mask) != 0
        whole = jnp.concatenate(
            [jnp.where(upper, other, whole), jnp.where(upper, whole, other)], axis=0
        )
        mask *= 2
    return whole


def scatter_vectors(whole):
    here = lax.axis_index("dev")
    mask = lax.axis_size("dev") // 2
    while mask:
        half = whole.shape[0] // 2
        upper = (here & mask) != 0
        mine = jnp.where(upper, whole[half:], whole[:half])
        yours = jnp.where(upper, whole[:half], whole[half:])
        whole = mine + swap(yours, mask)
        mask //= 2
    return whole


def z_groups(devices):
    return [list(range(low, devices, 8)) for low in range(8)]


def gather_z(shard):
    devices = lax.axis_size("dev")
    return lax.all_gather(shard, "dev", axis=0, tiled=False, axis_index_groups=z_groups(devices))


def place_blocks(pieces, held):
    block = (lax.axis_index("dev") & 7).astype(jnp.int32).reshape(1)
    arrays = [piece[0] for piece in pieces]
    rows, width = arrays[0].shape[1:]
    count = sum(array.shape[0] for array in arrays)

    def body(block_ref, *refs):
        piece_refs = refs[: len(arrays)]
        three_ref, last_ref, sems = refs[-3:]
        copies = []
        for ref, (array, mask, begin) in zip(piece_refs, pieces):
            target = block_ref[0] ^ mask
            for number in range(array.shape[0]):
                matrix = begin + number
                goal = last_ref.at[target] if matrix == 3 else three_ref.at[matrix, target]
                copies.append(
                    pltpu.make_async_copy(ref.at[number], goal, sems.at[len(copies)])
                )
                copies[-1].start()
        for copy in copies:
            copy.wait()

    anywhere = pl.BlockSpec(memory_space=pl.ANY)
    kind = arrays[0].dtype
    return pl.pallas_call(
        body,
        out_shape=(
            jax.ShapeDtypeStruct((3, 8, rows, width), kind),
            jax.ShapeDtypeStruct((8, rows, width), kind),
        ),
        in_specs=[pl.BlockSpec(memory_space=pltpu.SMEM)]
        + [anywhere] * (len(arrays) + len(held)),
        out_specs=(anywhere, anywhere),
        scratch_shapes=[pltpu.SemaphoreType.DMA((count,))],
        input_output_aliases={1 + len(arrays) + number: number for number in range(len(held))},
        cost_estimate=pl.CostEstimate(
            flops=0, bytes_accessed=4 * count * rows * width, transcendentals=0
        ),
    )(block, *arrays, *held)


def gather_attn(shard):
    devices = lax.axis_size("dev")
    if devices != 32:
        whole = lax.all_gather(shard, "dev", axis=0, tiled=True)
        width = shard.shape[1]
        return (whole[: 3 * width], whole[3 * width :], shard)
    own = gather_z(shard)
    along, across = swap(own, 4), swap(own, 2)
    beside = swap(own, 1)
    upper, lower = swap(along[:2], 2), swap(across[2:], 4)
    pieces = [(own, 0, 0), (beside, 1, 0), (along, 4, 0), (across, 2, 0)]
    pieces += [(swap(along, 1), 5, 0), (swap(across, 1), 3, 0)]
    held = place_blocks(pieces, ())
    pieces = [(upper, 6, 0), (lower, 6, 2), (swap(upper, 1), 7, 0), (swap(lower, 1), 7, 2)]
    three, last = place_blocks(pieces, held)
    width = shard.shape[1]
    return (three.reshape(3 * width, width), last.reshape(width, width), (upper, lower))


def scatter_attn(grads, sources):
    devices = lax.axis_size("dev")
    low = jnp.bfloat16
    first, mixed = sources
    own, width = first[0].shape
    if devices != 32:
        product = jnp.concatenate(
            [
                jnp.dot(grads[: 3 * width], first[0], preferred_element_type=jnp.float32),
                jnp.dot(grads[3 * width :], mixed[0], preferred_element_type=jnp.float32),
            ],
            axis=0,
        ).astype(low)
        return lax.psum_scatter(product, "dev", scatter_dimension=0, tiled=True).astype(jnp.float32)
    here = lax.axis_index("dev")
    block = here & 7
    grads = grads.reshape(4, 8, -1, own)
    rows = grads.shape[2]
    order = (6, 2, 4, 0)
    mine = jnp.stack([lax.dynamic_index_in_dim(grads, block ^ mask, 1, False) for mask in order])
    yours = jnp.stack(
        [lax.dynamic_index_in_dim(grads, block ^ mask ^ 1, 1, False) for mask in order]
    )
    both = jnp.concatenate([mine, swap(yours, 1)], axis=-1)
    first = jnp.concatenate(first, axis=0)
    mixed = jnp.concatenate(mixed, axis=0)

    def upper_part(place):
        left = both[place, :2].reshape(2 * rows, 2 * own)
        return jnp.dot(left, first, preferred_element_type=jnp.float32)

    def lower_part(place):
        return jnp.concatenate(
            [
                jnp.dot(both[place, 2], first, preferred_element_type=jnp.float32),
                jnp.dot(both[place, 3], mixed, preferred_element_type=jnp.float32),
            ],
            axis=0,
        )

    def wide(value):
        return value.astype(jnp.float32)

    across_diagonal = swap(upper_part(0).astype(low), 2)
    along_diagonal = swap(lower_part(0).astype(low), 4)
    across_upper = swap(upper_part(1).astype(low), 2)
    along_lower = swap(lower_part(2).astype(low), 4)
    across_lower = swap((lower_part(1) + wide(along_diagonal)).astype(low), 2)
    along_upper = swap((upper_part(2) + wide(across_diagonal)).astype(low), 4)
    upper = upper_part(3) + wide(across_upper) + wide(along_upper)
    lower = lower_part(3) + wide(across_lower) + wide(along_lower)
    total = jnp.concatenate([upper, lower], axis=0).reshape(4, rows, width)
    return scatter_z(total, here >> 3)


def gather_hidden(shard, near_ready):
    devices = lax.axis_size("dev")
    if devices != 32:
        both = lax.all_gather(
            shard, "dev", axis=0, tiled=True, axis_index_groups=same_low(devices)
        )
        return (both, None)
    cut = 128
    one, two = gather_z(shard[:cut]), gather_z(shard[cut:])
    one = after(one, near_ready)
    return ((one, swap(one, 4)), two)


def hidden_parts(gathered, here, devices, ready):
    half = devices // 2
    one, two = gathered
    if devices != 32:
        rows = one.shape[0] // 2
        blocks = jnp.arange(half // 4, dtype=jnp.int32) * 4 + (here & 3)
        return [(one[:rows], one[rows:], blocks, 0, rows // (half // 4))]
    two = after(two, ready)
    blocks = jnp.stack([here & 7, (here & 7) + 8])
    parts = []
    for pieces, numbers in (((one[0], two), blocks), ((one[1], swap(two, 4)), blocks ^ 4)):
        start = 0
        for piece in pieces:
            rows, width = piece.shape[1:]
            up, down = piece[:2].reshape(2 * rows, width), piece[2:].reshape(2 * rows, width)
            parts.append((up, down, numbers, start, start + rows))
            start += rows
    return parts


def scatter_hidden(grads, others):
    devices = lax.axis_size("dev")
    low = jnp.bfloat16
    if devices != 32:
        both = jnp.concatenate(grads[0], axis=0).astype(low)
        return lax.psum_scatter(
            both, "dev", scatter_dimension=0, tiled=True, axis_index_groups=same_low(devices)
        ).astype(jnp.float32)
    layer = lax.axis_index("dev") >> 3
    moved = [[swap(part.astype(low), 4) for part in pair] for pair in grads[2:]]
    shares = []
    for own, other in zip(grads[:2], moved):
        other = after(other, others)
        total = jnp.concatenate(
            [mine + part.astype(jnp.float32) for mine, part in zip(own, other)], axis=0
        )
        shares.append(scatter_z(total.reshape(4, -1, total.shape[1]), layer))
    return jnp.concatenate(shares, axis=0)


def scatter_z(total, layer):
    low = jnp.bfloat16
    result = lax.dynamic_index_in_dim(total, layer, 0, False)
    for mask in (1, 2, 3):
        part = lax.dynamic_index_in_dim(total, layer ^ mask, 0, False).astype(low)
        result = result + swap(part, 8 * mask).astype(jnp.float32)
    return result


def shards(
    tokens, attn_weight, mlp_weight, vectors, cotangent, seq_lengths, seq_device, seq_offset
):
    total_rows = tokens.shape[0]
    width = D
    scale = HEAD_SIZE ** (-0.5)
    low = jnp.bfloat16
    devices = lax.axis_size("dev")
    here = lax.axis_index("dev")
    chosen = (seq_device == here).astype(jnp.int32)
    begin = jnp.sum(chosen * seq_offset)
    finish = begin + jnp.sum(chosen * seq_lengths)
    positions = jnp.arange(total_rows, dtype=jnp.int32)
    keep = ((positions >= begin) & (positions < finish)).astype(jnp.int32)
    live = keep[:, None] == 1
    allowed = allowed_pairs(keep)
    head_shape = (total_rows, HEADS, HEAD_SIZE)

    full_vec = gather_vectors(vectors)
    grad_down = jnp.where(live, cotangent, jnp.zeros_like(cotangent))
    full_proj, full_out, attn_ready = gather_attn(attn_weight)
    gathered = gather_hidden(mlp_weight, attn_ready)
    grad_down_rows = gather_rows(grad_down)

    (
        gain_one,
        shift_one,
        query_bias,
        value_bias,
        out_bias,
        gain_two,
        shift_two,
        down_bias,
        up_bias,
    ) = split_vectors(full_vec)
    up_bias = up_bias.reshape(devices // 2, -1)

    inputs = tokens.astype(jnp.float32)
    first_out, normed_one, factor_one = normalize(inputs, gain_one, shift_one)
    first_low = first_out.astype(low)
    first_beside = swap(first_low, 1)
    projected = jnp.einsum(
        "rd,od->ro", first_low, full_proj, preferred_element_type=jnp.float32
    )
    queries = (projected[:, :width] + query_bias).astype(low).reshape(head_shape)
    keys = projected[:, width : 2 * width].astype(low).reshape(head_shape)
    values = (projected[:, 2 * width :] + value_bias).astype(low).reshape(head_shape)
    mixed, log_total = attend(queries, keys, values, allowed, scale)
    mixed_low = mixed.reshape(total_rows, width).astype(low)
    mixed_beside = swap(mixed_low, 1)
    branch = (
        jnp.einsum(
            "rd,od->ro", mixed_low, full_out, preferred_element_type=jnp.float32
        )
        + out_bias
    )
    middle = inputs + branch
    second_out, normed_two, factor_two = normalize(middle, gain_two, shift_two)
    second_own = second_out.astype(low)
    second_low = gather_rows(second_own)
    parts = hidden_parts(gathered, here, devices, second_own)

    kept = []
    grad_up_bias = jnp.zeros_like(up_bias)
    for up_weight, down_weight, blocks, start, stop in parts:
        bias = up_bias[:, start:stop][blocks].reshape(-1)
        up_sum = (
            jnp.einsum("rd,fd->rf", second_low, up_weight, preferred_element_type=jnp.float32)
            + bias
        )
        activated, slope = gelu_parts(up_sum)
        grad_act = jnp.einsum(
            "rd,fd->rf", grad_down_rows, down_weight, preferred_element_type=jnp.float32
        )
        grad_up = (grad_act * slope).astype(low)
        column_sums = jnp.sum(grad_up.astype(jnp.float32), axis=0)
        grad_up_bias = grad_up_bias.at[blocks, start:stop].set(
            column_sums.reshape(blocks.shape[0], -1)
        )
        kept.append((activated.astype(low), grad_up))
    grad_second, far = reduce_near([pair[1] for pair in kept], [part[0] for part in parts])
    grad_second = grad_second + swap(far, 2).astype(jnp.float32)
    kept = after(kept, far)
    grads = [
        (
            jnp.einsum("rf,rd->fd", grad_up, second_low, preferred_element_type=jnp.float32),
            jnp.einsum("rf,rd->fd", act_low, grad_down_rows, preferred_element_type=jnp.float32),
        )
        for act_low, grad_up in kept
    ]
    down, down_far = reduce_near([pair[0] for pair in kept], [part[1] for part in parts])

    grad_down_wide = grad_down.astype(jnp.float32)
    grad_down_bias = jnp.sum(grad_down_wide, axis=0)
    grad_gain_two = jnp.sum(grad_second * normed_two, axis=0)
    grad_shift_two = jnp.sum(grad_second, axis=0)
    grad_middle = grad_down_wide + normalize_back(grad_second, normed_two, factor_two, gain_two)
    grad_branch = grad_middle.astype(low)
    grad_out_bias = jnp.sum(grad_branch.astype(jnp.float32), axis=0)
    grad_mixed = jnp.dot(grad_branch, full_out, preferred_element_type=jnp.float32)
    grad_mixed_low = grad_mixed.astype(low).reshape(head_shape)
    grad_queries, grad_keys, grad_values = attend_back(
        queries, keys, values, allowed, scale, grad_mixed_low, log_total
    )
    grad_features = jnp.concatenate(
        [
            grad_queries.reshape(width, total_rows).astype(low),
            grad_keys.reshape(width, total_rows).astype(low),
            grad_values.reshape(width, total_rows).astype(low),
            grad_branch.T,
        ],
        axis=0,
    )
    attn_share = scatter_attn(
        grad_features, ((first_low, first_beside), (mixed_low, mixed_beside))
    )
    mlp_share = scatter_hidden(grads, grad_features)
    down_far = after(swap(down_far, 2), grad_features).astype(jnp.float32)
    output = jnp.where(live, middle + (down + down_far + down_bias), 0.0).astype(low)
    grad_projected = grad_features[: 3 * width]
    grad_columns = jnp.sum(grad_projected.astype(jnp.float32), axis=1)
    grad_first = jnp.einsum(
        "fr,fd->rd", grad_projected, full_proj, preferred_element_type=jnp.float32
    )
    grad_gain_one = jnp.sum(grad_first * normed_one, axis=0)
    grad_shift_one = jnp.sum(grad_first, axis=0)
    grad_inputs = grad_middle + normalize_back(grad_first, normed_one, factor_one, gain_one)
    grad_vec = jnp.concatenate(
        [
            grad_gain_one,
            grad_shift_one,
            grad_columns[:width],
            grad_columns[2 * width :],
            grad_out_bias,
            grad_gain_two,
            grad_shift_two,
            grad_down_bias,
            grad_up_bias.reshape(-1),
        ],
        axis=0,
    )
    vec_share = scatter_vectors(grad_vec)
    return (output, grad_inputs, attn_share, mlp_share, vec_share)


def solution(mesh):
    return jax.shard_map(
        shards,
        mesh=mesh,
        in_specs=(
            P("dev", None),
            P("dev", None),
            P("dev", None),
            P("dev"),
            P("dev", None),
            P(),
            P(),
            P(),
        ),
        out_specs=(P("dev", None), P("dev", None), P("dev", None), P("dev", None), P("dev")),
        check_vma=False,
    )
```

```python
import jax
import jax.numpy as jnp
from jax import lax
from jax.experimental import pallas as pl
from jax.experimental.pallas import tpu as pltpu
from jax.sharding import PartitionSpec as P

D = 1088
HEADS = 17
HEAD_SIZE = 64
FF = 4352
VMEM_LIMIT = 32 * 1024 * 1024


epsilon = 1e-05
neg_large = -1e30


def normalize(values, gain, shift):
    centre = values - jnp.mean(values, axis=-1, keepdims=True)
    spread = jnp.mean(centre * centre, axis=-1, keepdims=True)
    factor = lax.rsqrt(spread + epsilon)
    normed = centre * factor
    return (normed * gain + shift, normed, factor)


def normalize_back(grad_out, normed, factor, gain):
    inner = grad_out * gain
    return factor * (
        inner
        - jnp.mean(inner, axis=-1, keepdims=True)
        - normed * jnp.mean(inner * normed, axis=-1, keepdims=True)
    )


def split_vectors(whole_vec):
    width = D
    pieces = [
        whole_vec[number * width : (number + 1) * width].astype(jnp.float32) for number in range(8)
    ]
    return pieces + [whole_vec[8 * width :].astype(jnp.float32)]


def gelu_parts(values):
    share = 0.5 + 0.5 * lax.erf(values * (0.5**0.5))
    density = jnp.exp(-0.5 * values * values) * ((2.0 * jnp.pi) ** (-0.5))
    return (values * share, share + values * density)


def allowed_pairs(keep):
    position = jnp.arange(keep.shape[0], dtype=jnp.int32)
    return (position[None, :] <= position[:, None]) & (keep[None, :] == keep[:, None])


def attend(queries, keys, values, allowed, scale):
    scores = jnp.einsum("qhd,khd->hqk", queries, keys, preferred_element_type=jnp.float32) * scale
    scores = jnp.where(allowed[None], scores, neg_large)
    top = jnp.max(scores, axis=-1, keepdims=True)
    expo = jnp.exp(scores - top)
    total = jnp.sum(expo, axis=-1, keepdims=True)
    weights = (expo / total).astype(jnp.bfloat16)
    mixed = jnp.einsum("hqk,khd->qhd", weights, values, preferred_element_type=jnp.float32)
    return (mixed, top + jnp.log(total))


def attend_back(queries, keys, values, allowed, scale, grad_mixed, log_total):
    scores = jnp.einsum("qhd,khd->hqk", queries, keys, preferred_element_type=jnp.float32) * scale
    scores = jnp.where(allowed[None], scores, neg_large)
    probs = jnp.exp(scores - log_total)
    grad_values = jnp.einsum(
        "hqk,qhd->hdk", probs.astype(jnp.bfloat16), grad_mixed, preferred_element_type=jnp.float32
    )
    grad_probs = jnp.einsum("qhd,khd->hqk", grad_mixed, values, preferred_element_type=jnp.float32)
    inner = jnp.sum(probs * grad_probs, axis=-1, keepdims=True)
    grad_scores = (probs * (grad_probs - inner)).astype(jnp.bfloat16)
    grad_queries = (
        jnp.einsum("hqk,khd->hdq", grad_scores, keys, preferred_element_type=jnp.float32) * scale
    )
    grad_keys = (
        jnp.einsum("hqk,qhd->hdk", grad_scores, queries, preferred_element_type=jnp.float32) * scale
    )
    return (grad_queries, grad_keys, grad_values)


def gather_rows(own):
    across = swap(own, 2)
    beside = swap(own, 1)
    return jnp.concatenate([own, across, beside, swap(across, 1)], axis=0)


def row_products(left_parts, right_parts, start, stop):
    total = 0.0
    for left, right in zip(left_parts, right_parts):
        total = total + jnp.dot(left[start:stop], right, preferred_element_type=jnp.float32)
    return total


def reduce_near(left_parts, right_parts):
    low = jnp.bfloat16
    rows = left_parts[0].shape[0] // 4
    given = row_products(left_parts, right_parts, 2 * rows, 4 * rows).astype(low)
    taken = swap(given, 1).astype(jnp.float32)
    far = row_products(left_parts, right_parts, rows, 2 * rows) + taken[rows:]
    near = row_products(left_parts, right_parts, 0, rows) + taken[:rows]
    return (near, far.astype(low))


def after(values, others):
    return lax.optimization_barrier((values, others))[0]


def swap(piece, mask):
    devices = lax.axis_size("dev")
    return lax.ppermute(piece, "dev", [(number, number ^ mask) for number in range(devices)])


def same_low(devices):
    return [list(range(low, devices, 4)) for low in range(4)]


def gather_vectors(own):
    here = lax.axis_index("dev")
    whole = own
    mask = 1
    while mask < lax.axis_size("dev"):
        other = swap(whole, mask)
        upper = (here & mask) != 0
        whole = jnp.concatenate(
            [jnp.where(upper, other, whole), jnp.where(upper, whole, other)], axis=0
        )
        mask *= 2
    return whole


def scatter_vectors(whole):
    here = lax.axis_index("dev")
    mask = lax.axis_size("dev") // 2
    while mask:
        half = whole.shape[0] // 2
        upper = (here & mask) != 0
        mine = jnp.where(upper, whole[half:], whole[:half])
        yours = jnp.where(upper, whole[:half], whole[half:])
        whole = mine + swap(yours, mask)
        mask //= 2
    return whole


def z_groups(devices):
    return [list(range(low, devices, 8)) for low in range(8)]


def gather_z(shard):
    devices = lax.axis_size("dev")
    return lax.all_gather(shard, "dev", axis=0, tiled=False, axis_index_groups=z_groups(devices))


def place_blocks(pieces):
    block = (lax.axis_index("dev") & 7).astype(jnp.int32).reshape(1)
    arrays = [piece[0] for piece in pieces]
    rows, width = arrays[0].shape[1:]
    count = sum(array.shape[0] for array in arrays)

    def body(block_ref, *refs):
        piece_refs = refs[: len(arrays)]
        three_ref, last_ref, sems = refs[len(arrays) :]
        copies = []
        for ref, (array, mask, begin) in zip(piece_refs, pieces):
            target = block_ref[0] ^ mask
            for number in range(array.shape[0]):
                matrix = begin + number
                goal = last_ref.at[target] if matrix == 3 else three_ref.at[matrix, target]
                copies.append(
                    pltpu.make_async_copy(ref.at[number], goal, sems.at[len(copies)])
                )
                copies[-1].start()
        for copy in copies:
            copy.wait()

    kind = arrays[0].dtype
    return pl.pallas_call(
        body,
        out_shape=(
            jax.ShapeDtypeStruct((3, 8, rows, width), kind),
            jax.ShapeDtypeStruct((8, rows, width), kind),
        ),
        in_specs=[pl.BlockSpec(memory_space=pltpu.SMEM)]
        + [pl.BlockSpec(memory_space=pl.ANY)] * len(arrays),
        out_specs=(pl.BlockSpec(memory_space=pltpu.VMEM), pl.BlockSpec(memory_space=pltpu.VMEM)),
        scratch_shapes=[pltpu.SemaphoreType.DMA((count,))],
        compiler_params=pltpu.CompilerParams(vmem_limit_bytes=VMEM_LIMIT),
        cost_estimate=pl.CostEstimate(
            flops=0, bytes_accessed=4 * count * rows * width, transcendentals=0
        ),
    )(block, *arrays)


def gather_attn(shard):
    devices = lax.axis_size("dev")
    if devices != 32:
        whole = lax.all_gather(shard, "dev", axis=0, tiled=True)
        width = shard.shape[1]
        return (whole[: 3 * width], whole[3 * width :], shard)
    own = gather_z(shard)
    along, across = swap(own, 4), swap(own, 2)
    beside = swap(own, 1)
    upper, lower = swap(along[:2], 2), swap(across[2:], 4)
    pieces = [(own, 0, 0), (beside, 1, 0), (along, 4, 0), (across, 2, 0)]
    pieces += [(swap(along, 1), 5, 0), (swap(across, 1), 3, 0)]
    pieces += [(upper, 6, 0), (lower, 6, 2), (swap(upper, 1), 7, 0), (swap(lower, 1), 7, 2)]
    three, last = place_blocks(pieces)
    width = shard.shape[1]
    return (three.reshape(3 * width, width), last.reshape(width, width), (upper, lower))


def scatter_attn(grads, sources):
    devices = lax.axis_size("dev")
    low = jnp.bfloat16
    first, mixed = sources
    own, width = first[0].shape
    if devices != 32:
        product = jnp.concatenate(
            [
                jnp.dot(grads[: 3 * width], first[0], preferred_element_type=jnp.float32),
                jnp.dot(grads[3 * width :], mixed[0], preferred_element_type=jnp.float32),
            ],
            axis=0,
        ).astype(low)
        share = lax.psum_scatter(product, "dev", scatter_dimension=0, tiled=True)
        return (lambda: share.astype(jnp.float32), grads)
    pairs = (jnp.stack([first[0], mixed[0]]), jnp.stack([first[1], mixed[1]]))
    blocks = grads.reshape(4, 8, -1, own)
    diagonal, across, along, mine = attn_products(blocks, swap(blocks, 1), pairs)

    across_upper = swap(across[0], 2)
    along_lower = swap(along[1], 4)
    along_diagonal = swap(diagonal[1], 4).astype(jnp.float32)
    across_diagonal = swap(diagonal[0], 2).astype(jnp.float32)
    across_lower = swap((across[1] + along_diagonal).astype(low), 2)
    along_upper = swap((along[0] + across_diagonal).astype(low), 4)

    def finish():
        return scatter_z(mine, ((across_upper, along_upper), (across_lower, along_lower)))

    return (finish, (across[1], along[0]))


def attn_products(mine, beside, pairs):
    block = (lax.axis_index("dev") & 7).astype(jnp.int32).reshape(1)
    rows = mine.shape[2]
    width = pairs[0].shape[2]
    low, wide = jnp.bfloat16, jnp.float32
    kinds = (low, low, low, wide, wide, low, wide, wide)

    def body(block_ref, mine_ref, beside_ref, pair_ref, other_ref, *outs):
        for place, mask in enumerate((6, 2, 4, 0)):
            target = block_ref[0] ^ mask
            for half in range(2):
                out = outs[2 * place + half]

                @pl.loop(0, 2)
                def _(number):
                    side = number if half else 0
                    matrix = 2 * half + number
                    value = jnp.dot(
                        mine_ref[matrix, target], pair_ref[side], preferred_element_type=wide
                    ) + jnp.dot(
                        beside_ref[matrix, target], other_ref[side], preferred_element_type=wide
                    )
                    out[number] = value.astype(out.dtype)

    vmem = pl.BlockSpec(memory_space=pltpu.VMEM)
    outs = pl.pallas_call(
        body,
        out_shape=[jax.ShapeDtypeStruct((2, rows, width), kind) for kind in kinds],
        in_specs=[pl.BlockSpec(memory_space=pltpu.SMEM)] + [vmem] * 4,
        out_specs=[vmem] * 8,
        compiler_params=pltpu.CompilerParams(vmem_limit_bytes=VMEM_LIMIT),
        cost_estimate=pl.CostEstimate(
            flops=64 * rows * mine.shape[3] * width,
            bytes_accessed=30 * 1024 * 1024,
            transcendentals=0,
        ),
    )(block, mine, beside, *pairs)
    return [outs[2 * place : 2 * place + 2] for place in range(4)]


def gather_hidden(shard, near_ready):
    devices = lax.axis_size("dev")
    if devices != 32:
        both = lax.all_gather(
            shard, "dev", axis=0, tiled=True, axis_index_groups=same_low(devices)
        )
        return (both, None)
    cut = 128
    one, two = gather_z(shard[:cut]), gather_z(shard[cut:])
    one = after(one, near_ready)
    return ((one, swap(one, 4)), two)


def pick_blocks(bias, blocks, start, stop):
    picked = lax.dynamic_index_in_dim(bias, blocks, 1, False)
    return picked[:, start:stop].reshape(-1)


def put_blocks(bias, blocks, start, stop, values):
    values = values.reshape(bias.shape[0], 1, stop - start)
    return lax.dynamic_update_slice(bias, values, (0, blocks, start))


def hidden_parts(gathered, here, devices, ready):
    one, two = gathered
    if devices != 32:
        rows = one.shape[0] // 2
        return [(one[:rows], one[rows:], here & 3, 0, rows // (devices // 8))]
    two = after(two, ready)
    parts = []
    for pieces, number in (((one[0], two), here & 7), ((one[1], swap(two, 4)), (here & 7) ^ 4)):
        start = 0
        for piece in pieces:
            rows, width = piece.shape[1:]
            up, down = piece[:2].reshape(2 * rows, width), piece[2:].reshape(2 * rows, width)
            parts.append((up, down, number, start, start + rows))
            start += rows
    return parts


def scatter_hidden(grads, others):
    devices = lax.axis_size("dev")
    low = jnp.bfloat16
    if devices != 32:
        both = jnp.concatenate(grads[0], axis=0).astype(low)
        return lax.psum_scatter(
            both, "dev", scatter_dimension=0, tiled=True, axis_index_groups=same_low(devices)
        ).astype(jnp.float32)
    moved = [[swap(part.astype(low), 4) for part in pair] for pair in grads[2:]]
    shares = []
    for own, other in zip(grads[:2], moved):
        other = after(other, others)
        rows = own[0].shape[0] // 2
        own = [part.reshape(2, rows, -1) for part in own]
        other = [(part.reshape(2, rows, -1),) for part in other]
        shares.append(scatter_z(own, other))
    return jnp.concatenate(shares, axis=0)


def scatter_z(own, others):
    mine, one, two, three = route_z(own, others)
    wide = jnp.float32
    return (
        mine
        + swap(two, 16).astype(wide)
        + swap(three, 24).astype(wide)
        + swap(one, 8).astype(wide)
    )


def route_z(own, others):
    layer = (lax.axis_index("dev") >> 3).astype(jnp.int32).reshape(1)
    rows, width = own[0].shape[1:]
    count = len(others[0])

    def body(layer_ref, *refs):
        outs = refs[-4:]
        for mask, out in enumerate(outs):
            goal = layer_ref[0] ^ mask
            number = goal & 1
            for half in range(2):
                sources = refs[half * (count + 1) : (half + 1) * (count + 1)]

                @pl.when((goal >> 1) == half)
                def _():
                    total = sources[0][number]
                    for source in sources[1:]:
                        total = total + source[number].astype(jnp.float32)
                    out[...] = total.astype(out.dtype)

    vmem = pl.BlockSpec(memory_space=pltpu.VMEM)
    kinds = (jnp.float32, jnp.bfloat16, jnp.bfloat16, jnp.bfloat16)
    return pl.pallas_call(
        body,
        out_shape=[jax.ShapeDtypeStruct((rows, width), kind) for kind in kinds],
        in_specs=[pl.BlockSpec(memory_space=pltpu.SMEM)] + [vmem] * (2 * count + 2),
        out_specs=[vmem] * 4,
        compiler_params=pltpu.CompilerParams(vmem_limit_bytes=VMEM_LIMIT),
        cost_estimate=pl.CostEstimate(
            flops=4 * rows * width, bytes_accessed=30 * rows * width, transcendentals=0
        ),
    )(layer, own[0], *others[0], own[1], *others[1])


def shards(
    tokens, attn_weight, mlp_weight, vectors, cotangent, seq_lengths, seq_device, seq_offset
):
    total_rows = tokens.shape[0]
    width = D
    scale = HEAD_SIZE ** (-0.5)
    low = jnp.bfloat16
    devices = lax.axis_size("dev")
    here = lax.axis_index("dev")
    chosen = (seq_device == here).astype(jnp.int32)
    begin = jnp.sum(chosen * seq_offset)
    finish = begin + jnp.sum(chosen * seq_lengths)
    positions = jnp.arange(total_rows, dtype=jnp.int32)
    keep = ((positions >= begin) & (positions < finish)).astype(jnp.int32)
    live = keep[:, None] == 1
    allowed = allowed_pairs(keep)
    head_shape = (total_rows, HEADS, HEAD_SIZE)

    full_vec = gather_vectors(vectors)
    grad_down = jnp.where(live, cotangent, jnp.zeros_like(cotangent))
    full_proj, full_out, attn_ready = gather_attn(attn_weight)
    gathered = gather_hidden(mlp_weight, attn_ready)
    grad_down_rows = gather_rows(grad_down)

    (
        gain_one,
        shift_one,
        query_bias,
        value_bias,
        out_bias,
        gain_two,
        shift_two,
        down_bias,
        up_bias,
    ) = split_vectors(full_vec)
    low_count = 8 if devices == 32 else 4
    up_bias = up_bias.reshape(devices // 2 // low_count, low_count, -1)

    inputs = tokens.astype(jnp.float32)
    first_out, normed_one, factor_one = normalize(inputs, gain_one, shift_one)
    first_low = first_out.astype(low)
    first_beside = swap(first_low, 1)
    projected = jnp.einsum(
        "rd,od->ro", first_low, full_proj, preferred_element_type=jnp.float32
    )
    queries = (projected[:, :width] + query_bias).astype(low).reshape(head_shape)
    keys = projected[:, width : 2 * width].astype(low).reshape(head_shape)
    values = (projected[:, 2 * width :] + value_bias).astype(low).reshape(head_shape)
    mixed, log_total = attend(queries, keys, values, allowed, scale)
    mixed_low = mixed.reshape(total_rows, width).astype(low)
    mixed_beside = swap(mixed_low, 1)
    branch = (
        jnp.einsum(
            "rd,od->ro", mixed_low, full_out, preferred_element_type=jnp.float32
        )
        + out_bias
    )
    middle = inputs + branch
    second_out, normed_two, factor_two = normalize(middle, gain_two, shift_two)
    second_own = second_out.astype(low)
    second_low = gather_rows(second_own)
    parts = hidden_parts(gathered, here, devices, second_own)

    kept = []
    grad_up_bias = jnp.zeros_like(up_bias)
    for up_weight, down_weight, blocks, start, stop in parts:
        bias = pick_blocks(up_bias, blocks, start, stop)
        up_sum = (
            jnp.einsum("rd,fd->rf", second_low, up_weight, preferred_element_type=jnp.float32)
            + bias
        )
        activated, slope = gelu_parts(up_sum)
        grad_act = jnp.einsum(
            "rd,fd->rf", grad_down_rows, down_weight, preferred_element_type=jnp.float32
        )
        grad_up = (grad_act * slope).astype(low)
        column_sums = jnp.sum(grad_up.astype(jnp.float32), axis=0)
        grad_up_bias = put_blocks(grad_up_bias, blocks, start, stop, column_sums)
        kept.append((activated.astype(low), grad_up))
    grad_second, far = reduce_near([pair[1] for pair in kept], [part[0] for part in parts])
    grad_second = grad_second + swap(far, 2).astype(jnp.float32)
    kept = after(kept, far)
    grads = [
        (
            jnp.einsum("rf,rd->fd", grad_up, second_low, preferred_element_type=jnp.float32),
            jnp.einsum("rf,rd->fd", act_low, grad_down_rows, preferred_element_type=jnp.float32),
        )
        for act_low, grad_up in kept
    ]
    down, down_far = reduce_near([pair[0] for pair in kept], [part[1] for part in parts])

    grad_down_wide = grad_down.astype(jnp.float32)
    grad_down_bias = jnp.sum(grad_down_wide, axis=0)
    grad_gain_two = jnp.sum(grad_second * normed_two, axis=0)
    grad_shift_two = jnp.sum(grad_second, axis=0)
    grad_middle = grad_down_wide + normalize_back(grad_second, normed_two, factor_two, gain_two)
    grad_branch = grad_middle.astype(low)
    grad_out_bias = jnp.sum(grad_branch.astype(jnp.float32), axis=0)
    grad_mixed = jnp.dot(grad_branch, full_out, preferred_element_type=jnp.float32)
    grad_mixed_low = grad_mixed.astype(low).reshape(head_shape)
    grad_queries, grad_keys, grad_values = attend_back(
        queries, keys, values, allowed, scale, grad_mixed_low, log_total
    )
    grad_features = jnp.concatenate(
        [
            grad_queries.reshape(width, total_rows).astype(low),
            grad_keys.reshape(width, total_rows).astype(low),
            grad_values.reshape(width, total_rows).astype(low),
            grad_branch.T,
        ],
        axis=0,
    )
    attn_finish, attn_sent = scatter_attn(
        grad_features, ((first_low, first_beside), (mixed_low, mixed_beside))
    )
    mlp_share = scatter_hidden(grads, attn_sent)
    attn_share = attn_finish()
    grad_features = after(grad_features, attn_sent)
    down_far = after(swap(down_far, 2), attn_sent).astype(jnp.float32)
    output = jnp.where(live, middle + (down + down_far + down_bias), 0.0).astype(low)
    grad_projected = grad_features[: 3 * width]
    grad_columns = jnp.sum(grad_projected.astype(jnp.float32), axis=1)
    grad_first = jnp.einsum(
        "fr,fd->rd", grad_projected, full_proj, preferred_element_type=jnp.float32
    )
    grad_gain_one = jnp.sum(grad_first * normed_one, axis=0)
    grad_shift_one = jnp.sum(grad_first, axis=0)
    grad_inputs = grad_middle + normalize_back(grad_first, normed_one, factor_one, gain_one)
    grad_vec = jnp.concatenate(
        [
            grad_gain_one,
            grad_shift_one,
            grad_columns[:width],
            grad_columns[2 * width :],
            grad_out_bias,
            grad_gain_two,
            grad_shift_two,
            grad_down_bias,
            grad_up_bias.reshape(-1),
        ],
        axis=0,
    )
    vec_share = scatter_vectors(grad_vec)
    return (output, grad_inputs, attn_share, mlp_share, vec_share)


def solution(mesh):
    return jax.shard_map(
        shards,
        mesh=mesh,
        in_specs=(
            P("dev", None),
            P("dev", None),
            P("dev", None),
            P("dev"),
            P("dev", None),
            P(),
            P(),
            P(),
        ),
        out_specs=(P("dev", None), P("dev", None), P("dev", None), P("dev", None), P("dev")),
        check_vma=False,
    )
```

```python
import jax
import jax.numpy as jnp
from jax import lax
from jax.experimental import pallas as pl
from jax.experimental.pallas import tpu as pltpu
from jax.sharding import PartitionSpec as P

D = 1088
HEADS = 17
HEAD_SIZE = 64
FF = 4352
VMEM_LIMIT = 32 * 1024 * 1024


epsilon = 1e-05
neg_large = -1e30


def normalize(values, gain, shift):
    centre = values - jnp.mean(values, axis=-1, keepdims=True)
    spread = jnp.mean(centre * centre, axis=-1, keepdims=True)
    factor = lax.rsqrt(spread + epsilon)
    normed = centre * factor
    return (normed * gain + shift, normed, factor)


def normalize_back(grad_out, normed, factor, gain):
    inner = grad_out * gain
    return factor * (
        inner
        - jnp.mean(inner, axis=-1, keepdims=True)
        - normed * jnp.mean(inner * normed, axis=-1, keepdims=True)
    )


def split_vectors(whole_vec):
    width = D
    pieces = [
        whole_vec[number * width : (number + 1) * width].astype(jnp.float32) for number in range(8)
    ]
    return pieces + [whole_vec[8 * width :].astype(jnp.float32)]


def gelu_parts(values):
    share = 0.5 + 0.5 * lax.erf(values * (0.5**0.5))
    density = jnp.exp(-0.5 * values * values) * ((2.0 * jnp.pi) ** (-0.5))
    return (values * share, share + values * density)


def allowed_pairs(keep):
    position = jnp.arange(keep.shape[0], dtype=jnp.int32)
    return (position[None, :] <= position[:, None]) & (keep[None, :] == keep[:, None])


def attend(queries, keys, values, allowed, scale):
    scores = jnp.einsum("qhd,khd->hqk", queries, keys, preferred_element_type=jnp.float32) * scale
    scores = jnp.where(allowed[None], scores, neg_large)
    top = jnp.max(scores, axis=-1, keepdims=True)
    expo = jnp.exp(scores - top)
    total = jnp.sum(expo, axis=-1, keepdims=True)
    weights = (expo / total).astype(jnp.bfloat16)
    mixed = jnp.einsum("hqk,khd->qhd", weights, values, preferred_element_type=jnp.float32)
    return (mixed, top + jnp.log(total))


VMEM = pl.BlockSpec(memory_space=pltpu.VMEM)
SMEM = pl.BlockSpec(memory_space=pltpu.SMEM)


def local_kernel(body, outs, operands, flops, specs=None):
    outs = [jax.ShapeDtypeStruct(shape, kind) for shape, kind in outs]
    moved = sum(array.size * array.dtype.itemsize for array in (*outs, *operands))
    return pl.pallas_call(
        body,
        out_shape=outs,
        in_specs=specs or [VMEM] * len(operands),
        out_specs=[VMEM] * len(outs),
        compiler_params=pltpu.CompilerParams(vmem_limit_bytes=VMEM_LIMIT),
        cost_estimate=pl.CostEstimate(flops=flops, bytes_accessed=moved, transcendentals=0),
    )(*operands)


def product(left, right, left_axis, right_axis):
    return lax.dot_general(
        left, right, (((left_axis,), (right_axis,)), ((), ())), preferred_element_type=jnp.float32
    )


def attend_back(queries, keys, values, span, scale, grad_mixed, log_total):
    width, rows = queries.shape
    low = jnp.bfloat16

    def body(span_ref, q_ref, k_ref, v_ref, do_ref, log_ref, out_ref):
        begin, finish = span_ref[0], span_ref[1]

        def inside(axis):
            position = lax.broadcasted_iota(jnp.int32, (rows, rows), axis)
            return (position, (position >= begin) & (position < finish))

        key_pos, key_live = inside(0)
        query_pos, query_live = inside(1)
        allowed = (key_pos <= query_pos) & (key_live == query_live)

        @pl.loop(0, HEADS)
        def _(head):
            part = pl.ds(pl.multiple_of(head * HEAD_SIZE, HEAD_SIZE), HEAD_SIZE)
            q, k, v, do = q_ref[part, :], k_ref[part, :], v_ref[part, :], do_ref[part, :]
            scores = jnp.where(allowed, product(k, q, 0, 0) * scale, neg_large)
            probs = jnp.exp(scores - log_ref[head])
            out_ref[2, part, :] = product(do, probs.astype(low), 1, 1).astype(low)
            grad_probs = product(v, do, 0, 0)
            inner = jnp.sum(probs * grad_probs, axis=0, keepdims=True)
            grad_scores = (probs * (grad_probs - inner)).astype(low)
            out_ref[0, part, :] = (product(k, grad_scores, 1, 0) * scale).astype(low)
            out_ref[1, part, :] = (product(q, grad_scores, 1, 1) * scale).astype(low)

    return local_kernel(
        body,
        [((3, width, rows), low)],
        (span, queries, keys, values, grad_mixed, log_total),
        10 * rows * rows * width,
        [SMEM] + [VMEM] * 5,
    )[0]


def mlp_block(row_pair, grad_pair, weights, biases, before, last):
    rows, width = row_pair[0].shape
    low, wide = jnp.bfloat16, jnp.float32
    hidden = [2 * weight.shape[1] for weight in weights]
    outs = []
    for count in hidden:
        outs += [((2, rows, count), low), ((2, rows, count), low), ((1, count), wide)]
    sums = len(outs)
    if last:
        outs += [((rows, width), wide), ((rows, width), low)]
    else:
        outs += [((2, rows, width), wide)]
    number = len(weights)

    def body(*refs):
        row_refs, grad_refs = refs[:2], refs[2:4]
        weight_refs, bias_refs = refs[4 : 4 + number], refs[4 + number : 4 + 2 * number]
        out_refs = refs[-len(outs) :]
        for side in range(2):
            total = None if before is None else refs[4 + 2 * number][side]
            for place in range(number):
                weight, count = weight_refs[place], hidden[place]
                up = weight[0:2].reshape(count, width)
                down = weight[2:4].reshape(count, width)
                up_sum = product(row_refs[side][...], up, 1, 1) + bias_refs[place][...]
                activated, slope = gelu_parts(up_sum)
                grad_act = product(grad_refs[side][...], down, 1, 1)
                grad_up = (grad_act * slope).astype(low)
                act_ref, up_ref, sum_ref = out_refs[3 * place : 3 * place + 3]
                act_ref[side] = activated.astype(low)
                up_ref[side] = grad_up
                columns = jnp.sum(grad_up.astype(wide), axis=0, keepdims=True)
                sum_ref[...] = columns if side == 0 else sum_ref[...] + columns
                term = product(grad_up, up, 1, 0)
                total = term if total is None else total + term
            if last:
                out = out_refs[sums + side]
                out[...] = total.astype(out.dtype)
            else:
                out_refs[sums][side] = total

    operands = (*row_pair, *grad_pair, *weights, *biases)
    operands += () if before is None else (before,)
    result = local_kernel(body, outs, operands, 12 * rows * width * sum(hidden))
    return ([result[3 * place : 3 * place + 3] for place in range(number)], result[sums:])


def mlp_weight_grads(blocks, rows, grads, kind):
    width = rows[0].shape[1]
    operands, outs, number = [], [], len(rows)
    for near, far in blocks:
        operands += [near[0], far[0], near[1], far[1]]
        count = near[0].shape[2]
        outs += [((2, count // 2, width), kind)] * 2

    def body(*refs):
        row_refs = refs[len(operands) : len(operands) + number]
        grad_refs = refs[len(operands) + number : len(operands) + 2 * number]
        out_refs = refs[-len(outs) :]
        for place in range(len(blocks)):
            sources = refs[4 * place : 4 * place + 4]
            for out, pair, others in (
                (out_refs[2 * place], sources[2:], row_refs),
                (out_refs[2 * place + 1], sources[:2], grad_refs),
            ):
                total = None
                for which in range(number):
                    term = product(pair[which // 2][which % 2], others[which][...], 0, 0)
                    total = term if total is None else total + term
                out[...] = total.reshape(out.shape).astype(kind)

    flops = sum(16 * rows[0].shape[0] * near[0].shape[2] * width for near, far in blocks)
    result = local_kernel(body, outs, (*operands, *rows, *grads), flops)
    return [tuple(result[2 * place : 2 * place + 2]) for place in range(len(blocks))]


def mlp_outputs(blocks, weights):
    rows, width = blocks[0][0][0].shape[1], weights[0].shape[2]
    number = len(weights)
    operands = [near[0] for near, far in blocks] + [far[0] for near, far in blocks]

    def body(*refs):
        weight_refs, out_refs = refs[2 * number : 3 * number], refs[-2:]
        for group in range(2):
            for side in range(2):
                total = None
                for place in range(number):
                    weight = weight_refs[place]
                    down = weight[2:4].reshape(2 * weight.shape[1], width)
                    term = product(refs[group * number + place][side], down, 1, 0)
                    total = term if total is None else total + term
                out_refs[side][group] = total.astype(out_refs[side].dtype)

    outs = [((2, rows, width), jnp.float32), ((2, rows, width), jnp.bfloat16)]
    flops = 16 * rows * width * sum(weight.shape[1] for weight in weights)
    return local_kernel(body, outs, (*operands, *weights), flops)


def gather_rows(own):
    across = swap(own, 2)
    beside = swap(own, 1)
    return ((own, beside), (across, swap(across, 1)))


def after(values, others):
    return lax.optimization_barrier((values, others))[0]


def swap(piece, mask):
    devices = lax.axis_size("dev")
    return lax.ppermute(piece, "dev", [(number, number ^ mask) for number in range(devices)])


def same_low(devices):
    return [list(range(low, devices, 4)) for low in range(4)]


def gather_vectors(own):
    here = lax.axis_index("dev")
    whole = own
    mask = 1
    while mask < lax.axis_size("dev"):
        other = swap(whole, mask)
        upper = (here & mask) != 0
        whole = jnp.concatenate(
            [jnp.where(upper, other, whole), jnp.where(upper, whole, other)], axis=0
        )
        mask *= 2
    return whole


def scatter_vectors(whole):
    here = lax.axis_index("dev")
    mask = lax.axis_size("dev") // 2
    while mask:
        half = whole.shape[0] // 2
        upper = (here & mask) != 0
        mine = jnp.where(upper, whole[half:], whole[:half])
        yours = jnp.where(upper, whole[:half], whole[half:])
        whole = mine + swap(yours, mask)
        mask //= 2
    return whole


def z_groups(devices):
    return [list(range(low, devices, 8)) for low in range(8)]


def gather_z(shard):
    devices = lax.axis_size("dev")
    return lax.all_gather(shard, "dev", axis=0, tiled=False, axis_index_groups=z_groups(devices))


def place_blocks(pieces):
    block = (lax.axis_index("dev") & 7).astype(jnp.int32).reshape(1)
    arrays = [piece[0] for piece in pieces]
    rows, width = arrays[0].shape[1:]
    count = sum(array.shape[0] for array in arrays)

    def body(block_ref, *refs):
        piece_refs = refs[: len(arrays)]
        three_ref, last_ref, sems = refs[len(arrays) :]
        copies = []
        for ref, (array, mask, begin) in zip(piece_refs, pieces):
            target = block_ref[0] ^ mask
            for number in range(array.shape[0]):
                matrix = begin + number
                goal = last_ref.at[target] if matrix == 3 else three_ref.at[matrix, target]
                copies.append(
                    pltpu.make_async_copy(ref.at[number], goal, sems.at[len(copies)])
                )
                copies[-1].start()
        for copy in copies:
            copy.wait()

    kind = arrays[0].dtype
    return pl.pallas_call(
        body,
        out_shape=(
            jax.ShapeDtypeStruct((3, 8, rows, width), kind),
            jax.ShapeDtypeStruct((8, rows, width), kind),
        ),
        in_specs=[pl.BlockSpec(memory_space=pltpu.SMEM)]
        + [pl.BlockSpec(memory_space=pl.ANY)] * len(arrays),
        out_specs=(pl.BlockSpec(memory_space=pltpu.VMEM), pl.BlockSpec(memory_space=pltpu.VMEM)),
        scratch_shapes=[pltpu.SemaphoreType.DMA((count,))],
        compiler_params=pltpu.CompilerParams(vmem_limit_bytes=VMEM_LIMIT),
        cost_estimate=pl.CostEstimate(
            flops=0, bytes_accessed=4 * count * rows * width, transcendentals=0
        ),
    )(block, *arrays)


def gather_attn(shard):
    devices = lax.axis_size("dev")
    if devices != 32:
        whole = lax.all_gather(shard, "dev", axis=0, tiled=True)
        width = shard.shape[1]
        return (whole[: 3 * width], whole[3 * width :], shard)
    own = gather_z(shard)
    along, across = swap(own, 4), swap(own, 2)
    beside = swap(own, 1)
    upper, lower = swap(along[:2], 2), swap(across[2:], 4)
    pieces = [(own, 0, 0), (beside, 1, 0), (along, 4, 0), (across, 2, 0)]
    pieces += [(swap(along, 1), 5, 0), (swap(across, 1), 3, 0)]
    pieces += [(upper, 6, 0), (lower, 6, 2), (swap(upper, 1), 7, 0), (swap(lower, 1), 7, 2)]
    three, last = place_blocks(pieces)
    width = shard.shape[1]
    return (three.reshape(3 * width, width), last.reshape(width, width), (upper, lower))


def scatter_attn(grads, sources):
    devices = lax.axis_size("dev")
    low = jnp.bfloat16
    first, mixed = sources
    own, width = first[0].shape
    if devices != 32:
        product = jnp.concatenate(
            [
                jnp.dot(grads[0].reshape(3 * width, own), first[0], preferred_element_type=jnp.float32),
                jnp.dot(grads[1], mixed[0], preferred_element_type=jnp.float32),
            ],
            axis=0,
        ).astype(low)
        share = lax.psum_scatter(product, "dev", scatter_dimension=0, tiled=True)
        return (lambda: share.astype(jnp.float32), grads)
    pairs = (jnp.stack([first[0], mixed[0]]), jnp.stack([first[1], mixed[1]]))
    grads = [part.reshape(-1, 8, width // 8, own) for part in grads]
    diagonal, across, along, mine = attn_products(grads, [swap(part, 1) for part in grads], pairs)

    across_upper = swap(across[0], 2)
    along_lower = swap(along[1], 4)
    along_diagonal = swap(diagonal[1], 4).astype(jnp.float32)
    across_diagonal = swap(diagonal[0], 2).astype(jnp.float32)
    across_lower = swap((across[1] + along_diagonal).astype(low), 2)
    along_upper = swap((along[0] + across_diagonal).astype(low), 4)

    def finish():
        return scatter_z(mine, ((across_upper, along_upper), (across_lower, along_lower)))

    return (finish, (across[1], along[0]))


def attn_products(mine, beside, pairs):
    block = (lax.axis_index("dev") & 7).astype(jnp.int32).reshape(1)
    rows = mine[0].shape[2]
    width = pairs[0].shape[2]
    low, wide = jnp.bfloat16, jnp.float32
    kinds = (low, low, low, wide, wide, low, wide, wide)

    def body(block_ref, *refs):
        (three, last), (three_beside, last_beside) = refs[:2], refs[2:4]
        pair_ref, other_ref = refs[4:6]
        outs = refs[6:]
        for place, mask in enumerate((6, 2, 4, 0)):
            target = block_ref[0] ^ mask
            for half in range(2):
                out = outs[2 * place + half]
                for number in range(2):
                    matrix = 2 * half + number
                    left = last[0, target] if matrix == 3 else three[matrix, target]
                    left_beside = (
                        last_beside[0, target] if matrix == 3 else three_beside[matrix, target]
                    )
                    side = 1 if matrix == 3 else 0
                    value = product(left, pair_ref[side], 1, 0)
                    value = value + product(left_beside, other_ref[side], 1, 0)
                    out[number] = value.astype(out.dtype)

    outs = local_kernel(
        body,
        [((2, rows, width), kind) for kind in kinds],
        (block, *mine, *beside, *pairs),
        64 * rows * mine[0].shape[3] * width,
        [SMEM] + [VMEM] * 6,
    )
    return [outs[2 * place : 2 * place + 2] for place in range(4)]


def gather_hidden(shard, near_ready):
    devices = lax.axis_size("dev")
    if devices != 32:
        both = lax.all_gather(
            shard, "dev", axis=0, tiled=True, axis_index_groups=same_low(devices)
        )
        return (both, None)
    cut = 128
    one, two = gather_z(shard[:cut]), gather_z(shard[cut:])
    one = after(one, near_ready)
    return ((one, swap(one, 4)), two)


def pick_blocks(bias, blocks, start, stop):
    picked = lax.dynamic_index_in_dim(bias, blocks, 1, False)
    return picked[:, start:stop].reshape(-1)


def put_blocks(bias, blocks, start, stop, values):
    values = values.reshape(bias.shape[0], 1, stop - start)
    return lax.dynamic_update_slice(bias, values, (0, blocks, start))


def hidden_parts(gathered, here, devices, ready):
    one, two = gathered
    if devices != 32:
        rows = one.shape[0] // 4
        return [[(one.reshape(4, rows, -1), here & 3, 0, rows // (devices // 16))]]
    two = after(two, ready)
    cut, end = one[0].shape[1], one[0].shape[1] + two.shape[1]
    own, other = here & 7, (here & 7) ^ 4
    return [
        [(one[0], own, 0, cut), (two, own, cut, end)],
        [(one[1], other, 0, cut), (swap(two, 4), other, cut, end)],
    ]


def scatter_hidden(own, others, ready):
    devices = lax.axis_size("dev")
    low = jnp.bfloat16
    if devices != 32:
        width = own[0][0].shape[2]
        both = jnp.concatenate([part.reshape(-1, width) for part in own[0]], axis=0).astype(low)
        return lax.psum_scatter(
            both, "dev", scatter_dimension=0, tiled=True, axis_index_groups=same_low(devices)
        ).astype(jnp.float32)
    moved = [[swap(part, 4) for part in pair] for pair in others]
    shares = [
        scatter_z(mine, [(part,) for part in after(other, ready)])
        for mine, other in zip(own, moved)
    ]
    return jnp.concatenate(shares, axis=0)


def scatter_z(own, others):
    mine, one, two, three = route_z(own, others)
    wide = jnp.float32
    return (
        mine
        + swap(two, 16).astype(wide)
        + swap(three, 24).astype(wide)
        + swap(one, 8).astype(wide)
    )


def route_z(own, others):
    layer = (lax.axis_index("dev") >> 3).astype(jnp.int32).reshape(1)
    rows, width = own[0].shape[1:]
    count = len(others[0])

    def body(layer_ref, *refs):
        outs = refs[-4:]
        for mask, out in enumerate(outs):
            goal = layer_ref[0] ^ mask
            number = goal & 1
            for half in range(2):
                sources = refs[half * (count + 1) : (half + 1) * (count + 1)]

                @pl.when((goal >> 1) == half)
                def _():
                    total = sources[0][number]
                    for source in sources[1:]:
                        total = total + source[number].astype(jnp.float32)
                    out[...] = total.astype(out.dtype)

    vmem = pl.BlockSpec(memory_space=pltpu.VMEM)
    kinds = (jnp.float32, jnp.bfloat16, jnp.bfloat16, jnp.bfloat16)
    return pl.pallas_call(
        body,
        out_shape=[jax.ShapeDtypeStruct((rows, width), kind) for kind in kinds],
        in_specs=[pl.BlockSpec(memory_space=pltpu.SMEM)] + [vmem] * (2 * count + 2),
        out_specs=[vmem] * 4,
        compiler_params=pltpu.CompilerParams(vmem_limit_bytes=VMEM_LIMIT),
        cost_estimate=pl.CostEstimate(
            flops=4 * rows * width, bytes_accessed=30 * rows * width, transcendentals=0
        ),
    )(layer, own[0], *others[0], own[1], *others[1])


def shards(
    tokens, attn_weight, mlp_weight, vectors, cotangent, seq_lengths, seq_device, seq_offset
):
    total_rows = tokens.shape[0]
    width = D
    scale = HEAD_SIZE ** (-0.5)
    low = jnp.bfloat16
    devices = lax.axis_size("dev")
    here = lax.axis_index("dev")
    chosen = (seq_device == here).astype(jnp.int32)
    begin = jnp.sum(chosen * seq_offset)
    finish = begin + jnp.sum(chosen * seq_lengths)
    positions = jnp.arange(total_rows, dtype=jnp.int32)
    keep = ((positions >= begin) & (positions < finish)).astype(jnp.int32)
    live = keep[:, None] == 1
    allowed = allowed_pairs(keep)
    head_shape = (total_rows, HEADS, HEAD_SIZE)

    full_vec = gather_vectors(vectors)
    grad_down = jnp.where(live, cotangent, jnp.zeros_like(cotangent))
    full_proj, full_out, attn_ready = gather_attn(attn_weight)
    gathered = gather_hidden(mlp_weight, attn_ready)
    grad_down_rows = gather_rows(grad_down)

    (
        gain_one,
        shift_one,
        query_bias,
        value_bias,
        out_bias,
        gain_two,
        shift_two,
        down_bias,
        up_bias,
    ) = split_vectors(full_vec)
    low_count = 8 if devices == 32 else 4
    up_bias = up_bias.reshape(devices // 2 // low_count, low_count, -1)

    inputs = tokens.astype(jnp.float32)
    first_out, normed_one, factor_one = normalize(inputs, gain_one, shift_one)
    first_low = first_out.astype(low)
    first_beside = swap(first_low, 1)
    projected = jnp.einsum(
        "rd,od->ro", first_low, full_proj, preferred_element_type=jnp.float32
    )
    queries = (projected[:, :width] + query_bias).astype(low).reshape(head_shape)
    keys = projected[:, width : 2 * width].astype(low).reshape(head_shape)
    values = (projected[:, 2 * width :] + value_bias).astype(low).reshape(head_shape)
    mixed, log_total = attend(queries, keys, values, allowed, scale)
    mixed_low = mixed.reshape(total_rows, width).astype(low)
    mixed_beside = swap(mixed_low, 1)
    branch = (
        jnp.einsum(
            "rd,od->ro", mixed_low, full_out, preferred_element_type=jnp.float32
        )
        + out_bias
    )
    middle = inputs + branch
    second_out, normed_two, factor_two = normalize(middle, gain_two, shift_two)
    second_own = second_out.astype(low)
    near, far = gather_rows(second_own)
    parts = hidden_parts(gathered, here, devices, second_own)
    near_grads, far_grads = grad_down_rows

    sides = []
    near_sum = far_sum = None
    grad_up_bias = jnp.zeros_like(up_bias)
    for place, side in enumerate(parts):
        weights = [part[0] for part in side]
        biases = [pick_blocks(up_bias, *part[1:]).reshape(1, -1) for part in side]
        last = place == len(parts) - 1
        near_blocks, near_sum = mlp_block(near, near_grads, weights, biases, near_sum, last)
        far_blocks, far_sum = mlp_block(far, far_grads, weights, biases, far_sum, last)
        if not last:
            near_sum, far_sum = near_sum[0], far_sum[0]
        for part, one, two in zip(side, near_blocks, far_blocks):
            grad_up_bias = put_blocks(grad_up_bias, *part[1:], (one[2] + two[2]).reshape(-1))
        sides.append([(one[:2], two[:2]) for one, two in zip(near_blocks, far_blocks)])
    far_total = (far_sum[0] + swap(far_sum[1], 1).astype(jnp.float32)).astype(low)
    near_taken = swap(near_sum[1], 1)
    grad_second = near_sum[0] + near_taken.astype(jnp.float32)
    sides = after(sides, far_total)
    grad_second = grad_second + swap(far_total, 2).astype(jnp.float32)
    all_rows, all_grads = near + far, near_grads + far_grads
    other_grads = [mlp_weight_grads(side, all_rows, all_grads, low) for side in sides[1:]]
    own_grads = mlp_weight_grads(sides[0], all_rows, all_grads, jnp.float32)
    down_keep, down_give = mlp_outputs(sum(sides, []), [part[0] for side in parts for part in side])
    down_taken = swap(down_give, 1).astype(jnp.float32)
    down = down_keep[0] + down_taken[0]
    down_far = (down_keep[1] + down_taken[1]).astype(low)

    grad_down_wide = grad_down.astype(jnp.float32)
    grad_down_bias = jnp.sum(grad_down_wide, axis=0)
    grad_gain_two = jnp.sum(grad_second * normed_two, axis=0)
    grad_shift_two = jnp.sum(grad_second, axis=0)
    grad_middle = grad_down_wide + normalize_back(grad_second, normed_two, factor_two, gain_two)
    grad_branch = grad_middle.astype(low)
    grad_out_bias = jnp.sum(grad_branch.astype(jnp.float32), axis=0)
    grad_mixed = jnp.dot(grad_branch, full_out, preferred_element_type=jnp.float32)
    grad_mixed_low = grad_mixed.astype(low)
    grad_features = attend_back(
        queries.reshape(total_rows, width).T,
        keys.reshape(total_rows, width).T,
        values.reshape(total_rows, width).T,
        jnp.stack([begin, finish]),
        scale,
        grad_mixed_low.T,
        log_total.reshape(HEADS, 1, total_rows),
    )
    attn_finish, attn_sent = scatter_attn(
        (grad_features, grad_branch.T), ((first_low, first_beside), (mixed_low, mixed_beside))
    )
    mlp_share = scatter_hidden(own_grads, sum(other_grads, []), attn_sent)
    attn_share = attn_finish()
    grad_features = after(grad_features, attn_sent).reshape(3 * width, total_rows)
    down_far = after(swap(down_far, 2), attn_sent).astype(jnp.float32)
    output = jnp.where(live, middle + (down + down_far + down_bias), 0.0).astype(low)
    grad_columns = jnp.sum(grad_features.astype(jnp.float32), axis=1)
    grad_first = jnp.einsum(
        "fr,fd->rd", grad_features, full_proj, preferred_element_type=jnp.float32
    )
    grad_gain_one = jnp.sum(grad_first * normed_one, axis=0)
    grad_shift_one = jnp.sum(grad_first, axis=0)
    grad_inputs = grad_middle + normalize_back(grad_first, normed_one, factor_one, gain_one)
    grad_vec = jnp.concatenate(
        [
            grad_gain_one,
            grad_shift_one,
            grad_columns[:width],
            grad_columns[2 * width :],
            grad_out_bias,
            grad_gain_two,
            grad_shift_two,
            grad_down_bias,
            grad_up_bias.reshape(-1),
        ],
        axis=0,
    )
    vec_share = scatter_vectors(grad_vec)
    return (output, grad_inputs, attn_share, mlp_share, vec_share)


def solution(mesh):
    return jax.shard_map(
        shards,
        mesh=mesh,
        in_specs=(
            P("dev", None),
            P("dev", None),
            P("dev", None),
            P("dev"),
            P("dev", None),
            P(),
            P(),
            P(),
        ),
        out_specs=(P("dev", None), P("dev", None), P("dev", None), P("dev", None), P("dev")),
        check_vma=False,
    )
```

```python
import jax
import jax.numpy as jnp
from jax import lax
from jax.experimental import pallas as pl
from jax.experimental.layout import Layout, with_layout_constraint
from jax.experimental.pallas import tpu as pltpu
from jax.sharding import PartitionSpec as P

D = 1088
HEADS = 17
HEAD_SIZE = 64
FF = 4352
VMEM_LIMIT = 48 * 1024 * 1024


epsilon = 1e-05
neg_large = -1e30


def normalize(values, gain, shift):
    centre = values - jnp.mean(values, axis=-1, keepdims=True)
    spread = jnp.mean(centre * centre, axis=-1, keepdims=True)
    factor = lax.rsqrt(spread + epsilon)
    normed = centre * factor
    return (normed * gain + shift, normed, factor)


def normalize_back(grad_out, normed, factor, gain):
    inner = grad_out * gain
    return factor * (
        inner
        - jnp.mean(inner, axis=-1, keepdims=True)
        - normed * jnp.mean(inner * normed, axis=-1, keepdims=True)
    )


def split_vectors(whole_vec):
    width = D
    pieces = [
        whole_vec[number * width : (number + 1) * width].astype(jnp.float32) for number in range(8)
    ]
    return pieces + [whole_vec[8 * width :].astype(jnp.float32)]


def gelu_parts(values):
    share = 0.5 + 0.5 * lax.erf(values * (0.5**0.5))
    density = jnp.exp(-0.5 * values * values) * ((2.0 * jnp.pi) ** (-0.5))
    return (values * share, share + values * density)


def allowed_pairs(keep):
    position = jnp.arange(keep.shape[0], dtype=jnp.int32)
    return (position[None, :] <= position[:, None]) & (keep[None, :] == keep[:, None])


def attend(queries, keys, values, allowed, scale):
    scores = jnp.einsum("qhd,khd->hqk", queries, keys, preferred_element_type=jnp.float32) * scale
    scores = jnp.where(allowed[None], scores, neg_large)
    top = jnp.max(scores, axis=-1, keepdims=True)
    expo = jnp.exp(scores - top)
    total = jnp.sum(expo, axis=-1, keepdims=True)
    weights = (expo / total).astype(jnp.bfloat16)
    mixed = jnp.einsum("hqk,khd->qhd", weights, values, preferred_element_type=jnp.float32)
    return (mixed, top + jnp.log(total))


def local_kernel(body, outs, operands, flops, scalars=(), earlier=()):
    outs = [jax.ShapeDtypeStruct(shape, kind) for shape, kind in outs]
    moved = sum(array.size * array.dtype.itemsize for array in (*outs, *operands))
    first, count, total = len(scalars), len(operands), len(operands) + len(outs)

    def whole(*refs):
        scalar_refs, sources = refs[:first], refs[first : first + count]
        goals = refs[first + count + len(earlier) :][: len(outs)]
        buffers, sems = refs[-total - 1 : -1], refs[-1]
        ends = tuple(zip(sources, buffers)) + tuple(zip(buffers[count:], goals))
        copies = [
            pltpu.make_async_copy(source, goal, sems.at[number])
            for number, (source, goal) in enumerate(ends)
        ]
        for copy in copies[:count]:
            copy.start()
        for copy in copies[:count]:
            copy.wait()
        body(*scalar_refs, *buffers)
        for copy in copies[count:]:
            copy.start()
        for copy in copies[count:]:
            copy.wait()

    anywhere = pl.BlockSpec(memory_space=pl.ANY)
    return pl.pallas_call(
        whole,
        out_shape=outs,
        in_specs=[pl.BlockSpec(memory_space=pltpu.SMEM)] * first
        + [anywhere] * (count + len(earlier)),
        out_specs=[anywhere] * len(outs),
        scratch_shapes=[pltpu.VMEM(array.shape, array.dtype) for array in (*operands, *outs)]
        + [pltpu.SemaphoreType.DMA((total,))],
        compiler_params=pltpu.CompilerParams(vmem_limit_bytes=VMEM_LIMIT),
        cost_estimate=pl.CostEstimate(flops=flops, bytes_accessed=moved, transcendentals=0),
    )(*scalars, *operands, *earlier)


def row_major(values):
    return with_layout_constraint(values, Layout(major_to_minor=tuple(range(values.ndim))))


def product(left, right, left_axis, right_axis):
    return lax.dot_general(
        left, right, (((left_axis,), (right_axis,)), ((), ())), preferred_element_type=jnp.float32
    )


def attend_back(queries, keys, values, span, scale, grad_mixed, log_total):
    width, rows = queries.shape
    low = jnp.bfloat16

    def body(span_ref, q_ref, k_ref, v_ref, do_ref, log_ref, out_ref):
        begin, finish = span_ref[0], span_ref[1]

        def inside(axis):
            position = lax.broadcasted_iota(jnp.int32, (rows, rows), axis)
            return (position, (position >= begin) & (position < finish))

        key_pos, key_live = inside(0)
        query_pos, query_live = inside(1)
        allowed = (key_pos <= query_pos) & (key_live == query_live)

        @pl.loop(0, HEADS)
        def _(head):
            part = pl.ds(pl.multiple_of(head * HEAD_SIZE, HEAD_SIZE), HEAD_SIZE)
            q, k, v, do = q_ref[part, :], k_ref[part, :], v_ref[part, :], do_ref[part, :]
            scores = jnp.where(allowed, product(k, q, 0, 0) * scale, neg_large)
            probs = jnp.exp(scores - log_ref[head])
            out_ref[2, part, :] = product(do, probs.astype(low), 1, 1).astype(low)
            grad_probs = product(v, do, 0, 0)
            inner = jnp.sum(probs * grad_probs, axis=0, keepdims=True)
            grad_scores = (probs * (grad_probs - inner)).astype(low)
            out_ref[0, part, :] = (product(k, grad_scores, 1, 0) * scale).astype(low)
            out_ref[1, part, :] = (product(q, grad_scores, 1, 1) * scale).astype(low)

    return local_kernel(
        body,
        [((3, width, rows), low)],
        (queries, keys, values, grad_mixed, log_total),
        10 * rows * rows * width,
        (span,),
    )[0]


def mlp_block(row_pair, grad_pair, weights, biases, before, last):
    rows, width = row_pair[0].shape
    low, wide = jnp.bfloat16, jnp.float32
    hidden = [2 * weight.shape[1] for weight in weights]
    outs = []
    for count in hidden:
        outs += [((2, rows, count), low), ((2, rows, count), low), ((1, count), wide)]
    sums = len(outs)
    if last:
        outs += [((rows, width), wide), ((rows, width), low)]
    else:
        outs += [((2, rows, width), wide)]
    number = len(weights)

    def body(*refs):
        row_refs, grad_refs = refs[:2], refs[2:4]
        weight_refs, bias_refs = refs[4 : 4 + number], refs[4 + number : 4 + 2 * number]
        out_refs = refs[-len(outs) :]
        for side in range(2):
            total = None if before is None else refs[4 + 2 * number][side]
            for place in range(number):
                weight, count = weight_refs[place], hidden[place]
                up = weight[0:2].reshape(count, width)
                down = weight[2:4].reshape(count, width)
                up_sum = product(row_refs[side][...], up, 1, 1) + bias_refs[place][...]
                activated, slope = gelu_parts(up_sum)
                grad_act = product(grad_refs[side][...], down, 1, 1)
                grad_up = (grad_act * slope).astype(low)
                act_ref, up_ref, sum_ref = out_refs[3 * place : 3 * place + 3]
                act_ref[side] = activated.astype(low)
                up_ref[side] = grad_up
                columns = jnp.sum(grad_up.astype(wide), axis=0, keepdims=True)
                sum_ref[...] = columns if side == 0 else sum_ref[...] + columns
                term = product(grad_up, up, 1, 0)
                total = term if total is None else total + term
            if last:
                out = out_refs[sums + side]
                out[...] = total.astype(out.dtype)
            else:
                out_refs[sums][side] = total

    operands = (*row_pair, *grad_pair, *weights, *biases)
    operands += () if before is None else (before,)
    result = local_kernel(body, outs, operands, 12 * rows * width * sum(hidden))
    return ([result[3 * place : 3 * place + 3] for place in range(number)], result[sums:])


def mlp_weight_grads(blocks, rows, grads, kind, earlier):
    width = rows[0].shape[1]
    operands, outs, number = [], [], len(rows)
    for near, far in blocks:
        operands += [near[0], far[0], near[1], far[1]]
        count = near[0].shape[2]
        outs += [((2, count // 2, width), kind)] * 2

    def body(*refs):
        row_refs = refs[len(operands) : len(operands) + number]
        grad_refs = refs[len(operands) + number : len(operands) + 2 * number]
        out_refs = refs[-len(outs) :]
        for place in range(len(blocks)):
            sources = refs[4 * place : 4 * place + 4]
            for out, pair, others in (
                (out_refs[2 * place], sources[2:], row_refs),
                (out_refs[2 * place + 1], sources[:2], grad_refs),
            ):
                total = None
                for which in range(number):
                    term = product(pair[which // 2][which % 2], others[which][...], 0, 0)
                    total = term if total is None else total + term
                out[...] = total.reshape(out.shape).astype(kind)

    flops = sum(16 * rows[0].shape[0] * near[0].shape[2] * width for near, far in blocks)
    result = local_kernel(body, outs, (*operands, *rows, *grads), flops, (), earlier)
    return [tuple(result[2 * place : 2 * place + 2]) for place in range(len(blocks))]


def mlp_outputs(blocks, weights, earlier):
    rows, width = blocks[0][0][0].shape[1], weights[0].shape[2]
    number = len(weights)
    operands = [near[0] for near, far in blocks] + [far[0] for near, far in blocks]

    def body(*refs):
        weight_refs, out_refs = refs[2 * number : 3 * number], refs[-2:]
        for group in range(2):
            for side in range(2):
                total = None
                for place in range(number):
                    weight = weight_refs[place]
                    down = weight[2:4].reshape(2 * weight.shape[1], width)
                    term = product(refs[group * number + place][side], down, 1, 0)
                    total = term if total is None else total + term
                out_refs[side][group] = total.astype(out_refs[side].dtype)

    outs = [((2, rows, width), jnp.float32), ((2, rows, width), jnp.bfloat16)]
    flops = 16 * rows * width * sum(weight.shape[1] for weight in weights)
    return local_kernel(body, outs, (*operands, *weights), flops, (), earlier)


def gather_rows(own):
    across = swap(own, 2)
    beside = swap(own, 1)
    return ((own, beside), (across, swap(across, 1)))


def after(values, others):
    return lax.optimization_barrier((values, others))[0]


def swap(piece, mask):
    devices = lax.axis_size("dev")
    return lax.ppermute(piece, "dev", [(number, number ^ mask) for number in range(devices)])


def same_low(devices):
    return [list(range(low, devices, 4)) for low in range(4)]


def gather_vectors(own):
    here = lax.axis_index("dev")
    whole = own
    mask = 1
    while mask < lax.axis_size("dev"):
        other = swap(whole, mask)
        upper = (here & mask) != 0
        whole = jnp.concatenate(
            [jnp.where(upper, other, whole), jnp.where(upper, whole, other)], axis=0
        )
        mask *= 2
    return whole


def scatter_vectors(whole):
    here = lax.axis_index("dev")
    mask = lax.axis_size("dev") // 2
    while mask:
        half = whole.shape[0] // 2
        upper = (here & mask) != 0
        mine = jnp.where(upper, whole[half:], whole[:half])
        yours = jnp.where(upper, whole[:half], whole[half:])
        whole = mine + swap(yours, mask)
        mask //= 2
    return whole


def z_groups(devices):
    return [list(range(low, devices, 8)) for low in range(8)]


def gather_z(shard):
    devices = lax.axis_size("dev")
    return lax.all_gather(shard, "dev", axis=0, tiled=False, axis_index_groups=z_groups(devices))


def place_blocks(pieces):
    block = (lax.axis_index("dev") & 7).astype(jnp.int32).reshape(1)
    arrays = [piece[0] for piece in pieces]
    rows, width = arrays[0].shape[1:]
    count = sum(array.shape[0] for array in arrays)

    def body(block_ref, *refs):
        piece_refs = refs[: len(arrays)]
        three_ref, last_ref, sems = refs[len(arrays) :]
        copies = []
        for ref, (array, mask, begin) in zip(piece_refs, pieces):
            target = block_ref[0] ^ mask
            for number in range(array.shape[0]):
                matrix = begin + number
                goal = last_ref.at[target] if matrix == 3 else three_ref.at[matrix, target]
                copies.append(
                    pltpu.make_async_copy(ref.at[number], goal, sems.at[len(copies)])
                )
                copies[-1].start()
        for copy in copies:
            copy.wait()

    kind = arrays[0].dtype
    return pl.pallas_call(
        body,
        out_shape=(
            jax.ShapeDtypeStruct((3, 8, rows, width), kind),
            jax.ShapeDtypeStruct((8, rows, width), kind),
        ),
        in_specs=[pl.BlockSpec(memory_space=pltpu.SMEM)]
        + [pl.BlockSpec(memory_space=pl.ANY)] * len(arrays),
        out_specs=(pl.BlockSpec(memory_space=pltpu.VMEM), pl.BlockSpec(memory_space=pltpu.VMEM)),
        scratch_shapes=[pltpu.SemaphoreType.DMA((count,))],
        compiler_params=pltpu.CompilerParams(vmem_limit_bytes=VMEM_LIMIT),
        cost_estimate=pl.CostEstimate(
            flops=0, bytes_accessed=4 * count * rows * width, transcendentals=0
        ),
    )(block, *arrays)


def gather_attn(shard):
    devices = lax.axis_size("dev")
    if devices != 32:
        whole = lax.all_gather(shard, "dev", axis=0, tiled=True)
        width = shard.shape[1]
        return (whole[: 3 * width], whole[3 * width :], shard)
    own = gather_z(shard)
    along, across = swap(own, 4), swap(own, 2)
    beside = swap(own, 1)
    upper, lower = swap(along[:2], 2), swap(across[2:], 4)
    pieces = [(own, 0, 0), (beside, 1, 0), (along, 4, 0), (across, 2, 0)]
    pieces += [(swap(along, 1), 5, 0), (swap(across, 1), 3, 0)]
    pieces += [(upper, 6, 0), (lower, 6, 2), (swap(upper, 1), 7, 0), (swap(lower, 1), 7, 2)]
    three, last = place_blocks(pieces)
    width = shard.shape[1]
    return (three.reshape(3 * width, width), last.reshape(width, width), (upper, lower))


def scatter_attn(grads, sources):
    devices = lax.axis_size("dev")
    low = jnp.bfloat16
    first, mixed = sources
    own, width = first[0].shape
    if devices != 32:
        product = jnp.concatenate(
            [
                jnp.dot(grads[0].reshape(3 * width, own), first[0], preferred_element_type=jnp.float32),
                jnp.dot(grads[1], mixed[0], preferred_element_type=jnp.float32),
            ],
            axis=0,
        ).astype(low)
        share = lax.psum_scatter(product, "dev", scatter_dimension=0, tiled=True)
        return (lambda: share.astype(jnp.float32), grads)
    pairs = ((first[0], mixed[0]), (first[1], mixed[1]))
    grads = [part.reshape(-1, 8, width // 8, own) for part in grads]
    diagonal, across, along, mine = attn_products(grads, [swap(part, 1) for part in grads], pairs)

    across_upper = swap(across[0], 2)
    along_lower = swap(along[1], 4)
    along_diagonal = swap(diagonal[1], 4).astype(jnp.float32)
    across_diagonal = swap(diagonal[0], 2).astype(jnp.float32)
    across_lower = swap((across[1] + along_diagonal).astype(low), 2)
    along_upper = swap((along[0] + across_diagonal).astype(low), 4)

    def finish():
        return scatter_z(mine, ((across_upper, along_upper), (across_lower, along_lower)))

    return (finish, (across[1], along[0]))


def attn_products(mine, beside, pairs):
    block = (lax.axis_index("dev") & 7).astype(jnp.int32).reshape(1)
    rows = mine[0].shape[2]
    width = pairs[0][0].shape[1]
    low, wide = jnp.bfloat16, jnp.float32
    kinds = (low, low, low, wide, wide, low, wide, wide)

    def body(block_ref, *refs):
        (three, last), (three_beside, last_beside) = refs[:2], refs[2:4]
        pair_refs, other_refs = refs[4:6], refs[6:8]
        outs = refs[8:]
        for place, mask in enumerate((6, 2, 4, 0)):
            target = block_ref[0] ^ mask
            for half in range(2):
                out = outs[2 * place + half]
                for number in range(2):
                    matrix = 2 * half + number
                    left = last[0, target] if matrix == 3 else three[matrix, target]
                    left_beside = (
                        last_beside[0, target] if matrix == 3 else three_beside[matrix, target]
                    )
                    side = 1 if matrix == 3 else 0
                    value = product(left, pair_refs[side][...], 1, 0)
                    value = value + product(left_beside, other_refs[side][...], 1, 0)
                    out[number] = value.astype(out.dtype)

    outs = local_kernel(
        body,
        [((2, rows, width), kind) for kind in kinds],
        (*mine, *beside, *pairs[0], *pairs[1]),
        64 * rows * mine[0].shape[3] * width,
        (block,),
    )
    return [outs[2 * place : 2 * place + 2] for place in range(4)]


def gather_hidden(shard):
    devices = lax.axis_size("dev")
    if devices != 32:
        both = lax.all_gather(
            shard, "dev", axis=0, tiled=True, axis_index_groups=same_low(devices)
        )
        return (both, None)
    cut = 128
    one, two = gather_z(shard[:cut]), gather_z(shard[cut:])
    return ((one, swap(one, 4)), two)


def pick_blocks(bias, blocks, start, stop):
    picked = lax.dynamic_index_in_dim(bias, blocks, 1, False)
    return picked[:, start:stop].reshape(-1)


def put_blocks(bias, blocks, start, stop, values):
    values = values.reshape(bias.shape[0], 1, stop - start)
    return lax.dynamic_update_slice(bias, values, (0, blocks, start))


def hidden_parts(gathered, here, devices, ready):
    one, two = gathered
    if devices != 32:
        rows = one.shape[0] // 4
        return [[(one.reshape(4, rows, -1), here & 3, 0, rows // (devices // 16))]]
    two = after(two, ready)
    cut, end = one[0].shape[1], one[0].shape[1] + two.shape[1]
    own, other = here & 7, (here & 7) ^ 4
    return [
        [(one[0], own, 0, cut), (two, own, cut, end)],
        [(one[1], other, 0, cut), (swap(two, 4), other, cut, end)],
    ]


def scatter_hidden(own, others, ready):
    devices = lax.axis_size("dev")
    low = jnp.bfloat16
    if devices != 32:
        width = own[0][0].shape[2]
        both = jnp.concatenate([part.reshape(-1, width) for part in own[0]], axis=0).astype(low)
        return lax.psum_scatter(
            both, "dev", scatter_dimension=0, tiled=True, axis_index_groups=same_low(devices)
        ).astype(jnp.float32)
    moved = [[swap(part, 4) for part in pair] for pair in others]
    shares = [
        scatter_z(mine, [(part,) for part in other], ready)
        for mine, other in zip(own, moved)
    ]
    return jnp.concatenate(shares, axis=0)


def scatter_z(own, others, earlier=()):
    mine, one, two, three = route_z(own, others, earlier)
    wide = jnp.float32
    return (
        mine
        + swap(two, 16).astype(wide)
        + swap(three, 24).astype(wide)
        + swap(one, 8).astype(wide)
    )


def route_z(own, others, earlier):
    layer = (lax.axis_index("dev") >> 3).astype(jnp.int32).reshape(1)
    rows, width = own[0].shape[1:]
    count = len(others[0])

    def body(layer_ref, *refs):
        outs = refs[-4:]
        for mask, out in enumerate(outs):
            goal = layer_ref[0] ^ mask
            number = goal & 1
            for half in range(2):
                sources = refs[half * (count + 1) : (half + 1) * (count + 1)]

                @pl.when((goal >> 1) == half)
                def _():
                    total = sources[0][number]
                    for source in sources[1:]:
                        total = total + source[number].astype(jnp.float32)
                    out[...] = total.astype(out.dtype)

    kinds = (jnp.float32, jnp.bfloat16, jnp.bfloat16, jnp.bfloat16)
    return local_kernel(
        body,
        [((rows, width), kind) for kind in kinds],
        (own[0], *others[0], own[1], *others[1]),
        4 * rows * width,
        (layer,),
        earlier,
    )


def shards(
    tokens, attn_weight, mlp_weight, vectors, cotangent, seq_lengths, seq_device, seq_offset
):
    total_rows = tokens.shape[0]
    width = D
    scale = HEAD_SIZE ** (-0.5)
    low = jnp.bfloat16
    devices = lax.axis_size("dev")
    here = lax.axis_index("dev")
    chosen = (seq_device == here).astype(jnp.int32)
    begin = jnp.sum(chosen * seq_offset)
    finish = begin + jnp.sum(chosen * seq_lengths)
    positions = jnp.arange(total_rows, dtype=jnp.int32)
    keep = ((positions >= begin) & (positions < finish)).astype(jnp.int32)
    live = keep[:, None] == 1
    allowed = allowed_pairs(keep)
    head_shape = (total_rows, HEADS, HEAD_SIZE)

    full_vec = gather_vectors(vectors)
    grad_down = row_major(jnp.where(live, cotangent, jnp.zeros_like(cotangent)))
    full_proj, full_out, attn_ready = gather_attn(attn_weight)
    gathered = gather_hidden(mlp_weight)
    grad_down_rows = gather_rows(grad_down)

    (
        gain_one,
        shift_one,
        query_bias,
        value_bias,
        out_bias,
        gain_two,
        shift_two,
        down_bias,
        up_bias,
    ) = split_vectors(full_vec)
    low_count = 8 if devices == 32 else 4
    up_bias = up_bias.reshape(devices // 2 // low_count, low_count, -1)

    inputs = tokens.astype(jnp.float32)
    first_out, normed_one, factor_one = normalize(inputs, gain_one, shift_one)
    first_low = row_major(first_out.astype(low))
    first_beside = swap(first_low, 1)
    projected = jnp.einsum(
        "rd,od->ro", first_low, full_proj, preferred_element_type=jnp.float32
    )
    queries = (projected[:, :width] + query_bias).astype(low).reshape(head_shape)
    keys = projected[:, width : 2 * width].astype(low).reshape(head_shape)
    values = (projected[:, 2 * width :] + value_bias).astype(low).reshape(head_shape)
    mixed, log_total = attend(queries, keys, values, allowed, scale)
    mixed_low = row_major(mixed.reshape(total_rows, width).astype(low))
    mixed_beside = swap(mixed_low, 1)
    branch = (
        jnp.einsum(
            "rd,od->ro", mixed_low, full_out, preferred_element_type=jnp.float32
        )
        + out_bias
    )
    middle = inputs + branch
    second_out, normed_two, factor_two = normalize(middle, gain_two, shift_two)
    second_own = row_major(second_out.astype(low))
    near, far = gather_rows(second_own)
    parts = hidden_parts(gathered, here, devices, second_own)
    near_grads, far_grads = grad_down_rows

    sides = []
    near_sum = far_sum = None
    grad_up_bias = jnp.zeros_like(up_bias)
    for place, side in enumerate(parts):
        weights = [part[0] for part in side]
        biases = [pick_blocks(up_bias, *part[1:]).reshape(1, -1) for part in side]
        last = place == len(parts) - 1
        near_blocks, near_sum = mlp_block(near, near_grads, weights, biases, near_sum, last)
        far_blocks, far_sum = mlp_block(far, far_grads, weights, biases, far_sum, last)
        if not last:
            near_sum, far_sum = near_sum[0], far_sum[0]
        for part, one, two in zip(side, near_blocks, far_blocks):
            grad_up_bias = put_blocks(grad_up_bias, *part[1:], (one[2] + two[2]).reshape(-1))
        sides.append([(one[:2], two[:2]) for one, two in zip(near_blocks, far_blocks)])
    far_total = (far_sum[0] + swap(far_sum[1], 1).astype(jnp.float32)).astype(low)
    near_taken = swap(near_sum[1], 1)
    grad_second = near_sum[0] + near_taken.astype(jnp.float32)
    all_rows, all_grads = near + far, near_grads + far_grads
    other_grads = [
        mlp_weight_grads(side, all_rows, all_grads, low, (far_total,)) for side in sides[1:]
    ]
    far_taken = after(swap(far_total, 2), other_grads)
    grad_second = grad_second + far_taken.astype(jnp.float32)

    grad_down_wide = grad_down.astype(jnp.float32)
    grad_down_bias = jnp.sum(grad_down_wide, axis=0)
    grad_gain_two = jnp.sum(grad_second * normed_two, axis=0)
    grad_shift_two = jnp.sum(grad_second, axis=0)
    grad_middle = grad_down_wide + normalize_back(grad_second, normed_two, factor_two, gain_two)
    grad_branch = grad_middle.astype(low)
    grad_out_bias = jnp.sum(grad_branch.astype(jnp.float32), axis=0)
    grad_mixed = jnp.dot(grad_branch, full_out, preferred_element_type=jnp.float32)
    grad_mixed_low = grad_mixed.astype(low)
    grad_features = attend_back(
        queries.reshape(total_rows, width).T,
        keys.reshape(total_rows, width).T,
        values.reshape(total_rows, width).T,
        jnp.stack([begin, finish]),
        scale,
        grad_mixed_low.T,
        log_total.reshape(HEADS, 1, total_rows),
    )
    attn_finish, attn_sent = scatter_attn(
        (grad_features, grad_branch.T), ((first_low, first_beside), (mixed_low, mixed_beside))
    )
    own_grads = mlp_weight_grads(sides[0], all_rows, all_grads, jnp.float32, attn_sent)
    down_keep, down_give = mlp_outputs(
        sum(sides, []),
        [part[0] for side in parts for part in side],
        sum(own_grads, ()),
    )
    down_taken = swap(down_give, 1).astype(jnp.float32)
    down = down_keep[0] + down_taken[0]
    down_far = swap((down_keep[1] + down_taken[1]).astype(low), 2).astype(jnp.float32)
    mlp_share = scatter_hidden(own_grads, sum(other_grads, []), attn_sent)
    attn_share = attn_finish()
    grad_features = after(grad_features, attn_sent).reshape(3 * width, total_rows)
    output = jnp.where(live, middle + (down + down_far + down_bias), 0.0).astype(low)
    grad_columns = jnp.sum(grad_features.astype(jnp.float32), axis=1)
    grad_first = jnp.einsum(
        "fr,fd->rd", grad_features, full_proj, preferred_element_type=jnp.float32
    )
    grad_gain_one = jnp.sum(grad_first * normed_one, axis=0)
    grad_shift_one = jnp.sum(grad_first, axis=0)
    grad_inputs = grad_middle + normalize_back(grad_first, normed_one, factor_one, gain_one)
    grad_vec = jnp.concatenate(
        [
            grad_gain_one,
            grad_shift_one,
            grad_columns[:width],
            grad_columns[2 * width :],
            grad_out_bias,
            grad_gain_two,
            grad_shift_two,
            grad_down_bias,
            grad_up_bias.reshape(-1),
        ],
        axis=0,
    )
    vec_share = scatter_vectors(grad_vec)
    return (output, grad_inputs, attn_share, mlp_share, vec_share)


def solution(mesh):
    return jax.shard_map(
        shards,
        mesh=mesh,
        in_specs=(
            P("dev", None),
            P("dev", None),
            P("dev", None),
            P("dev"),
            P("dev", None),
            P(),
            P(),
            P(),
        ),
        out_specs=(P("dev", None), P("dev", None), P("dev", None), P("dev", None), P("dev")),
        check_vma=False,
    )
```

```python
import jax
import jax.numpy as jnp
from jax import lax
from jax.experimental import pallas as pl
from jax.experimental.pallas import tpu as pltpu
from jax.sharding import PartitionSpec as P

D = 1088
HEADS = 17
HEAD_SIZE = 64
FF = 4352
VMEM_LIMIT = 60 * 1024 * 1024


epsilon = 1e-05
neg_large = -1e30


def normalize(values, gain, shift):
    centre = values - jnp.mean(values, axis=-1, keepdims=True)
    spread = jnp.mean(centre * centre, axis=-1, keepdims=True)
    factor = lax.rsqrt(spread + epsilon)
    normed = centre * factor
    return (normed * gain + shift, normed, factor)


def normalize_back(grad_out, normed, factor, gain):
    inner = grad_out * gain
    return factor * (
        inner
        - jnp.mean(inner, axis=-1, keepdims=True)
        - normed * jnp.mean(inner * normed, axis=-1, keepdims=True)
    )


def split_vectors(whole_vec):
    width = D
    pieces = [
        whole_vec[number * width : (number + 1) * width].astype(jnp.float32) for number in range(8)
    ]
    return pieces + [whole_vec[8 * width :].astype(jnp.float32)]


def gelu_parts(values):
    share = 0.5 + 0.5 * lax.erf(values * (0.5**0.5))
    density = jnp.exp(-0.5 * values * values) * ((2.0 * jnp.pi) ** (-0.5))
    return (values * share, share + values * density)


def allowed_pairs(keep):
    position = jnp.arange(keep.shape[0], dtype=jnp.int32)
    return (position[None, :] <= position[:, None]) & (keep[None, :] == keep[:, None])


def attend(queries, keys, values, allowed, scale):
    scores = jnp.einsum("qhd,khd->hqk", queries, keys, preferred_element_type=jnp.float32) * scale
    scores = jnp.where(allowed[None], scores, neg_large)
    top = jnp.max(scores, axis=-1, keepdims=True)
    expo = jnp.exp(scores - top)
    total = jnp.sum(expo, axis=-1, keepdims=True)
    weights = (expo / total).astype(jnp.bfloat16)
    mixed = jnp.einsum("hqk,khd->qhd", weights, values, preferred_element_type=jnp.float32)
    return (mixed, top + jnp.log(total))


def local_kernel(body, outs, operands, flops, scalars=(), earlier=()):
    outs = [jax.ShapeDtypeStruct(shape, kind) for shape, kind in outs]
    moved = sum(array.size * array.dtype.itemsize for array in (*outs, *operands))
    first, count, total = len(scalars), len(operands), len(operands) + len(outs)

    def whole(*refs):
        scalar_refs, sources = refs[:first], refs[first : first + count]
        goals = refs[first + count + len(earlier) :][: len(outs)]
        buffers, sems = refs[-total - 1 : -1], refs[-1]
        ends = tuple(zip(sources, buffers)) + tuple(zip(buffers[count:], goals))
        copies = [
            pltpu.make_async_copy(source, goal, sems.at[number])
            for number, (source, goal) in enumerate(ends)
        ]
        for copy in copies[:count]:
            copy.start()
        waiting = list(range(count))
        unsent = list(range(len(outs)))

        def need(*numbers):
            for number in numbers or tuple(waiting):
                if number in waiting:
                    waiting.remove(number)
                    copies[number].wait()

        def send(*numbers):
            for number in numbers:
                unsent.remove(number)
                copies[count + number].start()

        body(need, send, *scalar_refs, *buffers)
        if waiting:
            need()
        send(*tuple(unsent))
        for copy in copies[count:]:
            copy.wait()

    anywhere = pl.BlockSpec(memory_space=pl.ANY)
    return pl.pallas_call(
        whole,
        out_shape=outs,
        in_specs=[pl.BlockSpec(memory_space=pltpu.SMEM)] * first
        + [anywhere] * (count + len(earlier)),
        out_specs=[anywhere] * len(outs),
        scratch_shapes=[pltpu.VMEM(array.shape, array.dtype) for array in (*operands, *outs)]
        + [pltpu.SemaphoreType.DMA((total,))],
        compiler_params=pltpu.CompilerParams(vmem_limit_bytes=VMEM_LIMIT),
        cost_estimate=pl.CostEstimate(flops=flops, bytes_accessed=moved, transcendentals=0),
    )(*scalars, *operands, *earlier)


def product(left, right, left_axis, right_axis):
    return lax.dot_general(
        left, right, (((left_axis,), (right_axis,)), ((), ())), preferred_element_type=jnp.float32
    )


def attend_back(queries, keys, values, span, scale, grad_mixed, log_total):
    width, rows = queries.shape
    low = jnp.bfloat16

    def body(need, send, span_ref, q_ref, k_ref, v_ref, do_ref, log_ref, out_ref):
        need()
        begin, finish = span_ref[0], span_ref[1]

        def inside(axis):
            position = lax.broadcasted_iota(jnp.int32, (rows, rows), axis)
            return (position, (position >= begin) & (position < finish))

        key_pos, key_live = inside(0)
        query_pos, query_live = inside(1)
        allowed = (key_pos <= query_pos) & (key_live == query_live)

        @pl.loop(0, HEADS)
        def _(head):
            part = pl.ds(pl.multiple_of(head * HEAD_SIZE, HEAD_SIZE), HEAD_SIZE)
            q, k, v, do = q_ref[part, :], k_ref[part, :], v_ref[part, :], do_ref[part, :]
            scores = jnp.where(allowed, product(k, q, 0, 0) * scale, neg_large)
            probs = jnp.exp(scores - log_ref[head])
            out_ref[2, part, :] = product(do, probs.astype(low), 1, 1).astype(low)
            grad_probs = product(v, do, 0, 0)
            inner = jnp.sum(probs * grad_probs, axis=0, keepdims=True)
            grad_scores = (probs * (grad_probs - inner)).astype(low)
            out_ref[0, part, :] = (product(k, grad_scores, 1, 0) * scale).astype(low)
            out_ref[1, part, :] = (product(q, grad_scores, 1, 1) * scale).astype(low)

    return local_kernel(
        body,
        [((3, width, rows), low)],
        (queries, keys, values, grad_mixed, log_total),
        10 * rows * rows * width,
        (span,),
    )[0]


def mlp_block(row_pair, grad_pair, weights, biases):
    width, rows = row_pair[0].shape
    low, wide = jnp.bfloat16, jnp.float32
    hidden = [2 * weight.shape[1] for weight in weights]
    outs = []
    for count in hidden:
        outs += [((2, count, rows), low), ((2, count, rows), low), ((count, 1), wide)]
    sums = len(outs)
    outs += [((width, rows), wide), ((width, rows), low)]
    number = len(weights)

    def body(need, send, *refs):
        row_refs, grad_refs = refs[:2], refs[2:4]
        weight_refs, bias_refs = refs[4 : 4 + number], refs[4 + number : 4 + 2 * number]
        out_refs = refs[-len(outs) :]
        for side in (1, 0):
            total = None
            for place in range(number):
                need(side, 2 + side, 4 + place, 4 + number + place)
                weight, count = weight_refs[place], hidden[place]
                up = weight[0:2].reshape(count, width)
                down = weight[2:4].reshape(count, width)
                up_sum = product(up, row_refs[side][...], 1, 0) + bias_refs[place][...]
                activated, slope = gelu_parts(up_sum)
                grad_act = product(down, grad_refs[side][...], 1, 0)
                grad_up = (grad_act * slope).astype(low)
                act_ref, up_ref, sum_ref = out_refs[3 * place : 3 * place + 3]
                act_ref[side] = activated.astype(low)
                up_ref[side] = grad_up
                columns = jnp.sum(grad_up.astype(wide), axis=1, keepdims=True)
                sum_ref[...] = columns if side == 1 else sum_ref[...] + columns
                if side == 0:
                    send(3 * place, 3 * place + 1, 3 * place + 2)
                term = product(up, grad_up, 0, 0)
                total = term if total is None else total + term
            out = out_refs[sums + side]
            out[...] = total.astype(out.dtype)
            send(sums + side)

    operands = (*row_pair, *grad_pair, *weights, *biases)
    result = local_kernel(body, outs, operands, 12 * rows * width * sum(hidden))
    return ([result[3 * place : 3 * place + 3] for place in range(number)], result[sums:])


def mlp_weight_grads(blocks, rows, grads, kind, earlier):
    width = rows[0].shape[0]
    operands, outs, number = [], [], len(rows)
    operands += [*rows, *grads]
    for near, far in blocks:
        operands += [near[0], far[0], near[1], far[1]]
        count = near[0].shape[1]
        outs += [((2, count // 2, width), kind)] * 2

    def body(need, send, *refs):
        row_refs, grad_refs = refs[:number], refs[number : 2 * number]
        out_refs = refs[-len(outs) :]
        need(*range(2 * number))
        for place in range(len(blocks)):
            start = 2 * number + 4 * place
            need(*range(start, start + 4))
            sources = refs[start : start + 4]
            for which, pair, others in ((0, sources[2:], row_refs), (1, sources[:2], grad_refs)):
                out = out_refs[2 * place + which]
                total = None
                for group in range(number):
                    term = product(pair[group // 2][group % 2], others[group][...], 1, 1)
                    total = term if total is None else total + term
                out[...] = total.reshape(out.shape).astype(kind)
                send(2 * place + which)

    flops = sum(16 * rows[0].shape[1] * near[0].shape[1] * width for near, far in blocks)
    result = local_kernel(body, outs, operands, flops, (), earlier)
    return [tuple(result[2 * place : 2 * place + 2]) for place in range(len(blocks))]


def mlp_outputs(blocks, weights, earlier):
    rows, width = blocks[0][0][0].shape[2], weights[0].shape[2]
    number = len(weights)
    operands = [near[0] for near, far in blocks] + [far[0] for near, far in blocks]

    def body(need, send, *refs):
        need()
        weight_refs, out_refs = refs[2 * number : 3 * number], refs[-2:]
        for group in range(2):
            for side in range(2):
                total = None
                for place in range(number):
                    weight = weight_refs[place]
                    down = weight[2:4].reshape(2 * weight.shape[1], width)
                    term = product(down, refs[group * number + place][side], 0, 0)
                    total = term if total is None else total + term
                out_refs[side][group] = total.astype(out_refs[side].dtype)

    outs = [((2, width, rows), jnp.float32), ((2, width, rows), jnp.bfloat16)]
    flops = 16 * rows * width * sum(weight.shape[1] for weight in weights)
    return local_kernel(body, outs, (*operands, *weights), flops, (), earlier)


def gather_rows(own):
    across = swap(own, 2)
    beside = swap(own, 1)
    return ((own, beside), (across, swap(across, 1)))


def after(values, others):
    return lax.optimization_barrier((values, others))[0]


def swap(piece, mask):
    devices = lax.axis_size("dev")
    return lax.ppermute(piece, "dev", [(number, number ^ mask) for number in range(devices)])


def same_low(devices):
    return [list(range(low, devices, 4)) for low in range(4)]


def gather_vectors(own):
    here = lax.axis_index("dev")
    whole = own
    mask = 1
    while mask < lax.axis_size("dev"):
        other = swap(whole, mask)
        upper = (here & mask) != 0
        whole = jnp.concatenate(
            [jnp.where(upper, other, whole), jnp.where(upper, whole, other)], axis=0
        )
        mask *= 2
    return whole


def scatter_vectors(whole):
    here = lax.axis_index("dev")
    mask = lax.axis_size("dev") // 2
    while mask:
        half = whole.shape[0] // 2
        upper = (here & mask) != 0
        mine = jnp.where(upper, whole[half:], whole[:half])
        yours = jnp.where(upper, whole[:half], whole[half:])
        whole = mine + swap(yours, mask)
        mask //= 2
    return whole


def z_groups(devices):
    return [list(range(low, devices, 8)) for low in range(8)]


def gather_z(shard):
    devices = lax.axis_size("dev")
    return lax.all_gather(shard, "dev", axis=0, tiled=False, axis_index_groups=z_groups(devices))


def place_blocks(pieces):
    block = (lax.axis_index("dev") & 7).astype(jnp.int32).reshape(1)
    arrays = [piece[0] for piece in pieces]
    rows, width = arrays[0].shape[1:]
    count = sum(array.shape[0] for array in arrays)

    def body(block_ref, *refs):
        piece_refs = refs[: len(arrays)]
        three_ref, last_ref, sems = refs[len(arrays) :]
        copies = []
        for ref, (array, mask, begin) in zip(piece_refs, pieces):
            target = block_ref[0] ^ mask
            for number in range(array.shape[0]):
                matrix = begin + number
                goal = last_ref.at[target] if matrix == 3 else three_ref.at[matrix, target]
                copies.append(
                    pltpu.make_async_copy(ref.at[number], goal, sems.at[len(copies)])
                )
                copies[-1].start()
        for copy in copies:
            copy.wait()

    kind = arrays[0].dtype
    return pl.pallas_call(
        body,
        out_shape=(
            jax.ShapeDtypeStruct((3, 8, rows, width), kind),
            jax.ShapeDtypeStruct((8, rows, width), kind),
        ),
        in_specs=[pl.BlockSpec(memory_space=pltpu.SMEM)]
        + [pl.BlockSpec(memory_space=pl.ANY)] * len(arrays),
        out_specs=(pl.BlockSpec(memory_space=pltpu.VMEM), pl.BlockSpec(memory_space=pltpu.VMEM)),
        scratch_shapes=[pltpu.SemaphoreType.DMA((count,))],
        compiler_params=pltpu.CompilerParams(vmem_limit_bytes=24 * 1024 * 1024),
        cost_estimate=pl.CostEstimate(
            flops=0, bytes_accessed=4 * count * rows * width, transcendentals=0
        ),
    )(block, *arrays)


def gather_attn(shard):
    devices = lax.axis_size("dev")
    if devices != 32:
        whole = lax.all_gather(shard, "dev", axis=0, tiled=True)
        width = shard.shape[1]
        return (whole[: 3 * width], whole[3 * width :], shard)
    own = gather_z(shard)
    along, across = swap(own, 4), swap(own, 2)
    beside = swap(own, 1)
    upper, lower = swap(along[:2], 2), swap(across[2:], 4)
    pieces = [(own, 0, 0), (beside, 1, 0), (along, 4, 0), (across, 2, 0)]
    pieces += [(swap(along, 1), 5, 0), (swap(across, 1), 3, 0)]
    pieces += [(upper, 6, 0), (lower, 6, 2), (swap(upper, 1), 7, 0), (swap(lower, 1), 7, 2)]
    three, last = place_blocks(pieces)
    width = shard.shape[1]
    return (three.reshape(3 * width, width), last.reshape(width, width), (upper, lower))


def scatter_attn(grads, sources):
    devices = lax.axis_size("dev")
    low = jnp.bfloat16
    first, mixed = sources
    width, own = first[0].shape
    if devices != 32:
        product = jnp.concatenate(
            [
                jnp.einsum('fr,dr->fd', grads[0].reshape(3 * width, own), first[0], preferred_element_type=jnp.float32),
                jnp.einsum('fr,dr->fd', grads[1], mixed[0], preferred_element_type=jnp.float32),
            ],
            axis=0,
        ).astype(low)
        share = lax.psum_scatter(product, "dev", scatter_dimension=0, tiled=True)
        return (lambda: share.astype(jnp.float32), grads)
    pairs = ((first[0], mixed[0]), (first[1], mixed[1]))
    grads = [part.reshape(-1, 8, width // 8, own) for part in grads]
    diagonal, across, along, mine = attn_products(grads, [swap(part, 1) for part in grads], pairs)

    across_upper = swap(across[0], 2)
    along_lower = swap(along[1], 4)
    along_diagonal = swap(diagonal[1], 4).astype(jnp.float32)
    across_diagonal = swap(diagonal[0], 2).astype(jnp.float32)
    across_lower = swap((across[1] + along_diagonal).astype(low), 2)
    along_upper = swap((along[0] + across_diagonal).astype(low), 4)

    def finish():
        return scatter_z(mine, ((across_upper, along_upper), (across_lower, along_lower)))

    return (finish, (across[1], along[0]))


def attn_products(mine, beside, pairs):
    block = (lax.axis_index("dev") & 7).astype(jnp.int32).reshape(1)
    rows = mine[0].shape[2]
    width = pairs[0][0].shape[0]
    low, wide = jnp.bfloat16, jnp.float32
    kinds = (low, low, low, wide, wide, low, wide, wide)

    def body(need, send, block_ref, *refs):
        need()
        (three, last), (three_beside, last_beside) = refs[:2], refs[2:4]
        pair_refs, other_refs = refs[4:6], refs[6:8]
        outs = refs[8:]
        for place, mask in enumerate((6, 2, 4, 0)):
            target = block_ref[0] ^ mask
            for half in range(2):
                out = outs[2 * place + half]
                for number in range(2):
                    matrix = 2 * half + number
                    left = last[0, target] if matrix == 3 else three[matrix, target]
                    left_beside = (
                        last_beside[0, target] if matrix == 3 else three_beside[matrix, target]
                    )
                    side = 1 if matrix == 3 else 0
                    value = product(left, pair_refs[side][...], 1, 1)
                    value = value + product(left_beside, other_refs[side][...], 1, 1)
                    out[number] = value.astype(out.dtype)
                send(2 * place + half)

    outs = local_kernel(
        body,
        [((2, rows, width), kind) for kind in kinds],
        (*mine, *beside, *pairs[0], *pairs[1]),
        64 * rows * mine[0].shape[3] * width,
        (block,),
    )
    return [outs[2 * place : 2 * place + 2] for place in range(4)]


def gather_hidden(shard):
    devices = lax.axis_size("dev")
    if devices != 32:
        both = lax.all_gather(
            shard, "dev", axis=0, tiled=True, axis_index_groups=same_low(devices)
        )
        return (both, None)
    cut = shard.shape[0] // 2
    one, two = gather_z(shard[:cut]), gather_z(shard[cut:])
    return ((one, swap(one, 4)), two)


def pick_blocks(bias, blocks, start, stop):
    picked = lax.dynamic_index_in_dim(bias, blocks, 1, False)
    return picked[:, start:stop].reshape(-1)


def put_blocks(bias, blocks, start, stop, values):
    values = values.reshape(bias.shape[0], 1, stop - start)
    return lax.dynamic_update_slice(bias, values, (0, blocks, start))


def hidden_parts(gathered, here, devices, ready):
    one, two = gathered
    if devices != 32:
        rows = one.shape[0] // 4
        return [[(one.reshape(4, rows, -1), here & 3, 0, rows // (devices // 16))]]
    two = after(two, ready)
    cut, end = one[0].shape[1], one[0].shape[1] + two.shape[1]
    own, other = here & 7, (here & 7) ^ 4
    return [
        [(one[0], own, 0, cut), (two, own, cut, end)],
        [(one[1], other, 0, cut), (swap(two, 4), other, cut, end)],
    ]


def scatter_hidden(own, others, ready):
    devices = lax.axis_size("dev")
    low = jnp.bfloat16
    if devices != 32:
        width = own[0][0].shape[2]
        both = jnp.concatenate([part.reshape(-1, width) for part in own[0]], axis=0).astype(low)
        return lax.psum_scatter(
            both, "dev", scatter_dimension=0, tiled=True, axis_index_groups=same_low(devices)
        ).astype(jnp.float32)
    moved = [[swap(part, 4) for part in pair] for pair in others]
    shares = [
        scatter_z(mine, [(part,) for part in other], ready)
        for mine, other in zip(own, moved)
    ]
    return jnp.concatenate(shares, axis=0)


def scatter_z(own, others, earlier=()):
    mine, one, two, three = route_z(own, others, earlier)
    wide = jnp.float32
    return (
        mine
        + swap(two, 16).astype(wide)
        + swap(three, 24).astype(wide)
        + swap(one, 8).astype(wide)
    )


def route_z(own, others, earlier):
    layer = (lax.axis_index("dev") >> 3).astype(jnp.int32).reshape(1)
    rows, width = own[0].shape[1:]
    count = len(others[0])

    def body(need, send, layer_ref, *refs):
        need()
        outs = refs[-4:]
        for mask, out in enumerate(outs):
            goal = layer_ref[0] ^ mask
            number = goal & 1
            for half in range(2):
                sources = refs[half * (count + 1) : (half + 1) * (count + 1)]

                @pl.when((goal >> 1) == half)
                def _():
                    total = sources[0][number]
                    for source in sources[1:]:
                        total = total + source[number].astype(jnp.float32)
                    out[...] = total.astype(out.dtype)

    kinds = (jnp.float32, jnp.bfloat16, jnp.bfloat16, jnp.bfloat16)
    return local_kernel(
        body,
        [((rows, width), kind) for kind in kinds],
        (own[0], *others[0], own[1], *others[1]),
        4 * rows * width,
        (layer,),
        earlier,
    )


def shards(
    tokens, attn_weight, mlp_weight, vectors, cotangent, seq_lengths, seq_device, seq_offset
):
    total_rows = tokens.shape[0]
    width = D
    scale = HEAD_SIZE ** (-0.5)
    low = jnp.bfloat16
    devices = lax.axis_size("dev")
    here = lax.axis_index("dev")
    chosen = (seq_device == here).astype(jnp.int32)
    begin = jnp.sum(chosen * seq_offset)
    finish = begin + jnp.sum(chosen * seq_lengths)
    positions = jnp.arange(total_rows, dtype=jnp.int32)
    keep = ((positions >= begin) & (positions < finish)).astype(jnp.int32)
    live = keep[:, None] == 1
    allowed = allowed_pairs(keep)
    head_shape = (total_rows, HEADS, HEAD_SIZE)

    full_vec = gather_vectors(vectors)
    grad_down = jnp.where(live, cotangent, jnp.zeros_like(cotangent))
    full_proj, full_out, attn_ready = gather_attn(attn_weight)
    gathered = gather_hidden(mlp_weight)
    grad_down_rows = gather_rows(grad_down.T)

    (
        gain_one,
        shift_one,
        query_bias,
        value_bias,
        out_bias,
        gain_two,
        shift_two,
        down_bias,
        up_bias,
    ) = split_vectors(full_vec)
    low_count = 8 if devices == 32 else 4
    up_bias = up_bias.reshape(devices // 2 // low_count, low_count, -1)

    inputs = tokens.astype(jnp.float32)
    first_out, normed_one, factor_one = normalize(inputs, gain_one, shift_one)
    first_low = first_out.astype(low)
    first_beside = swap(first_low.T, 1)
    projected = jnp.einsum(
        "rd,od->ro", first_low, full_proj, preferred_element_type=jnp.float32
    )
    queries = (projected[:, :width] + query_bias).astype(low).reshape(head_shape)
    keys = projected[:, width : 2 * width].astype(low).reshape(head_shape)
    values = (projected[:, 2 * width :] + value_bias).astype(low).reshape(head_shape)
    mixed, log_total = attend(queries, keys, values, allowed, scale)
    mixed_low = mixed.reshape(total_rows, width).astype(low)
    mixed_beside = swap(mixed_low.T, 1)
    branch = (
        jnp.einsum(
            "rd,od->ro", mixed_low, full_out, preferred_element_type=jnp.float32
        )
        + out_bias
    )
    middle = inputs + branch
    second_out, normed_two, factor_two = normalize(middle, gain_two, shift_two)
    second_own = second_out.astype(low).T
    near, far = gather_rows(second_own)
    parts = hidden_parts(gathered, here, devices, projected)
    near_grads, far_grads = grad_down_rows

    every = sum(parts, [])
    weights = [part[0] for part in every]
    biases = [pick_blocks(up_bias, *part[1:]).reshape(-1, 1) for part in every]
    far_blocks, far_sum = mlp_block(far, far_grads, weights, biases)
    near_blocks, near_sum = mlp_block(near, near_grads, weights, biases)
    grad_up_bias = jnp.zeros_like(up_bias)
    for part, one, two in zip(every, near_blocks, far_blocks):
        grad_up_bias = put_blocks(grad_up_bias, *part[1:], (one[2] + two[2]).reshape(-1))
    blocks = [(one[:2], two[:2]) for one, two in zip(near_blocks, far_blocks)]
    own_count = len(parts[0])
    far_total = (far_sum[0] + swap(far_sum[1], 1).astype(jnp.float32)).astype(low)
    grad_second = near_sum[0] + swap(near_sum[1], 1).astype(jnp.float32)
    all_rows, all_grads = near + far, near_grads + far_grads
    other_grads = []
    if len(parts) > 1:
        other_grads = mlp_weight_grads(blocks[own_count:], all_rows, all_grads, low, (far_total,))
    far_taken = after(swap(far_total, 2), other_grads)
    grad_second = (grad_second + far_taken.astype(jnp.float32)).T

    grad_down_wide = grad_down.astype(jnp.float32)
    grad_down_bias = jnp.sum(grad_down_wide, axis=0)
    grad_gain_two = jnp.sum(grad_second * normed_two, axis=0)
    grad_shift_two = jnp.sum(grad_second, axis=0)
    grad_middle = grad_down_wide + normalize_back(grad_second, normed_two, factor_two, gain_two)
    grad_branch = grad_middle.astype(low)
    grad_out_bias = jnp.sum(grad_branch.astype(jnp.float32), axis=0)
    grad_mixed = jnp.dot(grad_branch, full_out, preferred_element_type=jnp.float32)
    grad_mixed_low = grad_mixed.astype(low)
    grad_features = attend_back(
        queries.reshape(total_rows, width).T,
        keys.reshape(total_rows, width).T,
        values.reshape(total_rows, width).T,
        jnp.stack([begin, finish]),
        scale,
        grad_mixed_low.T,
        log_total.reshape(HEADS, 1, total_rows),
    )
    attn_finish, attn_sent = scatter_attn(
        (grad_features, grad_branch.T), ((first_low.T, first_beside), (mixed_low.T, mixed_beside))
    )
    own_grads = mlp_weight_grads(blocks[:own_count], all_rows, all_grads, jnp.float32, attn_sent)
    down_keep, down_give = mlp_outputs(blocks, weights, sum(own_grads, ()))
    down_taken = swap(down_give, 1).astype(jnp.float32)
    down = (down_keep[0] + down_taken[0]).T
    down_far = swap((down_keep[1] + down_taken[1]).astype(low), 2).astype(jnp.float32).T
    mlp_share = scatter_hidden(own_grads, other_grads, attn_sent)
    attn_share = attn_finish()
    grad_features = after(grad_features, attn_sent).reshape(3 * width, total_rows)
    output = jnp.where(live, middle + (down + down_far + down_bias), 0.0).astype(low)
    grad_columns = jnp.sum(grad_features.astype(jnp.float32), axis=1)
    grad_first = jnp.einsum(
        "fr,fd->rd", grad_features, full_proj, preferred_element_type=jnp.float32
    )
    grad_gain_one = jnp.sum(grad_first * normed_one, axis=0)
    grad_shift_one = jnp.sum(grad_first, axis=0)
    grad_inputs = grad_middle + normalize_back(grad_first, normed_one, factor_one, gain_one)
    grad_vec = jnp.concatenate(
        [
            grad_gain_one,
            grad_shift_one,
            grad_columns[:width],
            grad_columns[2 * width :],
            grad_out_bias,
            grad_gain_two,
            grad_shift_two,
            grad_down_bias,
            grad_up_bias.reshape(-1),
        ],
        axis=0,
    )
    vec_share = scatter_vectors(grad_vec)
    return (output, grad_inputs, attn_share, mlp_share, vec_share)


def solution(mesh):
    return jax.shard_map(
        shards,
        mesh=mesh,
        in_specs=(
            P("dev", None),
            P("dev", None),
            P("dev", None),
            P("dev"),
            P("dev", None),
            P(),
            P(),
            P(),
        ),
        out_specs=(P("dev", None), P("dev", None), P("dev", None), P("dev", None), P("dev")),
        check_vma=False,
    )
```

```python
import jax
import jax.numpy as jnp
from jax import lax
from jax.experimental import pallas as pl
from jax.experimental.pallas import tpu as pltpu
from jax.sharding import PartitionSpec as P

D = 1088
HEADS = 17
HEAD_SIZE = 64
FF = 4352
VMEM_LIMIT = 60 * 1024 * 1024


epsilon = 1e-05
neg_large = -1e30


def normalize(values, gain, shift):
    centre = values - jnp.mean(values, axis=-1, keepdims=True)
    spread = jnp.mean(centre * centre, axis=-1, keepdims=True)
    factor = lax.rsqrt(spread + epsilon)
    normed = centre * factor
    return (normed * gain + shift, normed, factor)


def normalize_back(grad_out, normed, factor, gain):
    inner = grad_out * gain
    return factor * (
        inner
        - jnp.mean(inner, axis=-1, keepdims=True)
        - normed * jnp.mean(inner * normed, axis=-1, keepdims=True)
    )


def split_vectors(whole_vec):
    width = D
    pieces = [
        whole_vec[number * width : (number + 1) * width].astype(jnp.float32) for number in range(8)
    ]
    return pieces + [whole_vec[8 * width :].astype(jnp.float32)]


def gelu_parts(values):
    share = 0.5 + 0.5 * lax.erf(values * (0.5**0.5))
    density = jnp.exp(-0.5 * values * values) * ((2.0 * jnp.pi) ** (-0.5))
    return (values * share, share + values * density)


def allowed_pairs(keep):
    position = jnp.arange(keep.shape[0], dtype=jnp.int32)
    return (position[None, :] <= position[:, None]) & (keep[None, :] == keep[:, None])


def attend(queries, keys, values, allowed, scale):
    scores = jnp.einsum("qhd,khd->hqk", queries, keys, preferred_element_type=jnp.float32) * scale
    scores = jnp.where(allowed[None], scores, neg_large)
    top = jnp.max(scores, axis=-1, keepdims=True)
    expo = jnp.exp(scores - top)
    total = jnp.sum(expo, axis=-1, keepdims=True)
    weights = (expo / total).astype(jnp.bfloat16)
    mixed = jnp.einsum("hqk,khd->qhd", weights, values, preferred_element_type=jnp.float32)
    return (mixed, top + jnp.log(total))


def local_kernel(body, outs, operands, scalars=(), earlier=()):
    outs = [jax.ShapeDtypeStruct(shape, kind) for shape, kind in outs]
    first, count, total = len(scalars), len(operands), len(operands) + len(outs)

    def whole(*refs):
        scalar_refs, sources = refs[:first], refs[first : first + count]
        goals = refs[first + count + len(earlier) :][: len(outs)]
        buffers, sems = refs[-total - 1 : -1], refs[-1]
        ends = tuple(zip(sources, buffers)) + tuple(zip(buffers[count:], goals))
        copies = [
            pltpu.make_async_copy(source, goal, sems.at[number])
            for number, (source, goal) in enumerate(ends)
        ]
        for copy in copies[:count]:
            copy.start()
        waiting = list(range(count))
        unsent = list(range(len(outs)))

        def need(*numbers):
            for number in numbers or tuple(waiting):
                if number in waiting:
                    waiting.remove(number)
                    copies[number].wait()

        def send(*numbers):
            for number in numbers:
                unsent.remove(number)
                copies[count + number].start()

        body(need, send, *scalar_refs, *buffers)
        if waiting:
            need()
        send(*tuple(unsent))
        for copy in copies[count:]:
            copy.wait()

    anywhere = pl.BlockSpec(memory_space=pl.ANY)
    return pl.pallas_call(
        whole,
        out_shape=outs,
        in_specs=[pl.BlockSpec(memory_space=pltpu.SMEM)] * first
        + [anywhere] * (count + len(earlier)),
        out_specs=[anywhere] * len(outs),
        scratch_shapes=[pltpu.VMEM(array.shape, array.dtype) for array in (*operands, *outs)]
        + [pltpu.SemaphoreType.DMA((total,))],
        compiler_params=pltpu.CompilerParams(vmem_limit_bytes=VMEM_LIMIT),
        cost_estimate=pl.CostEstimate(flops=1, bytes_accessed=1, transcendentals=0),
    )(*scalars, *operands, *earlier)


def product(left, right, left_axis, right_axis):
    return lax.dot_general(
        left, right, (((left_axis,), (right_axis,)), ((), ())), preferred_element_type=jnp.float32
    )


def attend_back(queries, keys, values, span, scale, grad_mixed, log_total):
    width, rows = queries.shape
    low = jnp.bfloat16

    def body(need, send, span_ref, q_ref, k_ref, v_ref, do_ref, log_ref, out_ref):
        need()
        begin, finish = span_ref[0], span_ref[1]

        def inside(axis):
            position = lax.broadcasted_iota(jnp.int32, (rows, rows), axis)
            return (position, (position >= begin) & (position < finish))

        key_pos, key_live = inside(0)
        query_pos, query_live = inside(1)
        allowed = (key_pos <= query_pos) & (key_live == query_live)

        for head in range(HEADS):
            part = pl.ds(head * HEAD_SIZE, HEAD_SIZE)
            q, k, v, do = q_ref[part, :], k_ref[part, :], v_ref[part, :], do_ref[part, :]
            scores = jnp.where(allowed, product(k, q, 0, 0) * scale, neg_large)
            probs = jnp.exp(scores - log_ref[head])
            out_ref[2, part, :] = product(do, probs.astype(low), 1, 1).astype(low)
            grad_probs = product(v, do, 0, 0)
            inner = jnp.sum(probs * grad_probs, axis=0, keepdims=True)
            grad_scores = (probs * (grad_probs - inner)).astype(low)
            out_ref[0, part, :] = (product(k, grad_scores, 1, 0) * scale).astype(low)
            out_ref[1, part, :] = (product(q, grad_scores, 1, 1) * scale).astype(low)

    return local_kernel(
        body,
        [((3, width, rows), low)],
        (queries, keys, values, grad_mixed, log_total),
        (span,),
    )[0]


def mlp_block(row_pair, grad_pair, weights, bias):
    width, rows = row_pair[0].shape
    low, wide = jnp.bfloat16, jnp.float32
    count = 2 * weights.shape[1]

    def body(need, send, *refs):
        row_refs, grad_refs, (weight, bias_ref) = refs[:2], refs[2:4], refs[4:6]
        act_ref, up_ref, sum_ref = refs[6:9]
        for side in (1, 0):
            need(side, 2 + side, 4, 5)
            total = None
            for part in range(2):
                span = slice(part * (count // 2), (part + 1) * (count // 2))
                up, down = weight[part], weight[2 + part]
                up_sum = product(up, row_refs[side][...], 1, 0) + bias_ref[span, :]
                activated, slope = gelu_parts(up_sum)
                grad_act = product(down, grad_refs[side][...], 1, 0)
                grad_up = (grad_act * slope).astype(low)
                act_ref[side, span, :] = activated.astype(low)
                up_ref[side, span, :] = grad_up
                columns = jnp.sum(grad_up.astype(wide), axis=1, keepdims=True)
                sum_ref[span, :] = columns if side == 1 else sum_ref[span, :] + columns
                term = product(grad_up, up, 0, 0)
                total = term if total is None else total + term
            out = refs[9 + side]
            out[...] = total.T.astype(out.dtype)
            send(3 + side)

    outs = [((2, count, rows), low), ((2, count, rows), low), ((count, 1), wide)]
    outs += [((width, rows), wide), ((width, rows), low)]
    result = local_kernel(body, outs, (*row_pair, *grad_pair, weights, bias))
    return (result[:3], result[3:])


def mlp_weight_grads(near, far, rows, grads, earlier):
    width, number = rows[0].shape[0], len(rows)
    count = near[0].shape[1]
    low = jnp.bfloat16

    def body(need, send, *refs):
        need()
        row_refs, grad_refs = refs[:number], refs[number : 2 * number]
        near_act, far_act, near_up, far_up, out = refs[2 * number :]
        for which, pair, others in (
            (0, (near_up, far_up), row_refs),
            (1, (near_act, far_act), grad_refs),
        ):
            for part in range(2):
                span = slice(part * (count // 2), (part + 1) * (count // 2))
                total = None
                for group in range(number):
                    left = pair[group // 2][group % 2, span, :]
                    term = product(left, others[group][...], 1, 1)
                    total = term if total is None else total + term
                start = which * count + part * (count // 2)
                out[start : start + count // 2, :] = total.astype(low)

    operands = (*rows, *grads, near[0], far[0], near[1], far[1])
    return local_kernel(body, [((2 * count, width), low)], operands, (), earlier)[0]


def mlp_outputs(near, far, weights, earlier):
    rows, half, width = near.shape[2], weights.shape[1], weights.shape[2]

    def body(need, send, *refs):
        need()
        weight, outs = refs[2], refs[3:]
        for group in range(2):
            for side in range(2):
                total = product(refs[group][side, :half, :], weight[2], 0, 0)
                total = total + product(refs[group][side, half:, :], weight[3], 0, 0)
                outs[side][group] = total.T.astype(outs[side].dtype)

    outs = [((2, width, rows), jnp.float32), ((2, width, rows), jnp.bfloat16)]
    return local_kernel(body, outs, (near, far, weights), (), earlier)


def gather_rows(own):
    across = swap(own, 2)
    beside = swap(own, 1)
    return ((own, beside), (across, swap(across, 1)))


def after(values, others):
    return lax.optimization_barrier((values, others))[0]


def swap(piece, mask):
    devices = lax.axis_size("dev")
    return lax.ppermute(piece, "dev", [(number, number ^ mask) for number in range(devices)])


def same_low(devices):
    return [list(range(low, devices, 4)) for low in range(4)]


def gather_vectors(own):
    here = lax.axis_index("dev")
    whole = own
    mask = 1
    while mask < lax.axis_size("dev"):
        other = swap(whole, mask)
        upper = (here & mask) != 0
        whole = jnp.concatenate(
            [jnp.where(upper, other, whole), jnp.where(upper, whole, other)], axis=0
        )
        mask *= 2
    return whole


def scatter_vectors(whole):
    here = lax.axis_index("dev")
    mask = lax.axis_size("dev") // 2
    while mask:
        half = whole.shape[0] // 2
        upper = (here & mask) != 0
        mine = jnp.where(upper, whole[half:], whole[:half])
        yours = jnp.where(upper, whole[:half], whole[half:])
        whole = mine + swap(yours, mask)
        mask //= 2
    return whole


def z_groups(devices):
    return [list(range(low, devices, 8)) for low in range(8)]


def gather_z(shard):
    devices = lax.axis_size("dev")
    return lax.all_gather(shard, "dev", axis=0, tiled=False, axis_index_groups=z_groups(devices))


def place_blocks(pieces):
    block = (lax.axis_index("dev") & 7).astype(jnp.int32).reshape(1)
    arrays = [piece[0] for piece in pieces]
    rows, width = arrays[0].shape[1:]
    count = sum(array.shape[0] for array in arrays)

    def body(block_ref, *refs):
        piece_refs = refs[: len(arrays)]
        three_ref, last_ref, sems = refs[len(arrays) :]
        copies = []
        for ref, (array, mask, begin) in zip(piece_refs, pieces):
            target = block_ref[0] ^ mask
            for number in range(array.shape[0]):
                matrix = begin + number
                goal = last_ref.at[target] if matrix == 3 else three_ref.at[matrix, target]
                copies.append(
                    pltpu.make_async_copy(ref.at[number], goal, sems.at[len(copies)])
                )
                copies[-1].start()
        for copy in copies:
            copy.wait()

    kind = arrays[0].dtype
    return pl.pallas_call(
        body,
        out_shape=(
            jax.ShapeDtypeStruct((3, 8, rows, width), kind),
            jax.ShapeDtypeStruct((8, rows, width), kind),
        ),
        in_specs=[pl.BlockSpec(memory_space=pltpu.SMEM)]
        + [pl.BlockSpec(memory_space=pl.ANY)] * len(arrays),
        out_specs=(pl.BlockSpec(memory_space=pltpu.VMEM), pl.BlockSpec(memory_space=pltpu.VMEM)),
        scratch_shapes=[pltpu.SemaphoreType.DMA((count,))],
        compiler_params=pltpu.CompilerParams(vmem_limit_bytes=24 * 1024 * 1024),
        cost_estimate=pl.CostEstimate(flops=1, bytes_accessed=1, transcendentals=0),
    )(block, *arrays)


def gather_attn(shard):
    devices = lax.axis_size("dev")
    if devices != 32:
        whole = lax.all_gather(shard, "dev", axis=0, tiled=True)
        width = shard.shape[1]
        return (whole[: 3 * width], whole[3 * width :], shard)
    own = gather_z(shard)
    along, across = swap(own, 4), swap(own, 2)
    beside = swap(own, 1)
    upper, lower = swap(along[:2], 2), swap(across[2:], 4)
    pieces = [(own, 0, 0), (beside, 1, 0), (along, 4, 0), (across, 2, 0)]
    pieces += [(swap(along, 1), 5, 0), (swap(across, 1), 3, 0)]
    pieces += [(upper, 6, 0), (lower, 6, 2), (swap(upper, 1), 7, 0), (swap(lower, 1), 7, 2)]
    three, last = place_blocks(pieces)
    width = shard.shape[1]
    return (three.reshape(3 * width, width), last.reshape(width, width), (upper, lower))


def scatter_attn(grads, sources):
    devices = lax.axis_size("dev")
    low = jnp.bfloat16
    first, mixed = sources
    width, own = first[0].shape
    if devices != 32:
        product = jnp.concatenate(
            [
                jnp.einsum('fr,dr->fd', grads[0].reshape(3 * width, own), first[0], preferred_element_type=jnp.float32),
                jnp.einsum('fr,dr->fd', grads[1], mixed[0], preferred_element_type=jnp.float32),
            ],
            axis=0,
        ).astype(low)
        share = lax.psum_scatter(product, "dev", scatter_dimension=0, tiled=True)
        return (lambda: share.astype(jnp.float32), grads)
    pairs = ((first[0], mixed[0]), (first[1], mixed[1]))
    grads = [part.reshape(-1, 8, width // 8, own) for part in grads]
    diagonal, across, along, mine = attn_products(grads, [swap(part, 1) for part in grads], pairs)

    across_upper = swap(across[0], 2)
    along_lower = swap(along[1], 4)
    along_diagonal = swap(diagonal[1], 4).astype(jnp.float32)
    across_diagonal = swap(diagonal[0], 2).astype(jnp.float32)
    across_lower = swap((across[1] + along_diagonal).astype(low), 2)
    along_upper = swap((along[0] + across_diagonal).astype(low), 4)

    def finish():
        return add_z(*route_z(mine, ((across_upper, along_upper), (across_lower, along_lower)), ()))

    return (finish, (across[1], along[0]))


def attn_products(mine, beside, pairs):
    block = (lax.axis_index("dev") & 7).astype(jnp.int32).reshape(1)
    rows = mine[0].shape[2]
    width = pairs[0][0].shape[0]
    low, wide = jnp.bfloat16, jnp.float32
    kinds = (low, low, low, wide, wide, low, wide, wide)

    def body(need, send, block_ref, *refs):
        need()
        (three, last), (three_beside, last_beside) = refs[:2], refs[2:4]
        pair_refs, other_refs = refs[4:6], refs[6:8]
        outs = refs[8:]
        for place, mask in enumerate((6, 2, 4, 0)):
            target = block_ref[0] ^ mask
            for half in range(2):
                out = outs[2 * place + half]
                for number in range(2):
                    matrix = 2 * half + number
                    left = last[0, target] if matrix == 3 else three[matrix, target]
                    left_beside = (
                        last_beside[0, target] if matrix == 3 else three_beside[matrix, target]
                    )
                    side = 1 if matrix == 3 else 0
                    value = product(left, pair_refs[side][...], 1, 1)
                    value = value + product(left_beside, other_refs[side][...], 1, 1)
                    out[number] = value.astype(out.dtype)
                send(2 * place + half)

    outs = local_kernel(
        body,
        [((2, rows, width), kind) for kind in kinds],
        (*mine, *beside, *pairs[0], *pairs[1]),
        (block,),
    )
    return [outs[2 * place : 2 * place + 2] for place in range(4)]


def gather_hidden(shard):
    devices = lax.axis_size("dev")
    both = lax.all_gather(shard, "dev", axis=0, tiled=True, axis_index_groups=same_low(devices))
    return both.reshape(4, -1, both.shape[1])


def scatter_hidden(grads):
    devices = lax.axis_size("dev")
    share = lax.psum_scatter(
        grads, "dev", scatter_dimension=0, tiled=True, axis_index_groups=same_low(devices)
    )
    return share.astype(jnp.float32)


def add_z(mine, one, two, three):
    wide = jnp.float32
    return (
        mine
        + swap(two, 16).astype(wide)
        + swap(three, 24).astype(wide)
        + swap(one, 8).astype(wide)
    )


def route_z(own, others, earlier):
    layer = (lax.axis_index("dev") >> 3).astype(jnp.int32).reshape(1)
    rows, width = own[0].shape[1:]
    count = len(others[0])

    def body(need, send, layer_ref, *refs):
        need()
        outs = refs[-4:]
        for mask, out in enumerate(outs):
            goal = layer_ref[0] ^ mask
            number = goal & 1
            for half in range(2):
                sources = refs[half * (count + 1) : (half + 1) * (count + 1)]

                @pl.when((goal >> 1) == half)
                def _():
                    total = sources[0][number]
                    for source in sources[1:]:
                        total = total + source[number].astype(jnp.float32)
                    out[...] = total.astype(out.dtype)

    kinds = (jnp.float32, jnp.bfloat16, jnp.bfloat16, jnp.bfloat16)
    return local_kernel(
        body,
        [((rows, width), kind) for kind in kinds],
        (own[0], *others[0], own[1], *others[1]),
        (layer,),
        earlier,
    )


def shards(
    tokens, attn_weight, mlp_weight, vectors, cotangent, seq_lengths, seq_device, seq_offset
):
    total_rows = tokens.shape[0]
    width = D
    scale = HEAD_SIZE ** (-0.5)
    low = jnp.bfloat16
    devices = lax.axis_size("dev")
    here = lax.axis_index("dev")
    chosen = (seq_device == here).astype(jnp.int32)
    begin = jnp.sum(chosen * seq_offset)
    finish = begin + jnp.sum(chosen * seq_lengths)
    positions = jnp.arange(total_rows, dtype=jnp.int32)
    keep = ((positions >= begin) & (positions < finish)).astype(jnp.int32)
    live = keep[:, None] == 1
    allowed = allowed_pairs(keep)
    head_shape = (total_rows, HEADS, HEAD_SIZE)

    full_vec = gather_vectors(vectors)
    grad_down = jnp.where(live, cotangent, jnp.zeros_like(cotangent))
    full_proj, full_out, attn_ready = gather_attn(attn_weight)
    weights = gather_hidden(mlp_weight)
    grad_down_rows = gather_rows(grad_down.T)

    (
        gain_one,
        shift_one,
        query_bias,
        value_bias,
        out_bias,
        gain_two,
        shift_two,
        down_bias,
        up_bias,
    ) = split_vectors(full_vec)
    up_bias = up_bias.reshape(devices // 8, 4, -1)

    inputs = tokens.astype(jnp.float32)
    first_out, normed_one, factor_one = normalize(inputs, gain_one, shift_one)
    first_low = first_out.astype(low)
    first_beside = swap(first_low.T, 1)
    projected = jnp.einsum(
        "rd,od->ro", first_low, full_proj, preferred_element_type=jnp.float32
    )
    queries = (projected[:, :width] + query_bias).astype(low).reshape(head_shape)
    keys = projected[:, width : 2 * width].astype(low).reshape(head_shape)
    values = (projected[:, 2 * width :] + value_bias).astype(low).reshape(head_shape)
    mixed, log_total = attend(queries, keys, values, allowed, scale)
    mixed_low = mixed.reshape(total_rows, width).astype(low)
    mixed_beside = swap(mixed_low.T, 1)
    branch = (
        jnp.einsum(
            "rd,od->ro", mixed_low, full_out, preferred_element_type=jnp.float32
        )
        + out_bias
    )
    middle = inputs + branch
    second_out, normed_two, factor_two = normalize(middle, gain_two, shift_two)
    second_own = second_out.astype(low).T
    near, far = gather_rows(second_own)
    near_grads, far_grads = grad_down_rows
    mine = here & 3
    bias = lax.dynamic_index_in_dim(up_bias, mine, 1, False).reshape(-1, 1)
    far_block, far_sum = mlp_block(far, far_grads, weights, bias)
    near_block, near_sum = mlp_block(near, near_grads, weights, bias)
    column_sums = (near_block[2] + far_block[2]).reshape(up_bias.shape[0], 1, -1)
    grad_up_bias = lax.dynamic_update_slice(jnp.zeros_like(up_bias), column_sums, (0, mine, 0))
    far_total = (far_sum[0] + swap(far_sum[1], 1).astype(jnp.float32)).astype(low)
    grad_second = near_sum[0] + swap(near_sum[1], 1).astype(jnp.float32)
    weight_grads = mlp_weight_grads(
        near_block, far_block, near + far, near_grads + far_grads, (far_total,)
    )
    mlp_share = scatter_hidden(weight_grads)
    far_taken = after(swap(far_total, 2), weight_grads)
    grad_second = (grad_second + far_taken.astype(jnp.float32)).T

    grad_down_wide = grad_down.astype(jnp.float32)
    grad_down_bias = jnp.sum(grad_down_wide, axis=0)
    grad_gain_two = jnp.sum(grad_second * normed_two, axis=0)
    grad_shift_two = jnp.sum(grad_second, axis=0)
    grad_middle = grad_down_wide + normalize_back(grad_second, normed_two, factor_two, gain_two)
    grad_branch = grad_middle.astype(low)
    grad_out_bias = jnp.sum(grad_branch.astype(jnp.float32), axis=0)
    grad_mixed = jnp.dot(grad_branch, full_out, preferred_element_type=jnp.float32)
    grad_mixed_low = grad_mixed.astype(low)
    grad_features = attend_back(
        queries.reshape(total_rows, width).T,
        keys.reshape(total_rows, width).T,
        values.reshape(total_rows, width).T,
        jnp.stack([begin, finish]),
        scale,
        grad_mixed_low.T,
        log_total.reshape(HEADS, 1, total_rows),
    )
    attn_finish, attn_sent = scatter_attn(
        (grad_features, grad_branch.T), ((first_low.T, first_beside), (mixed_low.T, mixed_beside))
    )
    down_keep, down_give = mlp_outputs(near_block[0], far_block[0], weights, attn_sent)
    down_taken = swap(down_give, 1).astype(jnp.float32)
    down = (down_keep[0] + down_taken[0]).T
    down_far = swap((down_keep[1] + down_taken[1]).astype(low), 2).astype(jnp.float32).T
    attn_share = attn_finish()
    grad_features = after(grad_features, attn_sent).reshape(3 * width, total_rows)
    output = jnp.where(live, middle + (down + down_far + down_bias), 0.0).astype(low)
    grad_columns = jnp.sum(grad_features.astype(jnp.float32), axis=1)
    grad_first = jnp.einsum(
        "fr,fd->rd", grad_features, full_proj, preferred_element_type=jnp.float32
    )
    grad_gain_one = jnp.sum(grad_first * normed_one, axis=0)
    grad_shift_one = jnp.sum(grad_first, axis=0)
    grad_inputs = grad_middle + normalize_back(grad_first, normed_one, factor_one, gain_one)
    grad_vec = jnp.concatenate(
        [
            grad_gain_one,
            grad_shift_one,
            grad_columns[:width],
            grad_columns[2 * width :],
            grad_out_bias,
            grad_gain_two,
            grad_shift_two,
            grad_down_bias,
            grad_up_bias.reshape(-1),
        ],
        axis=0,
    )
    vec_share = scatter_vectors(grad_vec)
    return (output, grad_inputs, attn_share, mlp_share, vec_share)


def solution(mesh):
    return jax.shard_map(
        shards,
        mesh=mesh,
        in_specs=(
            P("dev", None),
            P("dev", None),
            P("dev", None),
            P("dev"),
            P("dev", None),
            P(),
            P(),
            P(),
        ),
        out_specs=(P("dev", None), P("dev", None), P("dev", None), P("dev", None), P("dev")),
        check_vma=False,
    )
```

```python
import jax
import jax.numpy as jnp
from jax import lax
from jax.experimental import pallas as pl
from jax.experimental.pallas import tpu as pltpu
from jax.sharding import PartitionSpec as P

D = 1088
HEADS = 17
HEAD_SIZE = 64
FF = 4352
VMEM_LIMIT = 60 * 1024 * 1024


epsilon = 1e-05
neg_large = -1e30


def normalize(values, gain, shift):
    centre = values - jnp.mean(values, axis=-1, keepdims=True)
    spread = jnp.mean(centre * centre, axis=-1, keepdims=True)
    factor = lax.rsqrt(spread + epsilon)
    normed = centre * factor
    return (normed * gain + shift, normed, factor)


def normalize_back(grad_out, normed, factor, gain):
    inner = grad_out * gain
    return factor * (
        inner
        - jnp.mean(inner, axis=-1, keepdims=True)
        - normed * jnp.mean(inner * normed, axis=-1, keepdims=True)
    )


def split_vectors(whole_vec):
    width = D
    pieces = [
        whole_vec[number * width : (number + 1) * width].astype(jnp.float32) for number in range(8)
    ]
    return pieces + [whole_vec[8 * width :].astype(jnp.float32)]


def gelu_parts(values):
    share = 0.5 + 0.5 * lax.erf(values * (0.5**0.5))
    density = jnp.exp(-0.5 * values * values) * ((2.0 * jnp.pi) ** (-0.5))
    return (values * share, share + values * density)


def allowed_pairs(keep):
    position = jnp.arange(keep.shape[0], dtype=jnp.int32)
    return (position[None, :] <= position[:, None]) & (keep[None, :] == keep[:, None])


def attend(queries, keys, values, allowed, scale):
    scores = jnp.einsum("qhd,khd->hqk", queries, keys, preferred_element_type=jnp.float32) * scale
    scores = jnp.where(allowed[None], scores, neg_large)
    top = jnp.max(scores, axis=-1, keepdims=True)
    expo = jnp.exp(scores - top)
    total = jnp.sum(expo, axis=-1, keepdims=True)
    weights = (expo / total).astype(jnp.bfloat16)
    mixed = jnp.einsum("hqk,khd->qhd", weights, values, preferred_element_type=jnp.float32)
    return (mixed, top + jnp.log(total))


def local_kernel(body, outs, operands, scalars=(), earlier=()):
    outs = [jax.ShapeDtypeStruct(shape, kind) for shape, kind in outs]
    first, count, total = len(scalars), len(operands), len(operands) + len(outs)

    def whole(*refs):
        scalar_refs, sources = refs[:first], refs[first : first + count]
        goals = refs[first + count + len(earlier) :][: len(outs)]
        buffers, sems = refs[-total - 1 : -1], refs[-1]
        ends = tuple(zip(sources, buffers)) + tuple(zip(buffers[count:], goals))
        copies = [
            pltpu.make_async_copy(source, goal, sems.at[number])
            for number, (source, goal) in enumerate(ends)
        ]
        for copy in copies[:count]:
            copy.start()
        waiting = list(range(count))
        unsent = list(range(len(outs)))

        def need(*numbers):
            for number in numbers or tuple(waiting):
                if number in waiting:
                    waiting.remove(number)
                    copies[number].wait()

        def send(*numbers):
            for number in numbers:
                unsent.remove(number)
                copies[count + number].start()

        body(need, send, *scalar_refs, *buffers)
        if waiting:
            need()
        send(*tuple(unsent))
        for copy in copies[count:]:
            copy.wait()

    anywhere = pl.BlockSpec(memory_space=pl.ANY)
    return pl.pallas_call(
        whole,
        out_shape=outs,
        in_specs=[pl.BlockSpec(memory_space=pltpu.SMEM)] * first
        + [anywhere] * (count + len(earlier)),
        out_specs=[anywhere] * len(outs),
        scratch_shapes=[pltpu.VMEM(array.shape, array.dtype) for array in (*operands, *outs)]
        + [pltpu.SemaphoreType.DMA((total,))],
        compiler_params=pltpu.CompilerParams(vmem_limit_bytes=VMEM_LIMIT),
        cost_estimate=pl.CostEstimate(flops=1, bytes_accessed=1, transcendentals=0),
    )(*scalars, *operands, *earlier)


def product(left, right, left_axis, right_axis):
    return lax.dot_general(
        left, right, (((left_axis,), (right_axis,)), ((), ())), preferred_element_type=jnp.float32
    )


def attend_back(queries, keys, values, span, scale, grad_mixed, log_total):
    width, rows = queries.shape
    low = jnp.bfloat16

    def body(need, send, span_ref, q_ref, k_ref, v_ref, do_ref, log_ref, out_ref):
        need()
        begin, finish = span_ref[0], span_ref[1]

        def inside(axis):
            position = lax.broadcasted_iota(jnp.int32, (rows, rows), axis)
            return (position, (position >= begin) & (position < finish))

        key_pos, key_live = inside(0)
        query_pos, query_live = inside(1)
        allowed = (key_pos <= query_pos) & (key_live == query_live)

        for head in range(HEADS):
            part = pl.ds(head * HEAD_SIZE, HEAD_SIZE)
            q, k, v, do = q_ref[part, :], k_ref[part, :], v_ref[part, :], do_ref[part, :]
            scores = jnp.where(allowed, product(k, q, 0, 0) * scale, neg_large)
            probs = jnp.exp(scores - log_ref[head])
            out_ref[2, part, :] = product(do, probs.astype(low), 1, 1).astype(low)
            grad_probs = product(v, do, 0, 0)
            inner = jnp.sum(probs * grad_probs, axis=0, keepdims=True)
            grad_scores = (probs * (grad_probs - inner)).astype(low)
            out_ref[0, part, :] = (product(k, grad_scores, 1, 0) * scale).astype(low)
            out_ref[1, part, :] = (product(q, grad_scores, 1, 1) * scale).astype(low)

    return local_kernel(
        body,
        [((3, width, rows), low)],
        (queries, keys, values, grad_mixed, log_total),
        (span,),
    )[0]


def mlp_block(row_pair, grad_pair, weights, bias):
    width, rows = row_pair[0].shape
    low, wide = jnp.bfloat16, jnp.float32
    count = 2 * weights.shape[1]

    def body(need, send, *refs):
        row_refs, grad_refs, (weight, bias_ref) = refs[:2], refs[2:4], refs[4:6]
        act_ref, up_ref, sum_ref = refs[6:9]
        for side in (1, 0):
            need(side, 2 + side, 4, 5)
            total = None
            for part in range(2):
                span = slice(part * (count // 2), (part + 1) * (count // 2))
                up, down = weight[part], weight[2 + part]
                up_sum = product(up, row_refs[side][...], 1, 0) + bias_ref[span, :]
                activated, slope = gelu_parts(up_sum)
                grad_act = product(down, grad_refs[side][...], 1, 0)
                grad_up = (grad_act * slope).astype(low)
                act_ref[side, span, :] = activated.astype(low)
                up_ref[side, span, :] = grad_up
                columns = jnp.sum(grad_up.astype(wide), axis=1, keepdims=True)
                sum_ref[span, :] = columns if side == 1 else sum_ref[span, :] + columns
                term = product(grad_up, up, 0, 0)
                total = term if total is None else total + term
            out = refs[9 + side]
            out[...] = total.T.astype(out.dtype)
            send(3 + side)

    outs = [((2, count, rows), low), ((2, count, rows), low), ((count, 1), wide)]
    outs += [((width, rows), wide), ((width, rows), low)]
    result = local_kernel(body, outs, (*row_pair, *grad_pair, weights, bias))
    return (result[:3], result[3:])


def mlp_weight_grads(near, far, rows, grads, earlier):
    width, number = rows[0].shape[0], len(rows)
    count = near[0].shape[1]
    low = jnp.bfloat16

    def body(need, send, *refs):
        near_up, far_up = refs[number : number + 2]
        row_refs, grad_refs = refs[:number], refs[number + 2 : 2 * number + 2]
        near_act, far_act, out = refs[2 * number + 2 :]
        need(*range(number + 2))
        for which, pair, others in (
            (0, (near_up, far_up), row_refs),
            (1, (near_act, far_act), grad_refs),
        ):
            if which:
                need()
            for part in range(2):
                span = slice(part * (count // 2), (part + 1) * (count // 2))
                total = None
                for group in range(number):
                    left = pair[group // 2][group % 2, span, :]
                    term = product(left, others[group][...], 1, 1)
                    total = term if total is None else total + term
                start = which * count + part * (count // 2)
                out[start : start + count // 2, :] = total.astype(low)

    operands = (*rows, near[1], far[1], *grads, near[0], far[0])
    return local_kernel(body, [((2 * count, width), low)], operands, (), earlier)[0]


def mlp_outputs(near, far, weights, earlier):
    rows, half, width = near.shape[2], weights.shape[1], weights.shape[2]

    def body(need, send, *refs):
        need()
        weight, outs = refs[2], refs[3:]
        for group in range(2):
            for side in range(2):
                total = product(refs[group][side, :half, :], weight[2], 0, 0)
                total = total + product(refs[group][side, half:, :], weight[3], 0, 0)
                outs[side][group] = total.T.astype(outs[side].dtype)

    outs = [((2, width, rows), jnp.float32), ((2, width, rows), jnp.bfloat16)]
    return local_kernel(body, outs, (near, far, weights), (), earlier)


def gather_rows(own):
    across = swap(own, 2)
    beside = swap(own, 1)
    return ((own, beside), (across, swap(across, 1)))


def after(values, others):
    return lax.optimization_barrier((values, others))[0]


def swap(piece, mask):
    devices = lax.axis_size("dev")
    return lax.ppermute(piece, "dev", [(number, number ^ mask) for number in range(devices)])


def same_low(devices):
    return [list(range(low, devices, 4)) for low in range(4)]


def gather_vectors(own):
    here = lax.axis_index("dev")
    whole = own
    mask = 1
    while mask < lax.axis_size("dev"):
        other = swap(whole, mask)
        upper = (here & mask) != 0
        whole = jnp.concatenate(
            [jnp.where(upper, other, whole), jnp.where(upper, whole, other)], axis=0
        )
        mask *= 2
    return whole


def scatter_vectors(whole):
    here = lax.axis_index("dev")
    mask = lax.axis_size("dev") // 2
    while mask:
        half = whole.shape[0] // 2
        upper = (here & mask) != 0
        mine = jnp.where(upper, whole[half:], whole[:half])
        yours = jnp.where(upper, whole[:half], whole[half:])
        whole = mine + swap(yours, mask)
        mask //= 2
    return whole


def z_groups(devices):
    return [list(range(low, devices, 8)) for low in range(8)]


def gather_z(shard):
    devices = lax.axis_size("dev")
    return lax.all_gather(shard, "dev", axis=0, tiled=False, axis_index_groups=z_groups(devices))


def place_blocks(pieces):
    block = (lax.axis_index("dev") & 7).astype(jnp.int32).reshape(1)
    arrays = [piece[0] for piece in pieces]
    rows, width = arrays[0].shape[1:]
    count = sum(array.shape[0] for array in arrays)

    def body(block_ref, *refs):
        piece_refs = refs[: len(arrays)]
        three_ref, last_ref, sems = refs[len(arrays) :]
        copies = []
        for ref, (array, mask, begin) in zip(piece_refs, pieces):
            target = block_ref[0] ^ mask
            for number in range(array.shape[0]):
                matrix = begin + number
                goal = last_ref.at[target] if matrix == 3 else three_ref.at[matrix, target]
                copies.append(
                    pltpu.make_async_copy(ref.at[number], goal, sems.at[len(copies)])
                )
                copies[-1].start()
        for copy in copies:
            copy.wait()

    kind = arrays[0].dtype
    return pl.pallas_call(
        body,
        out_shape=(
            jax.ShapeDtypeStruct((3, 8, rows, width), kind),
            jax.ShapeDtypeStruct((8, rows, width), kind),
        ),
        in_specs=[pl.BlockSpec(memory_space=pltpu.SMEM)]
        + [pl.BlockSpec(memory_space=pl.ANY)] * len(arrays),
        out_specs=(pl.BlockSpec(memory_space=pltpu.VMEM), pl.BlockSpec(memory_space=pltpu.VMEM)),
        scratch_shapes=[pltpu.SemaphoreType.DMA((count,))],
        compiler_params=pltpu.CompilerParams(vmem_limit_bytes=24 * 1024 * 1024),
        cost_estimate=pl.CostEstimate(flops=1, bytes_accessed=1, transcendentals=0),
    )(block, *arrays)


def gather_attn(shard):
    devices = lax.axis_size("dev")
    if devices != 32:
        whole = lax.all_gather(shard, "dev", axis=0, tiled=True)
        width = shard.shape[1]
        return (whole[: 3 * width], whole[3 * width :], shard)
    own = gather_z(shard)
    along, across = swap(own, 4), swap(own, 2)
    beside = swap(own, 1)
    upper, lower = swap(along[:2], 2), swap(across[2:], 4)
    pieces = [(own, 0, 0), (beside, 1, 0), (along, 4, 0), (across, 2, 0)]
    pieces += [(swap(along, 1), 5, 0), (swap(across, 1), 3, 0)]
    pieces += [(upper, 6, 0), (lower, 6, 2), (swap(upper, 1), 7, 0), (swap(lower, 1), 7, 2)]
    three, last = place_blocks(pieces)
    width = shard.shape[1]
    return (three.reshape(3 * width, width), last.reshape(width, width), (upper, lower))


def scatter_attn(grads, sources):
    devices = lax.axis_size("dev")
    low = jnp.bfloat16
    first, mixed = sources
    width, own = first[0].shape
    if devices != 32:
        product = jnp.concatenate(
            [
                jnp.einsum('fr,dr->fd', grads[0].reshape(3 * width, own), first[0], preferred_element_type=jnp.float32),
                jnp.einsum('fr,dr->fd', grads[1], mixed[0], preferred_element_type=jnp.float32),
            ],
            axis=0,
        ).astype(low)
        share = lax.psum_scatter(product, "dev", scatter_dimension=0, tiled=True)
        return (lambda: share.astype(jnp.float32), grads)
    pairs = ((first[0], mixed[0]), (first[1], mixed[1]))
    grads = [part.reshape(-1, 8, width // 8, own) for part in grads]
    diagonal, across, along, mine = attn_products(grads, [swap(part, 1) for part in grads], pairs)

    across_upper = swap(across[0], 2)
    along_lower = swap(along[1], 4)
    along_diagonal = swap(diagonal[1], 4).astype(jnp.float32)
    across_diagonal = swap(diagonal[0], 2).astype(jnp.float32)
    across_lower = swap((across[1] + along_diagonal).astype(low), 2)
    along_upper = swap((along[0] + across_diagonal).astype(low), 4)

    def finish():
        return add_z(*route_z(mine, ((across_upper, along_upper), (across_lower, along_lower)), ()))

    return (finish, (across[1], along[0]))


def attn_products(mine, beside, pairs):
    block = (lax.axis_index("dev") & 7).astype(jnp.int32).reshape(1)
    rows = mine[0].shape[2]
    width = pairs[0][0].shape[0]
    low, wide = jnp.bfloat16, jnp.float32
    kinds = (low, low, low, wide, wide, low, wide, wide)

    def body(need, send, block_ref, *refs):
        need()
        (three, last), (three_beside, last_beside) = refs[:2], refs[2:4]
        pair_refs, other_refs = refs[4:6], refs[6:8]
        outs = refs[8:]
        for place, mask in enumerate((6, 2, 4, 0)):
            target = block_ref[0] ^ mask
            for half in range(2):
                out = outs[2 * place + half]
                for number in range(2):
                    matrix = 2 * half + number
                    left = last[0, target] if matrix == 3 else three[matrix, target]
                    left_beside = (
                        last_beside[0, target] if matrix == 3 else three_beside[matrix, target]
                    )
                    side = 1 if matrix == 3 else 0
                    value = product(left, pair_refs[side][...], 1, 1)
                    value = value + product(left_beside, other_refs[side][...], 1, 1)
                    out[number] = value.astype(out.dtype)
                send(2 * place + half)

    outs = local_kernel(
        body,
        [((2, rows, width), kind) for kind in kinds],
        (*mine, *beside, *pairs[0], *pairs[1]),
        (block,),
    )
    return [outs[2 * place : 2 * place + 2] for place in range(4)]


def gather_hidden(shard):
    devices = lax.axis_size("dev")
    both = lax.all_gather(shard, "dev", axis=0, tiled=True, axis_index_groups=same_low(devices))
    return both.reshape(4, -1, both.shape[1])


def scatter_hidden(grads):
    devices = lax.axis_size("dev")
    share = lax.psum_scatter(
        grads, "dev", scatter_dimension=0, tiled=True, axis_index_groups=same_low(devices)
    )
    return share.astype(jnp.float32)


def add_z(mine, one, two, three):
    wide = jnp.float32
    return (
        mine
        + swap(two, 16).astype(wide)
        + swap(three, 24).astype(wide)
        + swap(one, 8).astype(wide)
    )


def route_z(own, others, earlier):
    layer = (lax.axis_index("dev") >> 3).astype(jnp.int32).reshape(1)
    rows, width = own[0].shape[1:]
    count = len(others[0])

    def body(need, send, layer_ref, *refs):
        need()
        outs = refs[-4:]
        for mask, out in enumerate(outs):
            goal = layer_ref[0] ^ mask
            number = goal & 1
            for half in range(2):
                sources = refs[half * (count + 1) : (half + 1) * (count + 1)]

                @pl.when((goal >> 1) == half)
                def _():
                    total = sources[0][number]
                    for source in sources[1:]:
                        total = total + source[number].astype(jnp.float32)
                    out[...] = total.astype(out.dtype)

    kinds = (jnp.float32, jnp.bfloat16, jnp.bfloat16, jnp.bfloat16)
    return local_kernel(
        body,
        [((rows, width), kind) for kind in kinds],
        (own[0], *others[0], own[1], *others[1]),
        (layer,),
        earlier,
    )


def shards(
    tokens, attn_weight, mlp_weight, vectors, cotangent, seq_lengths, seq_device, seq_offset
):
    total_rows = tokens.shape[0]
    width = D
    scale = HEAD_SIZE ** (-0.5)
    low = jnp.bfloat16
    devices = lax.axis_size("dev")
    here = lax.axis_index("dev")
    chosen = (seq_device == here).astype(jnp.int32)
    begin = jnp.sum(chosen * seq_offset)
    finish = begin + jnp.sum(chosen * seq_lengths)
    positions = jnp.arange(total_rows, dtype=jnp.int32)
    keep = ((positions >= begin) & (positions < finish)).astype(jnp.int32)
    live = keep[:, None] == 1
    allowed = allowed_pairs(keep)
    head_shape = (total_rows, HEADS, HEAD_SIZE)

    full_vec = gather_vectors(vectors)
    grad_down = jnp.where(live, cotangent, jnp.zeros_like(cotangent))
    full_proj, full_out, attn_ready = gather_attn(attn_weight)
    weights = gather_hidden(mlp_weight)
    grad_down_rows = gather_rows(grad_down.T)

    (
        gain_one,
        shift_one,
        query_bias,
        value_bias,
        out_bias,
        gain_two,
        shift_two,
        down_bias,
        up_bias,
    ) = split_vectors(full_vec)
    up_bias = up_bias.reshape(devices // 8, 4, -1)

    inputs = tokens.astype(jnp.float32)
    first_out, normed_one, factor_one = normalize(inputs, gain_one, shift_one)
    first_low = first_out.astype(low)
    first_beside = swap(first_low.T, 1)
    projected = jnp.einsum(
        "rd,od->ro", first_low, full_proj, preferred_element_type=jnp.float32
    )
    queries = (projected[:, :width] + query_bias).astype(low).reshape(head_shape)
    keys = projected[:, width : 2 * width].astype(low).reshape(head_shape)
    values = (projected[:, 2 * width :] + value_bias).astype(low).reshape(head_shape)
    mixed, log_total = attend(queries, keys, values, allowed, scale)
    mixed_low = mixed.reshape(total_rows, width).astype(low)
    mixed_beside = swap(mixed_low.T, 1)
    branch = (
        jnp.einsum(
            "rd,od->ro", mixed_low, full_out, preferred_element_type=jnp.float32
        )
        + out_bias
    )
    middle = inputs + branch
    second_out, normed_two, factor_two = normalize(middle, gain_two, shift_two)
    second_own = second_out.astype(low).T
    near, far = gather_rows(second_own)
    near_grads, far_grads = grad_down_rows
    mine = here & 3
    bias = lax.dynamic_index_in_dim(up_bias, mine, 1, False).reshape(-1, 1)
    far_block, far_sum = mlp_block(far, far_grads, weights, bias)
    near_block, near_sum = mlp_block(near, near_grads, weights, bias)
    column_sums = (near_block[2] + far_block[2]).reshape(up_bias.shape[0], 1, -1)
    grad_up_bias = lax.dynamic_update_slice(jnp.zeros_like(up_bias), column_sums, (0, mine, 0))
    far_total = (far_sum[0] + swap(far_sum[1], 1).astype(jnp.float32)).astype(low)
    grad_second = near_sum[0] + swap(near_sum[1], 1).astype(jnp.float32)
    weight_grads = mlp_weight_grads(
        near_block, far_block, near + far, near_grads + far_grads, (far_total,)
    )
    mlp_share = scatter_hidden(weight_grads)
    far_taken = after(swap(far_total, 2), weight_grads)
    grad_second = (grad_second + far_taken.astype(jnp.float32)).T

    grad_down_wide = grad_down.astype(jnp.float32)
    grad_down_bias = jnp.sum(grad_down_wide, axis=0)
    grad_gain_two = jnp.sum(grad_second * normed_two, axis=0)
    grad_shift_two = jnp.sum(grad_second, axis=0)
    grad_middle = grad_down_wide + normalize_back(grad_second, normed_two, factor_two, gain_two)
    grad_branch = grad_middle.astype(low)
    grad_out_bias = jnp.sum(grad_branch.astype(jnp.float32), axis=0)
    grad_mixed = jnp.dot(grad_branch, full_out, preferred_element_type=jnp.float32)
    grad_mixed_low = grad_mixed.astype(low)
    grad_features = attend_back(
        queries.reshape(total_rows, width).T,
        keys.reshape(total_rows, width).T,
        values.reshape(total_rows, width).T,
        jnp.stack([begin, finish]),
        scale,
        grad_mixed_low.T,
        log_total.reshape(HEADS, 1, total_rows),
    )
    attn_finish, attn_sent = scatter_attn(
        (grad_features, grad_branch.T), ((first_low.T, first_beside), (mixed_low.T, mixed_beside))
    )
    down_keep, down_give = mlp_outputs(near_block[0], far_block[0], weights, attn_sent)
    down_taken = swap(down_give, 1).astype(jnp.float32)
    down = (down_keep[0] + down_taken[0]).T
    down_far = swap((down_keep[1] + down_taken[1]).astype(low), 2).astype(jnp.float32).T
    attn_share = attn_finish()
    grad_features = after(grad_features, attn_sent).reshape(3 * width, total_rows)
    output = jnp.where(live, middle + (down + down_far + down_bias), 0.0).astype(low)
    grad_columns = jnp.sum(grad_features.astype(jnp.float32), axis=1)
    grad_first = jnp.einsum(
        "fr,fd->rd", grad_features, full_proj, preferred_element_type=jnp.float32
    )
    grad_gain_one = jnp.sum(grad_first * normed_one, axis=0)
    grad_shift_one = jnp.sum(grad_first, axis=0)
    grad_inputs = grad_middle + normalize_back(grad_first, normed_one, factor_one, gain_one)
    grad_vec = jnp.concatenate(
        [
            grad_gain_one,
            grad_shift_one,
            grad_columns[:width],
            grad_columns[2 * width :],
            grad_out_bias,
            grad_gain_two,
            grad_shift_two,
            grad_down_bias,
            grad_up_bias.reshape(-1),
        ],
        axis=0,
    )
    vec_share = scatter_vectors(grad_vec)
    return (output, grad_inputs, attn_share, mlp_share, vec_share)


def solution(mesh):
    return jax.shard_map(
        shards,
        mesh=mesh,
        in_specs=(
            P("dev", None),
            P("dev", None),
            P("dev", None),
            P("dev"),
            P("dev", None),
            P(),
            P(),
            P(),
        ),
        out_specs=(P("dev", None), P("dev", None), P("dev", None), P("dev", None), P("dev")),
        check_vma=False,
    )
```
